32 devices in a mesh: expert: 8 (over z, y), dp: 4 (over x, core).
Axes of the slice: x: 2, y: 2, z: 4, core: 2. Of those that a mesh axis runs over, the one named last changes fastest.
Arguments:
- tokens: bfloat16 [32768, 1024], P(('expert', 'dp')), may hold values from -6 to 6
- documents: int32 [32768], P(('expert', 'dp')), may hold values from 0 to 8, as said below
- routes: int32 [32768, 1], P(('expert', 'dp')), may hold values from 0 to 7; in each aligned block of 1024 rows (0 to 1023, 1024 to 2047, ...) at most 192 rows name the same one
- out_grad: bfloat16 [32768, 1024], P(('expert', 'dp')), may hold values from -6 to 6
- norm_params: float32 [4, 1024], P(None, ('expert', 'dp'))
- qkv_weight: float32 [1024, 3072], P(('expert', 'dp')), may hold values from -0.09375 to 0.09375
- proj_weight: float32 [1024, 1024], P(('expert', 'dp')), may hold values from -0.5 to 0.5
- centroids: float32 [8, 1024], P('expert', 'dp'), may hold values from -0.0625 to 0.0625
- expert_in: float32 [8, 1024, 4096], P('expert', 'dp'), may hold values from -0.09375 to 0.09375
- expert_out: float32 [8, 4096, 1024], P('expert', None, 'dp'), may hold values from -0.25 to 0.25
- norm_moment: float32 [4, 1024], P(None, ('expert', 'dp')), may hold values from -0.015625 to 0.015625
- qkv_moment: float32 [1024, 3072], P(('expert', 'dp')), may hold values from -0.0014648438 to 0.0014648438
- proj_moment: float32 [1024, 1024], P(('expert', 'dp')), may hold values from -0.0014648438 to 0.0014648438
- centroid_moment: float32 [8, 1024], P('expert', 'dp'), may hold values from -0.0014648438 to 0.0014648438
- in_moment: float32 [8, 1024, 4096], P('expert', 'dp'), may hold values from -0.0014648438 to 0.0014648438
- out_moment: float32 [8, 4096, 1024], P('expert', None, 'dp'), may hold values from -0.0014648438 to 0.0014648438
- norm_average: float32 [4, 1024], P(None, ('expert', 'dp')), may hold values from 0.5 to 1.5
- qkv_average: float32 [1024, 3072], P(('expert', 'dp')), may hold values from -0.09375 to 0.09375
- proj_average: float32 [1024, 1024], P(('expert', 'dp')), may hold values from -0.5 to 0.5
- centroid_average: float32 [8, 1024], P('expert', 'dp'), may hold values from -0.0625 to 0.0625
- in_average: float32 [8, 1024, 4096], P('expert', 'dp'), may hold values from -0.09375 to 0.09375
- out_average: float32 [8, 4096, 1024], P('expert', None, 'dp'), may hold values from -0.25 to 0.25
Outputs:
- activations: bfloat16 [32768, 1024], P(('expert', 'dp'))
- input_grad: float32 [32768, 1024], P(('expert', 'dp'))
- grad_norm: float32 [], replicated
- new_norm_params: float32 [4, 1024], P(None, ('expert', 'dp'))
- new_qkv_weight: float32 [1024, 3072], P(('expert', 'dp'))
- new_proj_weight: float32 [1024, 1024], P(('expert', 'dp'))
- new_centroids: float32 [8, 1024], P('expert', 'dp')
- new_expert_in: float32 [8, 1024, 4096], P('expert', 'dp')
- new_expert_out: float32 [8, 4096, 1024], P('expert', None, 'dp')
- new_norm_moment: float32 [4, 1024], P(None, ('expert', 'dp'))
- new_qkv_moment: float32 [1024, 3072], P(('expert', 'dp'))
- new_proj_moment: float32 [1024, 1024], P(('expert', 'dp'))
- new_centroid_moment: float32 [8, 1024], P('expert', 'dp')
- new_in_moment: float32 [8, 1024, 4096], P('expert', 'dp')
- new_out_moment: float32 [8, 4096, 1024], P('expert', None, 'dp')
- new_norm_average: float32 [4, 1024], P(None, ('expert', 'dp'))
- new_qkv_average: float32 [1024, 3072], P(('expert', 'dp'))
- new_proj_average: float32 [1024, 1024], P(('expert', 'dp'))
- new_centroid_average: float32 [8, 1024], P('expert', 'dp')
- new_in_average: float32 [8, 1024, 4096], P('expert', 'dp')
- new_out_average: float32 [8, 4096, 1024], P('expert', None, 'dp')
The draws below stay inside these ranges and needn't reach their ends.
Inputs may be any that keep to these rules, and one draw needn't show every extreme that they name: Each row of 1024 tokens holds 2 to 9 documents numbered 0, 1, ... in order, never falling; some row holds 9 and some row 2. `routes`: of one device's 1024 tokens at most 192 name the same expert; some expert is named by exactly 192 of some device's tokens.
All inputs are finite; a program needn't handle non-finite values.
Results may differ from the reference program's by a relative error of at most 0.014.
The reference program's roundings to bfloat16 on the way count: a program that leaves them out, or rounds other values in their place, can miss the bound.
Values may be sent and summed in bfloat16 or wider, within the bound.
No kernel may reach another device: no remote copies, remote signals or barrier semaphores. Data moves between devices by JAX's collectives and lax.ppermute only.
A program may use at most 320 MiB of HBM per device.

```python
import functools
import math
import jax
import jax.numpy as jnp
import numpy as np
from jax import lax

D = 1024
HEADS = 16
HEAD_DIM = 64
FF = 4096
SEQ = 1024
TOK_DEV = 1024
EXPERTS = 8
CAP = 192
TOKENS = 32768
N_EXPERT = 8
N_DP = 4


def draw_documents(key, part):
    key = jax.random.fold_in(key, 11)
    total_rows = TOKENS // SEQ
    row_keys = jax.random.split(jax.random.fold_in(key, 1), total_rows)
    counts = jax.random.randint(jax.random.fold_in(key, 2), (total_rows,), 2, 10)
    most_row = jax.random.randint(jax.random.fold_in(key, 3), (), 0, total_rows)
    least_row = (most_row + 1 + jax.random.randint(jax.random.fold_in(key, 4), (), 0, total_rows - 1)) % total_rows
    row_index = jnp.arange(total_rows)
    counts = jnp.where(row_index == most_row, 9, jnp.where(row_index == least_row, 2, counts))

    def one_row(row_key, doc_count):
        shuffled = jax.random.permutation(row_key, SEQ - 1)
        places = jnp.argsort(shuffled, stable=True)
        boundary = (places < doc_count - 1).astype(jnp.int32)
        return jnp.concatenate([jnp.zeros((1,), jnp.int32), jnp.cumsum(boundary).astype(jnp.int32)])
    return jax.vmap(one_row)(row_keys, counts).reshape(-1).astype(jnp.int32)


def draw_norm_params(key, part):
    key = jax.random.fold_in(key, 23)
    rising = jnp.arange(D, dtype=jnp.float32) / (D - 1)
    scales = (1.0 + 2.0 * rising) * jax.random.uniform(jax.random.fold_in(key, 1), (2, D), jnp.float32, 0.7, 1.3)
    biases = 0.3 * jax.random.normal(jax.random.fold_in(key, 2), (2, D), jnp.float32)
    return jnp.stack([scales[0], biases[0], scales[1], biases[1]])


def block_levels(key, extent, shards, smallest, largest):
    factor_of = 1.0
    for axis_at, blocks in shards:
        steps = jax.random.uniform(jax.random.fold_in(jax.random.fold_in(key, 6), axis_at), (blocks,), jnp.float32, smallest / len(shards), largest / len(shards))
        factor_of = factor_of * jnp.repeat(jnp.exp(steps), extent[axis_at] // blocks).reshape((-1,) + (1,) * (len(extent) - 1 - axis_at))
    return factor_of


def assign_block(stream_key, own, number, rows, count, top, reach, slope):
    ranking = jax.random.permutation(stream_key, count)
    crowded, common = portions_of(count, rows * top, reach, slope, True), portions_of(count, rows * top, reach, slope, False)
    places = jnp.arange(count)

    def named(sizes, turn):
        used = int((sizes > 0).sum())
        fixed = max(1, used // 4)
        shifted = fixed + (places - fixed + turn * (used - fixed)) % max(1, count - fixed)
        return jnp.zeros((count,), jnp.int32).at[ranking[jnp.where(places < fixed, places, shifted)]].set(jnp.asarray(sizes, jnp.int32))

    sizes = jnp.where(number % 4 == 0, named(crowded, number // 4), named(common, number - number // 4 - 1))
    mixed = jax.random.permutation(jax.random.fold_in(own, 3), count)
    giver, receiver = mixed[0:count // 2 * 2:2], mixed[1:count // 2 * 2:2]
    slack = jnp.minimum(sizes[giver] - 1, reach - sizes[receiver]) // 2
    slack = jnp.where((giver == ranking[0]) | (receiver == ranking[0]) | (sizes[receiver] == 0), 0, jnp.maximum(slack, 0))
    shifted = jax.random.randint(jax.random.fold_in(own, 4), (count // 2,), 0, 1 << 20) % (slack + 1)
    sizes = sizes.at[giver].add(-shifted).at[receiver].add(shifted)
    members = jnp.searchsorted(jnp.cumsum(sizes), jnp.arange(rows * top), side="right").astype(jnp.int32)
    table = members.reshape(top, rows).T
    table = table[jax.random.permutation(jax.random.fold_in(own, 1), rows)]
    turn = jax.random.randint(jax.random.fold_in(own, 2), (rows, 1), 0, top)
    return jnp.take_along_axis(table, (jnp.arange(top)[None, :] + turn) % top, axis=1)


def portions_of(amount, total, limit, skew, full):
    portions = [(1 << 20) // math.isqrt(grade ** skew) + 1 for grade in range(1, amount + 1)]
    largest = limit if full else min(limit, max(-(-total // amount), total * portions[0] // sum(portions)))
    least = 1 if total - largest >= amount - 1 else 0
    holding, surplus = [largest] + [least] * (amount - 1), total - largest - least * (amount - 1)
    while surplus > 0:
        candidates = [i for i in range(1, amount) if holding[i] < largest] or [i for i in range(1, amount) if holding[i] < limit]
        mass, remaining = sum([portions[i] for i in candidates]), surplus
        for i in candidates:
            more = min(limit - holding[i], max(1, remaining * portions[i] // mass), surplus)
            holding[i] = holding[i] + more
            surplus = surplus - more
    return np.array(holding)


def centred(own_key, extent, scale, reach, cuts=(), held_as=jnp.bfloat16):
    result = scale * jax.random.normal(own_key, extent, jnp.float32)
    if cuts:
        result = result * block_levels(own_key, extent, cuts, -0.22, 0.18)
    return jnp.clip(result, -reach, reach).astype(held_as)


def setup_inputs(seed: int = 0) -> dict:
    key_list = jax.random.split(jax.random.key(seed), 23)
    tokens = centred(key_list[0], (TOKENS, D), 1.0, 6.0, ((0, 32),))
    documents = draw_documents(jax.random.fold_in(key_list[22], 71), 0)
    routes_keys = jax.random.split(jax.random.fold_in(key_list[2], 1), TOKENS // TOK_DEV)
    routes_turns = jax.random.permutation(jax.random.fold_in(key_list[2], 3), TOKENS // TOK_DEV)
    routes = jax.vmap(lambda own, number: assign_block(jax.random.fold_in(key_list[2], 2), own, number, TOK_DEV, EXPERTS, 1, CAP, 2))(routes_keys, routes_turns).reshape((TOKENS, 1))
    out_grad = centred(key_list[3], (TOKENS, D), 1.0, 6.0, ((0, 32),))
    norm_params = draw_norm_params(jax.random.fold_in(key_list[22], 71), 0)
    qkv_weight = centred(key_list[5], (D, 3 * D), (4 * D) ** -0.5, 0.09375, ((0, 32),), jnp.float32)
    proj_weight = centred(key_list[6], (D, D), (D // 8) ** -0.5, 0.5, ((0, 32),), jnp.float32)
    centroids = centred(key_list[7], (EXPERTS, D), (9 * D) ** -0.5, 0.0625, ((0, 8), (1, 4)), jnp.float32)
    expert_in = centred(key_list[8], (EXPERTS, D, FF), (4 * D) ** -0.5, 0.09375, ((0, 8), (1, 4)), jnp.float32)
    expert_out = centred(key_list[9], (EXPERTS, FF, D), (FF // 8) ** -0.5, 0.25, ((0, 8), (2, 4)), jnp.float32)
    norm_moment = centred(key_list[10], (4, D), 0.001, 0.015625, ((1, 32),), jnp.float32)
    qkv_moment = centred(key_list[11], (D, 3 * D), 0.0001, 0.0014648438, ((0, 32),), jnp.float32)
    proj_moment = centred(key_list[12], (D, D), 0.0001, 0.0014648438, ((0, 32),), jnp.float32)
    centroid_moment = centred(key_list[13], (EXPERTS, D), 0.0001, 0.0014648438, ((0, 8), (1, 4)), jnp.float32)
    in_moment = centred(key_list[14], (EXPERTS, D, FF), 0.0001, 0.0014648438, ((0, 8), (1, 4)), jnp.float32)
    out_moment = centred(key_list[15], (EXPERTS, FF, D), 0.0001, 0.0014648438, ((0, 8), (2, 4)), jnp.float32)
    norm_average = jnp.clip(1.0 + 0.1 * jax.random.normal(key_list[16], (4, D), jnp.float32), 0.5, 1.5)
    qkv_average = centred(key_list[17], (D, 3 * D), (4 * D) ** -0.5, 0.09375, ((0, 32),), jnp.float32)
    proj_average = centred(key_list[18], (D, D), (D // 8) ** -0.5, 0.5, ((0, 32),), jnp.float32)
    centroid_average = centred(key_list[19], (EXPERTS, D), (9 * D) ** -0.5, 0.0625, ((0, 8), (1, 4)), jnp.float32)
    in_average = centred(key_list[20], (EXPERTS, D, FF), (4 * D) ** -0.5, 0.09375, ((0, 8), (1, 4)), jnp.float32)
    out_average = centred(key_list[21], (EXPERTS, FF, D), (FF // 8) ** -0.5, 0.25, ((0, 8), (2, 4)), jnp.float32)
    return {"tokens": tokens, "documents": documents, "routes": routes, "out_grad": out_grad, "norm_params": norm_params, "qkv_weight": qkv_weight, "proj_weight": proj_weight, "centroids": centroids, "expert_in": expert_in, "expert_out": expert_out, "norm_moment": norm_moment, "qkv_moment": qkv_moment, "proj_moment": proj_moment, "centroid_moment": centroid_moment, "in_moment": in_moment, "out_moment": out_moment, "norm_average": norm_average, "qkv_average": qkv_average, "proj_average": proj_average, "centroid_average": centroid_average, "in_average": in_average, "out_average": out_average}


@jax.custom_vjp
def low(v):
    return lax.optimization_barrier(v.astype(jnp.bfloat16)).astype(jnp.float32)

@jax.custom_vjp
def low_back(v):
    return v

def low_keep(v):
    return (low(v), None)

def low_pass(kept, grad):
    return (grad,)

def back_keep(v):
    return (v, None)

def back_low(kept, grad):
    return (low(grad),)
low.defvjp(low_keep, low_pass)
low_back.defvjp(back_keep, back_low)
eps = 1e-05
scale_qk = 0.125
momentum_rate = 0.9
learn_rate = 100.0
norm_rate = 500.0
average_rate = 0.9
clip_limit = 1.0
highest = lax.Precision.HIGHEST

def layer_norm(values, norm_gain, norm_bias):
    centre = values - lax.optimization_barrier(jnp.mean(values, axis=-1, keepdims=True))
    spread = lax.optimization_barrier(jnp.mean(centre * centre, axis=-1, keepdims=True))
    return centre * lax.rsqrt(spread + eps) * norm_gain + norm_bias

def masks_for(doc_row):
    places = jnp.arange(doc_row.shape[0])
    return (doc_row[:, None] == doc_row[None, :]) & (places[:, None] >= places[None, :])

def attend_group(norm_low, qkv_low, proj_low, inputs):
    rows_in, doc_rows = inputs
    group_rows = doc_rows.shape[0]
    seq_len = doc_rows.shape[1]
    normed = low(layer_norm(rows_in, norm_low[0], norm_low[1]))
    packed = low_back(low(jnp.einsum('gsd,de->gse', normed, qkv_low, precision=highest)))
    packed = packed.reshape(group_rows, seq_len, 3, HEADS, HEAD_DIM)
    scores = jnp.einsum('gqhd,gkhd->ghqk', packed[:, :, 0], packed[:, :, 1], precision=highest) * scale_qk
    allowed = jax.vmap(masks_for)(doc_rows)[:, None]
    scores = low_back(jnp.where(allowed, scores, -1000000000.0))
    attn_weights = low(jax.nn.softmax(scores, axis=-1))
    mixed_heads = jnp.einsum('ghqk,gkhd->gqhd', attn_weights, packed[:, :, 2], precision=highest)
    mixed_heads = low_back(low(mixed_heads)).reshape(group_rows, seq_len, HEADS * HEAD_DIM)
    attended = jnp.einsum('gsd,de->gse', mixed_heads, proj_low, precision=highest)
    return rows_in + low_back(attended)

def expert_tables(route_ids):
    token_total = route_ids.shape[0]
    order_idx = jnp.argsort(route_ids, stable=True).astype(jnp.int32)
    onehot = (route_ids[:, None] == jnp.arange(EXPERTS, dtype=jnp.int32)[None, :]).astype(jnp.int32)
    counts = lax.optimization_barrier(jnp.sum(onehot, axis=0)).astype(jnp.int32)
    starts = (jnp.cumsum(counts) - counts).astype(jnp.int32)
    slot_bound = N_EXPERT * N_DP * CAP
    offsets = jnp.arange(slot_bound, dtype=jnp.int32)
    places = jnp.minimum(starts[:, None] + offsets[None, :], token_total - 1).astype(jnp.int32)
    live_slot = (offsets[None, :] < counts[:, None]).astype(jnp.float32)
    return (order_idx[places], live_slot)

def run_expert(sent_rows, inputs):
    weight_in, weight_out, token_rows, live_slot = inputs
    picked = sent_rows[token_rows]
    preact = low_back(jnp.dot(picked, weight_in, precision=highest))
    hidden = low(jax.nn.gelu(preact, approximate=False))
    return jnp.dot(hidden, weight_out, precision=highest) * live_slot[:, None]

def forward(documents, route_ids, tokens_in, norm_in, qkv_in, proj_in, centre_in, expert_in, expert_out):
    norm_low = low(norm_in)
    qkv_low = low(qkv_in)
    proj_low = low(proj_in)
    centre_low = low(centre_in)
    in_low = low(expert_in)
    out_low = low(expert_out)
    total_rows = tokens_in.shape[0] // SEQ
    group_rows = 4 if total_rows % 4 == 0 else 1
    grouped = tokens_in.reshape(total_rows // group_rows, group_rows, SEQ, D)
    doc_groups = documents.reshape(total_rows // group_rows, group_rows, SEQ)
    attend_fn = jax.checkpoint(functools.partial(attend_group, norm_low, qkv_low, proj_low))
    after_attn = lax.map(attend_fn, (grouped, doc_groups)).reshape(-1, D)
    normed_two = layer_norm(after_attn, norm_low[2], norm_low[3])
    sent_low = low(normed_two)
    logits = lax.optimization_barrier(jnp.sum(sent_low * centre_low[route_ids], axis=-1))
    gate_value = jax.nn.sigmoid(logits)
    token_rows, live_slot = expert_tables(route_ids)
    expert_fn = jax.checkpoint(functools.partial(run_expert, low_back(sent_low)))
    results = lax.map(expert_fn, (in_low, out_low, token_rows, live_slot))
    returned = jnp.zeros_like(after_attn).at[token_rows.reshape(-1)].add(results.reshape(-1, D))
    returned = low_back(low(returned))
    return after_attn + gate_value[:, None] * returned

def update(weight, moment, average, gradient, factor, rate):
    clipped = gradient * factor
    moment_new = momentum_rate * moment + clipped
    weight_new = weight - rate * (clipped + momentum_rate * moment_new)
    average_new = average_rate * average + (1.0 - average_rate) * weight_new
    return (weight_new, moment_new, average_new)

def reference(tokens, documents, routes, out_grad, norm_params, qkv_weight, proj_weight, centroids, expert_in, expert_out, norm_moment, qkv_moment, proj_moment, centroid_moment, in_moment, out_moment, norm_average, qkv_average, proj_average, centroid_average, in_average, out_average):
    route_ids = routes[:, 0]
    outputs, pullback = jax.vjp(functools.partial(forward, documents, route_ids), tokens.astype(jnp.float32), norm_params, qkv_weight, proj_weight, centroids, expert_in, expert_out)
    gradients = pullback(out_grad.astype(jnp.float32))
    square_sum = jnp.zeros((), jnp.float32)
    for grad_piece in gradients[1:]:
        square_sum = square_sum + jnp.sum(grad_piece * grad_piece)
    grad_norm = jnp.sqrt(square_sum)
    factor = clip_limit / jnp.maximum(grad_norm, clip_limit)
    norm_new = update(norm_params, norm_moment, norm_average, gradients[1], factor, norm_rate)
    qkv_new = update(qkv_weight, qkv_moment, qkv_average, gradients[2], factor, learn_rate)
    proj_new = update(proj_weight, proj_moment, proj_average, gradients[3], factor, learn_rate)
    centre_new = update(centroids, centroid_moment, centroid_average, gradients[4], factor, learn_rate)
    in_new = update(expert_in, in_moment, in_average, gradients[5], factor, learn_rate)
    out_new = update(expert_out, out_moment, out_average, gradients[6], factor, learn_rate)
    return (outputs.astype(jnp.bfloat16), gradients[0], grad_norm, norm_new[0], qkv_new[0], proj_new[0], centre_new[0], in_new[0], out_new[0], norm_new[1], qkv_new[1], proj_new[1], centre_new[1], in_new[1], out_new[1], norm_new[2], qkv_new[2], proj_new[2], centre_new[2], in_new[2], out_new[2])
```

```python
import functools
import math

import jax
import jax.numpy as jnp
from jax import lax
from jax.experimental import pallas as pl
from jax.experimental.pallas import tpu as pltpu
from jax.sharding import PartitionSpec as P

HEAD_DIM = 64
SEQ = 1024
LANES = 128
BLOCK = 256

eps = 1e-05
scale_qk = 0.125
momentum_rate = 0.9
learn_rate = 100.0
norm_rate = 500.0
average_rate = 0.9
clip_limit = 1.0
masked_score = -1000000000.0
everywhere = ("expert", "dp")
low = jnp.bfloat16
f32 = jnp.float32

erfc_point = 0.4
erfc_terms = (
    0.11596270714310389,
    0.08090178846816841,
    0.2341610172367065,
    -0.1854824771652721,
    0.35459055762612957,
    -0.10013360714943426,
)


def dot_rows(left, right):
    return lax.dot_general(left, right, (((1,), (0,)), ((), ())), preferred_element_type=f32)


def dot_cols(left, right):
    return lax.dot_general(left, right, (((1,), (1,)), ((), ())), preferred_element_type=f32)


def layer_norm(values, norm_gain, norm_bias):
    centre = values - jnp.mean(values, axis=-1, keepdims=True)
    spread = jnp.mean(centre * centre, axis=-1, keepdims=True)
    return centre * lax.rsqrt(spread + eps) * norm_gain + norm_bias


def fill_bias(bias, doc_of_rows, doc_of_cols, rows_are_keys):
    for block in range(0, SEQ, BLOCK):
        rows = lax.broadcasted_iota(jnp.int32, (BLOCK, SEQ), 0) + block
        cols = lax.broadcasted_iota(jnp.int32, (BLOCK, SEQ), 1)
        causal = (rows <= cols) if rows_are_keys else (rows >= cols)
        same = doc_of_rows[block : block + BLOCK, :] == doc_of_cols[...]
        bias[block : block + BLOCK, :] = jnp.where(same & causal, 3.0e38, masked_score)


def in_head(shape, head, axis):
    return lax.broadcasted_iota(jnp.int32, shape, axis) // HEAD_DIM == head


def keep_head(values, head):
    return jnp.where(in_head(values.shape, head, 1), values, jnp.zeros_like(values))


def attend_kernel(q_ref, k_ref, v_ref, doc_col, doc_row, mixed_ref, lse_ref, bias):
    @pl.when(pl.program_id(1) == 0)
    def _():
        fill_bias(bias, doc_col, doc_row, False)

    for block in range(0, SEQ, BLOCK):
        seen = block + BLOCK
        query = q_ref[block:seen, :] * jnp.asarray(scale_qk, low)
        outs, stats = [], []
        for head in range(2):
            scores = dot_cols(keep_head(query, head), k_ref[:seen, :])
            scores = jnp.minimum(scores, bias[block:seen, :seen])
            top = jnp.max(scores, axis=-1, keepdims=True)
            exponent = jnp.exp(scores - top)
            total = jnp.sum(exponent, axis=-1, keepdims=True)
            outs.append(dot_rows(exponent.astype(low), v_ref[:seen, :]) / total)
            stats.append(top + jnp.log(total))
        first = in_head((BLOCK, LANES), 0, 1)
        mixed_ref[block:seen, :] = jnp.where(first, outs[0], outs[1]).astype(low)
        lane = lax.broadcasted_iota(jnp.int32, (BLOCK, LANES), 1)
        both = jnp.where(lane == 0, stats[0], stats[1])
        lse_ref[:, block:seen] = both.T[:8, :]


def attend(packed, doc_col, doc_row):
    count, wide = packed.shape
    width = wide // 3
    pairs = width // LANES

    def part(which):
        return pl.BlockSpec((SEQ, LANES), lambda r, p, w=which: (r, w * pairs + p))

    return pl.pallas_call(
        attend_kernel,
        grid=(count // SEQ, pairs),
        in_specs=[
            part(0),
            part(1),
            part(2),
            pl.BlockSpec((SEQ, 1), lambda r, p: (r, 0)),
            pl.BlockSpec((1, SEQ), lambda r, p: (0, r)),
        ],
        out_specs=[
            pl.BlockSpec((SEQ, LANES), lambda r, p: (r, p)),
            pl.BlockSpec((8, SEQ), lambda r, p: (p, r)),
        ],
        out_shape=[
            jax.ShapeDtypeStruct((count, width), low),
            jax.ShapeDtypeStruct((8 * pairs, count), f32),
        ],
        scratch_shapes=[pltpu.VMEM((SEQ, SEQ), f32)],
        compiler_params=pltpu.CompilerParams(vmem_limit_bytes=48 * 2**20),
        cost_estimate=pl.CostEstimate(
            flops=4 * count * SEQ * width, bytes_accessed=8 * count * width, transcendentals=0
        ),
        name="attend",
    )(packed, packed, packed, doc_col, doc_row)


def attend_back_kernel(
    q_ref, k_ref, v_ref, grad_ref, mixed_ref, lse_ref, doc_col, doc_row, out_ref, bias, grad_q_t
):
    @pl.when(pl.program_id(1) == 0)
    def _():
        fill_bias(bias, doc_col, doc_row, True)

    query = q_ref[...] * jnp.asarray(scale_qk, low)
    grad = grad_ref[...]
    product = grad.astype(f32) * mixed_ref[...].astype(f32)
    upper = product.astype(low)
    lower = (product - upper.astype(f32)).astype(low)
    chooser = (
        lax.broadcasted_iota(jnp.int32, (8, LANES), 0)
        == lax.broadcasted_iota(jnp.int32, (8, LANES), 1) // HEAD_DIM
    ).astype(low)
    inner = dot_cols(chooser, upper) + dot_cols(chooser, lower)
    key_t = k_ref[...].T
    for block in range(0, SEQ, BLOCK):
        after = block + BLOCK
        key = k_ref[block:after, :]
        value = v_ref[block:after, :]
        grad_k, grad_v = [], []
        for head in range(2):
            scores = dot_cols(keep_head(key, head), query[block:, :])
            scores = jnp.minimum(scores, bias[block:after, block:])
            weights = jnp.exp(scores - lse_ref[head : head + 1, block:])
            grad_w = dot_cols(keep_head(value, head), grad[block:, :])
            grad_s = (weights * (grad_w - inner[head : head + 1, block:])).astype(low)
            grad_v.append(dot_rows(weights.astype(low), grad[block:, :]))
            grad_k.append(dot_rows(grad_s, query[block:, :]))
            rows = slice(head * HEAD_DIM, (head + 1) * HEAD_DIM)
            moved = dot_rows(key_t[rows, block:after], grad_s)
            if block == 0:
                grad_q_t[rows, :] = moved
            else:
                grad_q_t[rows, block:] += moved
        first = in_head((BLOCK, LANES), 0, 1)
        out_ref[1, block:after, :] = jnp.where(first, grad_k[0], grad_k[1]).astype(low)
        out_ref[2, block:after, :] = jnp.where(first, grad_v[0], grad_v[1]).astype(low)
    out_ref[0] = (grad_q_t[...] * scale_qk).T.astype(low)


def attend_back(packed, grad_mixed, mixed, lse, doc_col, doc_row, first, pairs_here):
    count, wide = packed.shape
    width = wide // 3
    pairs = width // LANES

    def part(which):
        return pl.BlockSpec((SEQ, LANES), lambda r, p, w=which: (r, w * pairs + first + p))

    same = pl.BlockSpec((SEQ, LANES), lambda r, p: (r, first + p))
    return pl.pallas_call(
        attend_back_kernel,
        grid=(count // SEQ, pairs_here),
        in_specs=[
            part(0),
            part(1),
            part(2),
            same,
            same,
            pl.BlockSpec((8, SEQ), lambda r, p: (first + p, r)),
            pl.BlockSpec((SEQ, 1), lambda r, p: (r, 0)),
            pl.BlockSpec((1, SEQ), lambda r, p: (0, r)),
        ],
        out_specs=pl.BlockSpec((3, SEQ, LANES), lambda r, p: (0, r, p)),
        out_shape=jax.ShapeDtypeStruct((3, count, pairs_here * LANES), low),
        scratch_shapes=[pltpu.VMEM((SEQ, SEQ), f32), pltpu.VMEM((LANES, SEQ), f32)],
        compiler_params=pltpu.CompilerParams(vmem_limit_bytes=48 * 2**20),
        cost_estimate=pl.CostEstimate(
            flops=10 * count * SEQ * pairs_here * LANES,
            bytes_accessed=16 * count * pairs_here * LANES,
            transcendentals=0,
        ),
        name="attend_back",
    )(packed, packed, packed, grad_mixed, mixed, lse, doc_col, doc_row)


def gelu_and_slope(x):
    point = 1.0 / (1.0 + (erfc_point * math.sqrt(0.5)) * jnp.abs(x))
    bell = jnp.exp(-0.5 * x * x)
    tail = erfc_terms[-1]
    for term in erfc_terms[-2::-1]:
        tail = tail * point + term
    tail = tail * point * bell
    below = jnp.where(x >= 0.0, 1.0 - tail, tail)
    return x * below, below + x * bell * (1.0 / math.sqrt(2.0 * math.pi))


def expert_kernel(x_ref, in_ref, out_ref, hidden_ref, slope_ref, result_ref, total):
    step = pl.program_id(0)

    @pl.when(step == 0)
    def _():
        total[...] = jnp.zeros_like(total)

    for row in range(0, x_ref.shape[0], BLOCK):
        rows = slice(row, row + BLOCK)
        preact = dot_rows(x_ref[rows, :], in_ref[...])
        value, slope = gelu_and_slope(preact)
        hidden = value.astype(low)
        hidden_ref[rows, :] = hidden
        slope_ref[rows, :] = slope.astype(low)
        total[rows, :] += dot_rows(hidden, out_ref[...])

    @pl.when(step == pl.num_programs(0) - 1)
    def _():
        result_ref[...] = total[...].astype(low)


def expert_forward(arrived, weight_in, weight_out, tile=512):
    slots, width = arrived.shape
    inner = weight_in.shape[1]
    whole = pl.BlockSpec((slots, width), lambda j: (0, 0))
    strip = pl.BlockSpec((slots, tile), lambda j: (0, j))
    return pl.pallas_call(
        expert_kernel,
        grid=(inner // tile,),
        in_specs=[
            whole,
            pl.BlockSpec((width, tile), lambda j: (0, j)),
            pl.BlockSpec((tile, width), lambda j: (j, 0)),
        ],
        out_specs=[strip, strip, whole],
        out_shape=[
            jax.ShapeDtypeStruct((slots, inner), low),
            jax.ShapeDtypeStruct((slots, inner), low),
            jax.ShapeDtypeStruct((slots, width), low),
        ],
        scratch_shapes=[pltpu.VMEM((slots, width), f32)],
        compiler_params=pltpu.CompilerParams(vmem_limit_bytes=56 * 2**20),
        cost_estimate=pl.CostEstimate(
            flops=4 * slots * width * inner,
            bytes_accessed=4 * (slots + width) * inner,
            transcendentals=0,
        ),
        name="expert_forward",
    )(arrived, weight_in, weight_out)


def expert_back_kernel(
    grad_ref,
    slope_ref,
    in_ref,
    out_ref,
    x_ref,
    result_ref,
    centre_ref,
    grad_preact_ref,
    grad_rows_ref,
    grad_centre_ref,
    total,
):
    step = pl.program_id(0)

    @pl.when(step == 0)
    def _():
        total[...] = jnp.zeros_like(total)

    for row in range(0, grad_ref.shape[0], BLOCK):
        rows = slice(row, row + BLOCK)
        grad_hidden = dot_cols(grad_ref[rows, :], out_ref[...])
        grad_preact = (grad_hidden * slope_ref[rows, :].astype(f32)).astype(low)
        grad_preact_ref[rows, :] = grad_preact
        total[rows, :] += dot_cols(grad_preact, in_ref[...])

    @pl.when(step == pl.num_programs(0) - 1)
    def _():
        centre = centre_ref[...].astype(f32)
        grad_centre = jnp.zeros(grad_centre_ref.shape, f32)
        for row in range(0, grad_ref.shape[0], BLOCK):
            rows = slice(row, row + BLOCK)
            x = x_ref[rows, :].astype(f32)
            gate = jax.nn.sigmoid(jnp.sum(x * centre, axis=-1, keepdims=True))
            moved = grad_ref[rows, :].astype(f32) * result_ref[rows, :].astype(f32)
            grad_logit = jnp.sum(moved, axis=-1, keepdims=True) * (1.0 - gate)
            grad_rows_ref[rows, :] = (total[rows, :] + grad_logit * centre).astype(low)
            by_slot = (grad_logit * x).reshape(-1, 8, x.shape[1])
            grad_centre = grad_centre + jnp.sum(by_slot, axis=0)
        grad_centre_ref[...] = grad_centre


def expert_back(grad_arrived, slope, weight_in, weight_out, arrived, result, centre, tile=512):
    slots, width = arrived.shape
    inner = weight_in.shape[1]
    whole = pl.BlockSpec((slots, width), lambda j: (0, 0))
    strip = pl.BlockSpec((slots, tile), lambda j: (0, j))
    return pl.pallas_call(
        expert_back_kernel,
        grid=(inner // tile,),
        in_specs=[
            whole,
            strip,
            pl.BlockSpec((width, tile), lambda j: (0, j)),
            pl.BlockSpec((tile, width), lambda j: (j, 0)),
            whole,
            whole,
            pl.BlockSpec((1, width), lambda j: (0, 0)),
        ],
        out_specs=[strip, whole, pl.BlockSpec((8, width), lambda j: (0, 0))],
        out_shape=[
            jax.ShapeDtypeStruct((slots, inner), low),
            jax.ShapeDtypeStruct((slots, width), low),
            jax.ShapeDtypeStruct((8, width), f32),
        ],
        scratch_shapes=[pltpu.VMEM((slots, width), f32)],
        compiler_params=pltpu.CompilerParams(vmem_limit_bytes=56 * 2**20),
        cost_estimate=pl.CostEstimate(
            flops=4 * slots * width * inner,
            bytes_accessed=4 * (slots + width) * inner,
            transcendentals=0,
        ),
        name="expert_back",
    )(grad_arrived, slope, weight_in, weight_out, arrived, result, centre)


def swap(values, axis, distance):
    size = lax.axis_size(axis)
    return lax.ppermute(values, axis, [(i, i ^ distance) for i in range(size)])


def scatter_over_dp(values):
    me = lax.axis_index("dp")
    distance = 1
    held = values
    while distance < lax.axis_size("dp"):
        bit = (me // distance) % 2
        pairs = held.reshape((held.shape[0] // 2, 2) + held.shape[1:])
        mine = lax.dynamic_index_in_dim(pairs, bit, 1, keepdims=False)
        theirs = lax.dynamic_index_in_dim(pairs, 1 - bit, 1, keepdims=False)
        held = (mine.astype(f32) + swap(theirs, "dp", distance).astype(f32)).astype(low)
        distance *= 2
    return held[0]


def sum_everywhere(value):
    held = value.reshape(1, 1)
    for axis in ("dp", "expert"):
        distance = 1
        while distance < lax.axis_size(axis):
            held = held + swap(held, axis, distance)
            distance *= 2
    return held[0, 0]


def update(weight, moment, average, gradient, factor, rate):
    clipped = gradient * factor
    moment_new = momentum_rate * moment + clipped
    weight_new = weight - rate * (clipped + momentum_rate * moment_new)
    average_new = average_rate * average + (1.0 - average_rate) * weight_new
    return (weight_new, moment_new, average_new)


def shards(
    tokens,
    documents,
    routes,
    out_grad,
    norm_params,
    qkv_weight,
    proj_weight,
    centroids,
    expert_in,
    expert_out,
    norm_moment,
    qkv_moment,
    proj_moment,
    centroid_moment,
    in_moment,
    out_moment,
    norm_average,
    qkv_average,
    proj_average,
    centroid_average,
    in_average,
    out_average,
):
    local_tokens, width = tokens.shape
    experts = lax.axis_size("expert")
    dp = lax.axis_size("dp")
    devices = experts * dp
    slot_cap = max(2, 3 * local_tokens // (2 * experts))
    slots = experts * slot_cap
    rows_own = qkv_weight.shape[0]
    norm_own = norm_params.shape[1]
    centre_own = centroids.shape[1]

    small = jnp.concatenate([norm_params.reshape(-1), centroids.reshape(-1)]).astype(low)
    small = jnp.pad(small, (0, rows_own * LANES - small.shape[0])).reshape(rows_own, LANES)
    dense = jnp.concatenate([qkv_weight.astype(low), proj_weight.astype(low), small], axis=1)
    dense = lax.all_gather(dense, everywhere, axis=0, tiled=True)
    weight_in = lax.all_gather(expert_in.astype(low), "dp", axis=1, tiled=True)[0]
    weight_out = lax.all_gather(expert_out.astype(low), "dp", axis=2, tiled=True)[0]

    route_ids = routes[:, 0]
    onehot = route_ids[:, None] == jnp.arange(experts, dtype=jnp.int32)[None, :]
    running = jnp.cumsum(onehot.astype(jnp.int32), axis=0)
    within = jnp.sum(running * onehot.astype(jnp.int32), axis=1) - 1
    slot_index = route_ids * slot_cap + within

    qkv_full = dense[:, : 3 * width]
    proj_full = dense[:, 3 * width : 4 * width]
    small_full = dense[:, 4 * width :].reshape(devices, rows_own * LANES)
    norm_values = (
        small_full[:, : 4 * norm_own].reshape(devices, 4, norm_own).transpose(1, 0, 2)
    ).reshape(4, width).astype(f32)
    centre_table = small_full[:, 4 * norm_own : 4 * norm_own + centre_own].reshape(experts, width)

    x_in = tokens.astype(f32)
    normed_one, norm_back_one = jax.vjp(layer_norm, x_in, norm_values[0], norm_values[1])
    normed_low = normed_one.astype(low)
    packed = jnp.dot(normed_low, qkv_full, preferred_element_type=f32).astype(low)
    doc_col = documents[:, None]
    doc_row = documents[None, :]
    mixed_low, lse = attend(packed, doc_col, doc_row)
    attended = jnp.dot(mixed_low, proj_full, preferred_element_type=f32)
    after_attn = x_in + attended
    normed_two, norm_back_two = jax.vjp(layer_norm, after_attn, norm_values[2], norm_values[3])
    sent_low = normed_two.astype(low)
    picked_centre = jnp.dot(onehot.astype(low), centre_table, preferred_element_type=f32)
    logits = jnp.sum(sent_low.astype(f32) * picked_centre, axis=-1)
    gate_value = jax.nn.sigmoid(logits)
    grad_out = out_grad.astype(f32)
    grad_rows = (gate_value[:, None] * grad_out).astype(low)

    place = jnp.arange(slots, dtype=jnp.int32)[:, None] == slot_index[None, :]
    place = place.astype(low)

    def dispatch(rows):
        out = jnp.dot(place, rows, preferred_element_type=f32).astype(low)
        out = out.reshape(experts, slot_cap, width)
        out = lax.all_to_all(out, "expert", split_axis=0, concat_axis=0, tiled=True)
        return out.reshape(slots, width)

    def send_back(rows):
        rows = rows.reshape(experts, slot_cap, width)
        rows = lax.all_to_all(rows, "expert", split_axis=0, concat_axis=0, tiled=True)
        return rows.reshape(slots, width)

    def collect(rows):
        return lax.dot_general(
            place, rows, (((0,), (0,)), ((), ())), preferred_element_type=f32
        )

    arrived = dispatch(sent_low)
    grad_arrived = dispatch(grad_rows)
    hidden, slope, result = expert_forward(arrived, weight_in, weight_out)
    grad_weight_out = lax.dot_general(
        hidden, grad_arrived, (((0,), (0,)), ((), ())), preferred_element_type=f32
    ).astype(low)
    centre_own_row = lax.dynamic_slice_in_dim(centre_table, lax.axis_index("expert"), 1, 0)
    grad_preact, grad_input_rows, grad_centre = expert_back(
        grad_arrived, slope, weight_in, weight_out, arrived, result, centre_own_row
    )
    out_grad_w = lax.psum_scatter(
        grad_weight_out[None], "dp", scatter_dimension=2, tiled=True
    ).astype(f32)
    grad_back = send_back(grad_input_rows)
    grad_weight_in = lax.dot_general(
        arrived, grad_preact, (((0,), (0,)), ((), ())), preferred_element_type=f32
    ).astype(low)
    in_grad = lax.psum_scatter(
        grad_weight_in[None], "dp", scatter_dimension=1, tiled=True
    ).astype(f32)
    returned = send_back(result)

    grad_normed_two = collect(grad_back)
    grad_after, grad_gain_two, grad_bias_two = norm_back_two(grad_normed_two)
    grad_after = grad_after + grad_out
    grad_attended = grad_after.astype(low)
    grad_mixed = dot_cols(grad_attended, proj_full).astype(low)
    grad_proj = lax.dot_general(
        mixed_low, grad_attended, (((0,), (0,)), ((), ())), preferred_element_type=f32
    ).astype(low)

    pairs = width // LANES
    groups = 2
    each = pairs // groups
    grad_parts, grad_qkv = [], []
    grad_normed_one = jnp.zeros((local_tokens, width), f32)
    for group in range(groups):
        part = attend_back(
            packed, grad_mixed, mixed_low, lse, doc_col, doc_row, group * each, each
        )
        wide = each * LANES
        columns = [
            qkv_full[:, s * width + group * wide : s * width + (group + 1) * wide]
            for s in range(3)
        ]
        flat = jnp.concatenate([part[0], part[1], part[2]], axis=1)
        grad_parts.append(flat)
        grad_qkv.append(
            lax.dot_general(
                normed_low, flat, (((0,), (0,)), ((), ())), preferred_element_type=f32
            ).astype(low)
        )
        grad_normed_one = grad_normed_one + dot_cols(flat, jnp.concatenate(columns, axis=1))
    grad_x_norm, grad_gain_one, grad_bias_one = norm_back_one(grad_normed_one)
    input_grad = grad_after + grad_x_norm
    activations = (after_attn + gate_value[:, None] * collect(returned)).astype(low)

    def to_owners(values):
        columns = values.shape[1]
        held = values.reshape(experts, dp, rows_own, columns).transpose(1, 0, 2, 3)
        held = scatter_over_dp(held)
        held = lax.all_to_all(held, "expert", split_axis=0, concat_axis=0, tiled=True)
        return jnp.sum(held.astype(f32), axis=0)

    grad_norm_rows = jnp.stack([grad_gain_one, grad_bias_one, grad_gain_two, grad_bias_two])
    norm_flat = grad_norm_rows.reshape(4, devices, norm_own).transpose(1, 0, 2)
    norm_flat = norm_flat.reshape(devices, 4 * norm_own).astype(low)
    norm_flat = jnp.pad(norm_flat, ((0, 0), (0, rows_own * LANES - 4 * norm_own)))
    norm_flat = norm_flat.reshape(devices * rows_own, LANES)
    first_part = to_owners(jnp.concatenate([grad_proj, grad_qkv[0]], axis=1))
    second_part = to_owners(jnp.concatenate([grad_qkv[1], norm_flat], axis=1))
    proj_grad = first_part[:, :width]
    halves = [first_part[:, width:], second_part[:, : 3 * width // 2]]
    wide = each * LANES
    qkv_grad = jnp.concatenate(
        [half[:, s * wide : (s + 1) * wide] for s in range(3) for half in halves], axis=1
    )
    norm_grad = second_part[:, 3 * width // 2 :].reshape(-1)[: 4 * norm_own].reshape(4, norm_own)
    centre_sum = jnp.sum(grad_centre, axis=0).reshape(dp, centre_own)
    centre_grad = lax.psum_scatter(centre_sum, "dp", scatter_dimension=0, tiled=True)
    square_sum = (
        jnp.sum(qkv_grad * qkv_grad)
        + jnp.sum(proj_grad * proj_grad)
        + jnp.sum(norm_grad * norm_grad)
        + jnp.sum(centre_grad * centre_grad)
        + jnp.sum(in_grad * in_grad)
        + jnp.sum(out_grad_w * out_grad_w)
    )
    grad_norm = jnp.sqrt(sum_everywhere(square_sum))
    factor = clip_limit / jnp.maximum(grad_norm, clip_limit)
    norm_new = update(norm_params, norm_moment, norm_average, norm_grad, factor, norm_rate)
    qkv_new = update(qkv_weight, qkv_moment, qkv_average, qkv_grad, factor, learn_rate)
    proj_new = update(proj_weight, proj_moment, proj_average, proj_grad, factor, learn_rate)
    centre_new = update(
        centroids, centroid_moment, centroid_average, centre_grad, factor, learn_rate
    )
    in_new = update(expert_in, in_moment, in_average, in_grad, factor, learn_rate)
    out_new = update(expert_out, out_moment, out_average, out_grad_w, factor, learn_rate)
    return (
        activations,
        input_grad,
        grad_norm,
        norm_new[0],
        qkv_new[0],
        proj_new[0],
        centre_new[0],
        in_new[0],
        out_new[0],
        norm_new[1],
        qkv_new[1],
        proj_new[1],
        centre_new[1],
        in_new[1],
        out_new[1],
        norm_new[2],
        qkv_new[2],
        proj_new[2],
        centre_new[2],
        in_new[2],
        out_new[2],
    )


def solution(mesh):
    placed = (
        P(("expert", "dp"), None),
        P(("expert", "dp")),
        P(("expert", "dp"), None),
        P(("expert", "dp"), None),
        P(None, ("expert", "dp")),
        P(("expert", "dp"), None),
        P(("expert", "dp"), None),
        P("expert", "dp"),
        P("expert", "dp", None),
        P("expert", None, "dp"),
        P(None, ("expert", "dp")),
        P(("expert", "dp"), None),
        P(("expert", "dp"), None),
        P("expert", "dp"),
        P("expert", "dp", None),
        P("expert", None, "dp"),
        P(None, ("expert", "dp")),
        P(("expert", "dp"), None),
        P(("expert", "dp"), None),
        P("expert", "dp"),
        P("expert", "dp", None),
        P("expert", None, "dp"),
    )
    return jax.shard_map(
        shards,
        mesh=mesh,
        in_specs=placed,
        out_specs=(
            P(("expert", "dp"), None),
            P(("expert", "dp"), None),
            P(),
            P(None, ("expert", "dp")),
            P(("expert", "dp"), None),
            P(("expert", "dp"), None),
            P("expert", "dp"),
            P("expert", "dp", None),
            P("expert", None, "dp"),
            P(None, ("expert", "dp")),
            P(("expert", "dp"), None),
            P(("expert", "dp"), None),
            P("expert", "dp"),
            P("expert", "dp", None),
            P("expert", None, "dp"),
            P(None, ("expert", "dp")),
            P(("expert", "dp"), None),
            P(("expert", "dp"), None),
            P("expert", "dp"),
            P("expert", "dp", None),
            P("expert", None, "dp"),
        ),
        check_vma=False,
    )
```

```python
import functools
import math

import jax
import jax.numpy as jnp
from jax import lax
from jax.experimental import pallas as pl
from jax.experimental.pallas import tpu as pltpu
from jax.sharding import PartitionSpec as P

HEAD_DIM = 64
SEQ = 1024
LANES = 128
BLOCK = 256

eps = 1e-05
scale_qk = 0.125
momentum_rate = 0.9
learn_rate = 100.0
norm_rate = 500.0
average_rate = 0.9
clip_limit = 1.0
masked_score = -1000000000.0
everywhere = ("expert", "dp")
low = jnp.bfloat16
f32 = jnp.float32

erfc_point = 0.4
erfc_terms = (
    0.11596270714310389,
    0.08090178846816841,
    0.2341610172367065,
    -0.1854824771652721,
    0.35459055762612957,
    -0.10013360714943426,
)


def dot_rows(left, right):
    return lax.dot_general(left, right, (((1,), (0,)), ((), ())), preferred_element_type=f32)


def dot_cols(left, right):
    return lax.dot_general(left, right, (((1,), (1,)), ((), ())), preferred_element_type=f32)


def layer_norm(values, norm_gain, norm_bias):
    centre = values - jnp.mean(values, axis=-1, keepdims=True)
    spread = jnp.mean(centre * centre, axis=-1, keepdims=True)
    return centre * lax.rsqrt(spread + eps) * norm_gain + norm_bias


def fill_bias(bias, doc_of_rows, doc_of_cols, rows_are_keys):
    for block in range(0, SEQ, BLOCK):
        rows = lax.broadcasted_iota(jnp.int32, (BLOCK, SEQ), 0) + block
        cols = lax.broadcasted_iota(jnp.int32, (BLOCK, SEQ), 1)
        causal = (rows <= cols) if rows_are_keys else (rows >= cols)
        same = doc_of_rows[block : block + BLOCK, :] == doc_of_cols[...]
        bias[block : block + BLOCK, :] = jnp.where(same & causal, 3.0e38, masked_score)


def in_head(shape, head, axis):
    return lax.broadcasted_iota(jnp.int32, shape, axis) // HEAD_DIM == head


def keep_head(values, head):
    return jnp.where(in_head(values.shape, head, 1), values, jnp.zeros_like(values))


def attend_kernel(q_ref, k_ref, v_ref, doc_col, doc_row, mixed_ref, lse_ref, bias):
    @pl.when(pl.program_id(1) == 0)
    def _():
        fill_bias(bias, doc_col, doc_row, False)

    for block in range(0, SEQ, BLOCK):
        seen = block + BLOCK
        query = q_ref[block:seen, :] * jnp.asarray(scale_qk, low)
        outs, stats = [], []
        for head in range(2):
            scores = dot_cols(keep_head(query, head), k_ref[:seen, :])
            scores = jnp.minimum(scores, bias[block:seen, :seen])
            top = jnp.max(scores, axis=-1, keepdims=True)
            exponent = jnp.exp(scores - top)
            total = jnp.sum(exponent, axis=-1, keepdims=True)
            outs.append(dot_rows(exponent.astype(low), v_ref[:seen, :]) / total)
            stats.append(top + jnp.log(total))
        first = in_head((BLOCK, LANES), 0, 1)
        mixed_ref[block:seen, :] = jnp.where(first, outs[0], outs[1]).astype(low)
        lane = lax.broadcasted_iota(jnp.int32, (BLOCK, LANES), 1)
        both = jnp.where(lane == 0, stats[0], stats[1])
        lse_ref[:, block:seen] = both.T[:8, :]


def attend(packed, doc_col, doc_row):
    count, wide = packed.shape
    width = wide // 3
    pairs = width // LANES

    def part(which):
        return pl.BlockSpec((SEQ, LANES), lambda r, p, w=which: (r, w * pairs + p))

    return pl.pallas_call(
        attend_kernel,
        grid=(count // SEQ, pairs),
        in_specs=[
            part(0),
            part(1),
            part(2),
            pl.BlockSpec((SEQ, 1), lambda r, p: (r, 0)),
            pl.BlockSpec((1, SEQ), lambda r, p: (0, r)),
        ],
        out_specs=[
            pl.BlockSpec((SEQ, LANES), lambda r, p: (r, p)),
            pl.BlockSpec((8, SEQ), lambda r, p: (p, r)),
        ],
        out_shape=[
            jax.ShapeDtypeStruct((count, width), low),
            jax.ShapeDtypeStruct((8 * pairs, count), f32),
        ],
        scratch_shapes=[pltpu.VMEM((SEQ, SEQ), f32)],
        compiler_params=pltpu.CompilerParams(vmem_limit_bytes=48 * 2**20),
        cost_estimate=pl.CostEstimate(
            flops=4 * count * SEQ * width, bytes_accessed=8 * count * width, transcendentals=0
        ),
        name="attend",
    )(packed, packed, packed, doc_col, doc_row)


def attend_back_kernel(
    q_ref, k_ref, v_ref, grad_ref, mixed_ref, lse_ref, doc_col, doc_row, out_ref, bias, grad_q_t
):
    pair = pl.program_id(1)

    @pl.when(pair == 0)
    def _():
        fill_bias(bias, doc_col, doc_row, True)

    wide = out_ref.shape[1] // 3
    place = [pl.ds(pl.multiple_of(s * wide + pair * LANES, LANES), LANES) for s in range(3)]
    query = q_ref[...] * jnp.asarray(scale_qk, low)
    grad = grad_ref[...]
    product = grad.astype(f32) * mixed_ref[...].astype(f32)
    upper = product.astype(low)
    lower = (product - upper.astype(f32)).astype(low)
    chooser = (
        lax.broadcasted_iota(jnp.int32, (8, LANES), 0)
        == lax.broadcasted_iota(jnp.int32, (8, LANES), 1) // HEAD_DIM
    ).astype(low)
    inner = dot_cols(chooser, upper) + dot_cols(chooser, lower)
    key_t = k_ref[...].T
    for block in range(0, SEQ, BLOCK):
        after = block + BLOCK
        key = k_ref[block:after, :]
        value = v_ref[block:after, :]
        grad_k, grad_v = [], []
        for head in range(2):
            scores = dot_cols(keep_head(key, head), query[block:, :])
            scores = jnp.minimum(scores, bias[block:after, block:])
            weights = jnp.exp(scores - lse_ref[head : head + 1, block:])
            grad_w = dot_cols(keep_head(value, head), grad[block:, :])
            grad_s = (weights * (grad_w - inner[head : head + 1, block:])).astype(low)
            grad_v.append(dot_rows(weights.astype(low), grad[block:, :]))
            grad_k.append(dot_rows(grad_s, query[block:, :]))
            rows = slice(head * HEAD_DIM, (head + 1) * HEAD_DIM)
            moved = dot_rows(key_t[rows, block:after], grad_s)
            if block == 0:
                grad_q_t[rows, :] = moved
            else:
                grad_q_t[rows, block:] += moved
        first = in_head((BLOCK, LANES), 0, 1)
        out_ref[block:after, place[1]] = jnp.where(first, grad_k[0], grad_k[1]).astype(low)
        out_ref[block:after, place[2]] = jnp.where(first, grad_v[0], grad_v[1]).astype(low)
    out_ref[:, place[0]] = (grad_q_t[...] * scale_qk).T.astype(low)


def attend_back(packed, grad_mixed, mixed, lse, doc_col, doc_row, first, count):
    tokens, wide = packed.shape
    pairs = wide // 3 // LANES

    def part(which):
        return pl.BlockSpec((SEQ, LANES), lambda r, p, w=which: (r, w * pairs + first + p))

    return pl.pallas_call(
        attend_back_kernel,
        grid=(tokens // SEQ, count),
        in_specs=[
            part(0),
            part(1),
            part(2),
            pl.BlockSpec((SEQ, LANES), lambda r, p: (r, first + p)),
            pl.BlockSpec((SEQ, LANES), lambda r, p: (r, first + p)),
            pl.BlockSpec((8, SEQ), lambda r, p: (first + p, r)),
            pl.BlockSpec((SEQ, 1), lambda r, p: (r, 0)),
            pl.BlockSpec((1, SEQ), lambda r, p: (0, r)),
        ],
        out_specs=pl.BlockSpec((SEQ, 3 * count * LANES), lambda r, p: (r, 0)),
        out_shape=jax.ShapeDtypeStruct((tokens, 3 * count * LANES), low),
        scratch_shapes=[pltpu.VMEM((SEQ, SEQ), f32), pltpu.VMEM((LANES, SEQ), f32)],
        compiler_params=pltpu.CompilerParams(vmem_limit_bytes=48 * 2**20),
        cost_estimate=pl.CostEstimate(
            flops=20 * tokens * SEQ * count * LANES,
            bytes_accessed=16 * tokens * count * LANES,
            transcendentals=0,
        ),
        name="attend_back",
    )(packed, packed, packed, grad_mixed, mixed, lse, doc_col, doc_row)


def norm_parts(values):
    centre = values - jnp.mean(values, axis=-1, keepdims=True)
    spread = jnp.mean(centre * centre, axis=-1, keepdims=True)
    scale = lax.rsqrt(spread + eps)
    return centre * scale, scale


def norm_back(grad, normal, scale, gain):
    moved = grad * gain
    return scale * (
        moved
        - jnp.mean(moved, axis=-1, keepdims=True)
        - normal * jnp.mean(moved * normal, axis=-1, keepdims=True)
    )


def sum_slabs(values):
    return jnp.sum(values.reshape(-1, 8, values.shape[1]), axis=0)


def after_attend_kernel(
    mixed_refs, proj_ref, x_ref, grad_ref, norm_ref, centre_ref, route_ref, slot_ref, outs, sent
):
    after_ref, grad_rows_ref, gate_ref, out_refs = outs[0], outs[1], outs[2], outs[3:]
    step = pl.program_id(0)
    attended = 0.0
    depth = 0
    for mixed in mixed_refs:
        wide = mixed.shape[1]
        attended = attended + dot_rows(mixed[...], proj_ref[depth : depth + wide, :])
        depth += wide
    after = x_ref[...].astype(f32) + attended
    after_ref[...] = after
    normal, _ = norm_parts(after)
    sent_low = (normal * norm_ref[2:3, :] + norm_ref[3:4, :]).astype(low)
    sent[pl.ds(pl.multiple_of(step * BLOCK, BLOCK), BLOCK), :] = sent_low
    experts = centre_ref.shape[0]
    onehot = route_ref[...] == lax.broadcasted_iota(jnp.int32, (BLOCK, experts), 1)
    picked = dot_rows(onehot.astype(low), centre_ref[...])
    gate = jax.nn.sigmoid(jnp.sum(sent_low.astype(f32) * picked, axis=-1, keepdims=True))
    grad_rows_ref[...] = (gate * grad_ref[...].astype(f32)).astype(low)
    gate_ref[...] = jnp.broadcast_to(gate, gate_ref.shape)

    @pl.when(step == pl.num_programs(0) - 1)
    def _():
        base = 0
        for out_ref in out_refs:
            for row in range(0, out_ref.shape[0], BLOCK):
                slots = lax.broadcasted_iota(jnp.int32, (BLOCK, sent.shape[0]), 0) + base
                place = (slots == slot_ref[...]).astype(low)
                out_ref[row : row + BLOCK, :] = dot_rows(place, sent[...]).astype(low)
                base += BLOCK


def after_attend(mixed, proj, tokens, out_grad, norms, centres, routes, slot_row, chunk_rows):
    count, width = tokens.shape
    chunks = len(chunk_rows)
    tile = pl.BlockSpec((BLOCK, width), lambda i: (i, 0))

    def kernel(*refs):
        n = len(mixed)
        after_attend_kernel(refs[:n], *refs[n : n + 7], refs[n + 7 : -1], refs[-1])

    return pl.pallas_call(
        kernel,
        grid=(count // BLOCK,),
        in_specs=[pl.BlockSpec((BLOCK, m.shape[1]), lambda i: (i, 0)) for m in mixed]
        + [
            pl.BlockSpec((width, width), lambda i: (0, 3)),
            tile,
            tile,
            pl.BlockSpec(norms.shape, lambda i: (0, 0)),
            pl.BlockSpec(centres.shape, lambda i: (0, 0)),
            pl.BlockSpec((BLOCK, 1), lambda i: (i, 0)),
            pl.BlockSpec((1, count), lambda i: (0, 0)),
        ],
        out_specs=[tile, tile, pl.BlockSpec((BLOCK, LANES), lambda i: (i, 0))]
        + [pl.BlockSpec((rows, width), lambda i: (0, 0)) for rows in chunk_rows],
        out_shape=[
            jax.ShapeDtypeStruct((count, width), f32),
            jax.ShapeDtypeStruct((count, width), low),
            jax.ShapeDtypeStruct((count, LANES), f32),
        ]
        + [jax.ShapeDtypeStruct((rows, width), low) for rows in chunk_rows],
        scratch_shapes=[pltpu.VMEM((count, width), low)],
        compiler_params=pltpu.CompilerParams(vmem_limit_bytes=48 * 2**20),
        cost_estimate=pl.CostEstimate(
            flops=2 * count * width * (width + sum(chunk_rows)),
            bytes_accessed=12 * count * width,
            transcendentals=0,
        ),
        name="after_attend",
    )(*mixed, proj, tokens, out_grad, norms, centres, routes, slot_row)


def picked_rows(slot_ref, row_refs):
    base, total = 0, 0.0
    for rows in row_refs:
        slots = lax.broadcasted_iota(jnp.int32, (BLOCK, rows.shape[0]), 1) + base
        place = (slots == slot_ref[...]).astype(low)
        total = total + dot_rows(place, rows[...])
        base += rows.shape[0]
    return total


def before_attend_back_kernel(
    row_refs, slot_ref, after_ref, grad_ref, norm_ref, proj_ref, outs
):
    grad_after_ref, grad_low_ref, grad_mixed_ref, sums_ref = outs
    grad_normed = picked_rows(slot_ref, row_refs)
    normal, scale = norm_parts(after_ref[...])
    grad_after = grad_ref[...].astype(f32) + norm_back(
        grad_normed, normal, scale, norm_ref[2:3, :]
    )
    grad_after_ref[...] = grad_after
    grad_low = grad_after.astype(low)
    grad_low_ref[...] = grad_low
    grad_mixed_ref[...] = dot_cols(grad_low, proj_ref[...]).astype(low)
    sums = jnp.concatenate([sum_slabs(grad_normed * normal), sum_slabs(grad_normed)], axis=0)

    @pl.when(pl.program_id(0) == 0)
    def _():
        sums_ref[...] = sums

    @pl.when(pl.program_id(0) > 0)
    def _():
        sums_ref[...] += sums


def before_attend_back(rows, slot_col, after, out_grad, norms, proj):
    count, width = after.shape
    tile = pl.BlockSpec((BLOCK, width), lambda i: (i, 0))

    def kernel(*refs):
        n = len(rows)
        before_attend_back_kernel(refs[:n], *refs[n : n + 5], refs[n + 5 :])

    return pl.pallas_call(
        kernel,
        grid=(count // BLOCK,),
        in_specs=[pl.BlockSpec(r.shape, lambda i: (0, 0)) for r in rows]
        + [
            pl.BlockSpec((BLOCK, 1), lambda i: (i, 0)),
            tile,
            tile,
            pl.BlockSpec(norms.shape, lambda i: (0, 0)),
            pl.BlockSpec((width, width), lambda i: (0, 3)),
        ],
        out_specs=[tile, tile, tile, pl.BlockSpec((16, width), lambda i: (0, 0))],
        out_shape=[
            jax.ShapeDtypeStruct((count, width), f32),
            jax.ShapeDtypeStruct((count, width), low),
            jax.ShapeDtypeStruct((count, width), low),
            jax.ShapeDtypeStruct((16, width), f32),
        ],
        compiler_params=pltpu.CompilerParams(vmem_limit_bytes=48 * 2**20),
        cost_estimate=pl.CostEstimate(
            flops=5 * count * width * width, bytes_accessed=16 * count * width, transcendentals=0
        ),
        name="before_attend_back",
    )(*rows, slot_col, after, out_grad, norms, proj)


def input_grad_kernel(plan, grad_refs, weight_ref, x_ref, norm_ref, grad_after_ref, outs):
    out_ref, sums_ref = outs
    grad_normed = 0.0
    each = weight_ref.shape[1] // 3
    for grad, (offset, wide) in zip(grad_refs, plan):
        for s in range(3):
            start = s * each + offset
            grad_normed = grad_normed + dot_cols(
                grad[:, s * wide : (s + 1) * wide], weight_ref[:, start : start + wide]
            )
    normal, scale = norm_parts(x_ref[...].astype(f32))
    out_ref[...] = grad_after_ref[...] + norm_back(grad_normed, normal, scale, norm_ref[0:1, :])
    sums = jnp.concatenate([sum_slabs(grad_normed * normal), sum_slabs(grad_normed)], axis=0)

    @pl.when(pl.program_id(0) == 0)
    def _():
        sums_ref[...] = sums

    @pl.when(pl.program_id(0) > 0)
    def _():
        sums_ref[...] += sums


def input_gradient(plan, grads, dense, tokens, norms, grad_after):
    count, width = tokens.shape
    tile = pl.BlockSpec((BLOCK, width), lambda i: (i, 0))

    def kernel(*refs):
        n = len(grads)
        input_grad_kernel(plan, refs[:n], *refs[n : n + 4], refs[n + 4 :])

    return pl.pallas_call(
        kernel,
        grid=(count // BLOCK,),
        in_specs=[pl.BlockSpec((BLOCK, g.shape[1]), lambda i: (i, 0)) for g in grads]
        + [
            pl.BlockSpec((width, 3 * width), lambda i: (0, 0)),
            tile,
            pl.BlockSpec(norms.shape, lambda i: (0, 0)),
            tile,
        ],
        out_specs=[tile, pl.BlockSpec((16, width), lambda i: (0, 0))],
        out_shape=[
            jax.ShapeDtypeStruct((count, width), f32),
            jax.ShapeDtypeStruct((16, width), f32),
        ],
        compiler_params=pltpu.CompilerParams(vmem_limit_bytes=48 * 2**20),
        cost_estimate=pl.CostEstimate(
            flops=6 * count * width * width, bytes_accessed=16 * count * width, transcendentals=0
        ),
        name="input_gradient",
    )(*grads, dense, tokens, norms, grad_after)


def activations_of(rows, slot_col, gate, after):
    count, width = after.shape
    tile = pl.BlockSpec((BLOCK, width), lambda i: (i, 0))

    def kernel(*refs):
        n = len(rows)
        slot_ref, gate_ref, after_ref, out_ref = refs[n:]
        found = picked_rows(slot_ref, refs[:n])
        out_ref[...] = (after_ref[...] + gate_ref[:, :1] * found).astype(low)

    return pl.pallas_call(
        kernel,
        grid=(count // BLOCK,),
        in_specs=[pl.BlockSpec(r.shape, lambda i: (0, 0)) for r in rows]
        + [
            pl.BlockSpec((BLOCK, 1), lambda i: (i, 0)),
            pl.BlockSpec((BLOCK, LANES), lambda i: (i, 0)),
            tile,
        ],
        out_specs=tile,
        out_shape=jax.ShapeDtypeStruct((count, width), low),
        compiler_params=pltpu.CompilerParams(vmem_limit_bytes=48 * 2**20),
        cost_estimate=pl.CostEstimate(
            flops=3 * count * width * width, bytes_accessed=10 * count * width, transcendentals=0
        ),
        name="activations_of",
    )(*rows, slot_col, gate, after)


def gelu_and_slope(x):
    point = 1.0 / (1.0 + (erfc_point * math.sqrt(0.5)) * jnp.abs(x))
    bell = jnp.exp(-0.5 * x * x)
    tail = erfc_terms[-1]
    for term in erfc_terms[-2::-1]:
        tail = tail * point + term
    tail = tail * point * bell
    below = jnp.where(x >= 0.0, 1.0 - tail, tail)
    return x * below, below + x * bell * (1.0 / math.sqrt(2.0 * math.pi))


def row_groups(experts, each):
    group = max(g for g in range(1, experts + 1) if experts % g == 0 and g * each <= BLOCK)
    return group, group * each


def expert_kernel(x_ref, in_ref, *rest):
    hidden_ref, slope_ref = rest[-2:]
    experts, each, width = x_ref.shape
    group, size = row_groups(experts, each)
    for e in range(0, experts, group):
        preact = dot_rows(x_ref[e : e + group].reshape(size, width), in_ref[...])
        value, slope = gelu_and_slope(preact)
        hidden_ref[e : e + group] = value.astype(low).reshape(group, each, -1)
        slope_ref[e : e + group] = slope.astype(low).reshape(group, each, -1)


def expert_forward(arrived, weight_in, chunk, chunks, buffer=None, tile=512):
    experts, each, width = arrived.shape
    inner = weight_in.shape[1]
    return pl.pallas_call(
        expert_kernel,
        grid=(inner // tile,),
        in_specs=[
            pl.BlockSpec((experts, each, width), lambda j: (0, 0, 0)),
            pl.BlockSpec((width, tile), lambda j: (0, j)),
        ]
        + ([] if buffer is None else [pl.BlockSpec(memory_space=pl.ANY)]),
        out_specs=[
            pl.BlockSpec((experts, each, tile), lambda j: (0, chunk, j)),
            pl.BlockSpec((experts, each, tile), lambda j: (0, 0, j)),
        ],
        out_shape=[
            jax.ShapeDtypeStruct((experts, chunks * each, inner), low),
            jax.ShapeDtypeStruct((experts, each, inner), low),
        ],
        input_output_aliases={} if buffer is None else {2: 0},
        compiler_params=pltpu.CompilerParams(vmem_limit_bytes=56 * 2**20),
        cost_estimate=pl.CostEstimate(
            flops=4 * experts * each * width * inner,
            bytes_accessed=4 * (experts * each + width) * inner,
            transcendentals=0,
        ),
        name="expert_forward",
    )(arrived, weight_in, *([] if buffer is None else [buffer]))


def expert_back_kernel(
    grad_ref, slope_ref, in_ref, out_ref, x_ref, result_ref, centre_ref, *rest
):
    grad_preact_ref, grad_rows_ref, grad_centre_ref, strips, grad_logit_ref = rest[-5:]
    step = pl.program_id(0)
    count, size, tile = strips.shape
    each = grad_ref.shape[1]

    @pl.when(step < count)
    def _():
        grad_hidden = dot_cols(grad_ref[...].reshape(size, -1), out_ref[...])
        grad_preact = (grad_hidden * slope_ref[...].reshape(size, tile).astype(f32)).astype(low)
        strips[step] = grad_preact
        grad_preact_ref[...] = grad_preact.reshape(-1, each, tile)

    @pl.when(step == count)
    def _():
        centre = centre_ref[...].astype(f32)
        grad_centre = jnp.zeros(grad_centre_ref.shape, f32)
        group, rows = row_groups(grad_ref.shape[0], each)
        for e in range(0, grad_ref.shape[0], group):
            x = x_ref[e : e + group].reshape(rows, -1).astype(f32)
            gate = jax.nn.sigmoid(jnp.sum(x * centre, axis=-1, keepdims=True))
            grad = grad_ref[e : e + group].reshape(rows, -1).astype(f32)
            moved = grad * result_ref[e : e + group].reshape(rows, -1).astype(f32)
            grad_logit = jnp.sum(moved, axis=-1, keepdims=True) * (1.0 - gate)
            grad_logit_ref[e * each : e * each + rows, :] = jnp.broadcast_to(
                grad_logit, (rows, LANES)
            )
            grad_centre = grad_centre + sum_slabs(grad_logit * x)
        grad_centre_ref[...] = grad_centre

    @pl.when(step >= count)
    def _():
        columns = grad_rows_ref.shape[2]
        start = pl.multiple_of((step - count) * columns, columns)
        centre = centre_ref[:, pl.ds(start, columns)].astype(f32)
        total = grad_logit_ref[:, :1] * centre
        for k in range(count):
            total = total + dot_cols(strips[k], in_ref[:, k * tile : (k + 1) * tile])
        grad_rows_ref[...] = total.astype(low).reshape(-1, each, columns)


def expert_back(
    grad_arrived,
    slope,
    weight_in,
    weight_out,
    arrived,
    result,
    centre,
    chunk,
    chunks,
    buffer=None,
    tile=1024,
    columns=256,
):
    experts, each, width = grad_arrived.shape
    inner = weight_in.shape[1]
    count = inner // tile
    alone = pl.BlockSpec((experts, each, width), lambda j: (0, 0, 0))

    def strip(j):
        return jnp.minimum(j, count - 1)

    def part(j):
        return jnp.maximum(j - count, 0)

    return pl.pallas_call(
        expert_back_kernel,
        grid=(count + width // columns,),
        in_specs=[
            alone,
            pl.BlockSpec((experts, each, tile), lambda j: (0, 0, strip(j))),
            pl.BlockSpec((columns, inner), lambda j: (part(j), 0)),
            pl.BlockSpec((tile, width), lambda j: (strip(j), 0)),
            alone,
            pl.BlockSpec((experts, each, width), lambda j: (0, chunk, 0)),
            pl.BlockSpec((1, width), lambda j: (0, 0)),
        ]
        + ([] if buffer is None else [pl.BlockSpec(memory_space=pl.ANY)]),
        out_specs=[
            pl.BlockSpec((experts, each, tile), lambda j: (0, chunk, strip(j))),
            pl.BlockSpec((experts, each, columns), lambda j: (0, 0, part(j))),
            pl.BlockSpec((8, width), lambda j: (0, 0)),
        ],
        out_shape=[
            jax.ShapeDtypeStruct((experts, chunks * each, inner), low),
            jax.ShapeDtypeStruct((experts, each, width), low),
            jax.ShapeDtypeStruct((8, width), f32),
        ],
        scratch_shapes=[
            pltpu.VMEM((count, experts * each, tile), low),
            pltpu.VMEM((experts * each, LANES), f32),
        ],
        input_output_aliases={} if buffer is None else {7: 0},
        compiler_params=pltpu.CompilerParams(vmem_limit_bytes=58 * 2**20),
        cost_estimate=pl.CostEstimate(
            flops=4 * experts * each * width * inner,
            bytes_accessed=4 * (experts * each + width) * inner,
            transcendentals=0,
        ),
        name="expert_back",
    )(
        grad_arrived,
        slope,
        weight_in,
        weight_out,
        arrived,
        result,
        centre,
        *([] if buffer is None else [buffer]),
    )


def swap(values, axis, distance):
    size = lax.axis_size(axis)
    return lax.ppermute(values, axis, [(i, i ^ distance) for i in range(size)])


def sum_over_cores(held):
    bit = lax.axis_index("dp") % 2
    halves = held.reshape((held.shape[0], held.shape[1] // 2, 2) + held.shape[2:])
    mine = lax.dynamic_index_in_dim(halves, bit, 2, keepdims=False)
    theirs = lax.dynamic_index_in_dim(halves, 1 - bit, 2, keepdims=False)
    return (mine.astype(f32) + swap(theirs, "dp", 1).astype(f32)).astype(low)


def sum_over_pairs(held, partners, keep):
    experts, dp = lax.axis_size("expert"), lax.axis_size("dp")
    total = lax.dynamic_index_in_dim(held, keep, 0, keepdims=False).astype(f32)
    for offset, (far, near) in enumerate(partners, 1):
        block = lax.dynamic_index_in_dim(held, jnp.bitwise_xor(keep, offset), 0, keepdims=False)
        perm = [
            (e * dp + d, (e ^ far) * dp + (d ^ near)) for e in range(experts) for d in range(dp)
        ]
        total = total + lax.ppermute(block, everywhere, perm).astype(f32)
    return total


def sum_near(held):
    far = held.shape[1]
    held = held.reshape((held.shape[0] // 2, 2 * far) + held.shape[2:]).swapaxes(0, 1)
    partners = [(i // far, i % far * 2) for i in range(1, 2 * far)]
    keep = lax.axis_index("expert") % 2 * far + lax.axis_index("dp") // 2
    return sum_over_pairs(held, partners, keep).astype(low)


def sum_far(held):
    partners = [(2 * i, 0) for i in range(1, held.shape[0])]
    return sum_over_pairs(held, partners, lax.axis_index("expert") // 2)


def in_order(*values):
    return lax.optimization_barrier(values)


def sum_everywhere(value):
    held = value.reshape(1, 1)
    for axis in ("dp", "expert"):
        distance = 1
        while distance < lax.axis_size(axis):
            held = held + swap(held, axis, distance)
            distance *= 2
    return held[0, 0]


def update(weight, moment, average, gradient, factor, rate):
    clipped = gradient * factor
    moment_new = momentum_rate * moment + clipped
    weight_new = weight - rate * (clipped + momentum_rate * moment_new)
    average_new = average_rate * average + (1.0 - average_rate) * weight_new
    return (weight_new, moment_new, average_new)


def shards(
    tokens,
    documents,
    routes,
    out_grad,
    norm_params,
    qkv_weight,
    proj_weight,
    centroids,
    expert_in,
    expert_out,
    norm_moment,
    qkv_moment,
    proj_moment,
    centroid_moment,
    in_moment,
    out_moment,
    norm_average,
    qkv_average,
    proj_average,
    centroid_average,
    in_average,
    out_average,
):
    local_tokens, width = tokens.shape
    experts = lax.axis_size("expert")
    dp = lax.axis_size("dp")
    devices = experts * dp
    slot_cap = max(2, 3 * local_tokens // (2 * experts))
    slots = experts * slot_cap
    chunks = 2 if slot_cap % 32 == 0 else 1
    half_cap = slot_cap // chunks
    rows_own = qkv_weight.shape[0]
    norm_own = norm_params.shape[1]
    centre_own = centroids.shape[1]
    groups = 4

    small = jnp.concatenate([norm_params.reshape(-1), centroids.reshape(-1)]).astype(low)
    small = jnp.pad(small, (0, rows_own * LANES - small.shape[0])).reshape(rows_own, LANES)
    dense = jnp.concatenate([qkv_weight.astype(low), proj_weight.astype(low), small], axis=1)
    dense = lax.all_gather(dense, everywhere, axis=0, tiled=True)
    weight_in = lax.all_gather(expert_in.astype(low), "dp", axis=1, tiled=True)[0]
    weight_out = lax.all_gather(expert_out.astype(low), "dp", axis=2, tiled=True)[0]

    small_full = dense[:, 4 * width :].reshape(devices, rows_own * LANES)
    norms = (
        small_full[:, : 4 * norm_own].reshape(devices, 4, norm_own).transpose(1, 0, 2)
    ).reshape(4, width).astype(f32)
    centre_table = small_full[:, 4 * norm_own : 4 * norm_own + centre_own].reshape(experts, width)

    route_ids = routes[:, 0]
    onehot = route_ids[:, None] == jnp.arange(experts, dtype=jnp.int32)[None, :]
    running = jnp.cumsum(onehot.astype(jnp.int32), axis=0)
    within = jnp.sum(running * onehot.astype(jnp.int32), axis=1) - 1
    slot_index = route_ids * slot_cap + within
    chunked = (within // half_cap * experts + route_ids) * half_cap + within % half_cap
    slot_row, slot_col = slot_index[None, :], slot_index[:, None]
    chunked_row, chunked_col = chunked[None, :], chunked[:, None]
    doc_col = documents[:, None]
    doc_row = documents[None, :]

    normed_low = layer_norm(tokens.astype(f32), norms[0], norms[1]).astype(low)
    packed = jnp.dot(normed_low, dense[:, : 3 * width], preferred_element_type=f32).astype(low)
    mixed, lse = attend(packed, doc_col, doc_row)
    after, grad_rows, gate, *outgoing = after_attend(
        [mixed],
        dense,
        tokens,
        out_grad,
        norms,
        centre_table,
        routes,
        chunked_row,
        [slots // chunks] * chunks,
    )

    def exchange(rows):
        rows = rows.reshape(experts, -1, width)
        return lax.all_to_all(rows, "expert", split_axis=0, concat_axis=0, tiled=True)

    grad_outgoing = []
    for c in range(chunks):
        own = jnp.arange(slots // chunks, dtype=jnp.int32)[:, None] + c * (slots // chunks)
        place = (own == chunked_row).astype(low)
        grad_outgoing.append(jnp.dot(place, grad_rows, preferred_element_type=f32).astype(low))
    arrived, slope, hidden = [], [], None
    for c in range(chunks):
        if c:
            arrived[c - 1], outgoing[c] = in_order(arrived[c - 1], outgoing[c])
        arrived.append(exchange(outgoing[c]))
    for c in range(chunks):
        if c == chunks - 1:
            arrived[c], grad_outgoing[0] = in_order(arrived[c], grad_outgoing[0])
        hidden, slope_c = expert_forward(arrived[c], weight_in, c, chunks, hidden)
        slope.append(slope_c)
        if c == 0 and chunks > 1:
            hidden, grad_outgoing[0] = in_order(hidden, grad_outgoing[0])
    grad_arrived = [exchange(grad_outgoing[0])]
    hidden = hidden.reshape(slots, -1)
    result = jnp.dot(hidden, weight_out, preferred_element_type=f32).astype(low)
    result = result.reshape(experts, slot_cap, width)
    for c in range(1, chunks):
        grad_arrived[c - 1], grad_outgoing[c], result = in_order(
            grad_arrived[c - 1], grad_outgoing[c], result
        )
        grad_arrived.append(exchange(grad_outgoing[c]))
    centre_row = lax.dynamic_slice_in_dim(centre_table, lax.axis_index("expert"), 1, 0)
    grad_preact = grad_weight_out = None
    grad_input, grad_centre = [], 0.0
    for c in range(chunks):
        last = c == chunks - 1
        if last:
            grad_weight_out = lax.dot_general(
                hidden,
                jnp.concatenate(grad_arrived, axis=1).reshape(slots, width),
                (((0,), (0,)), ((), ())),
                preferred_element_type=f32,
            ).astype(low)
            grad_arrived[c], grad_weight_out = in_order(grad_arrived[c], grad_weight_out)
        grad_preact, rows_c, centre_c = expert_back(
            grad_arrived[c],
            slope[c],
            weight_in,
            weight_out,
            arrived[c],
            result,
            centre_row,
            c,
            chunks,
            grad_preact,
        )
        if not last:
            rows_c, grad_arrived[c + 1] = in_order(rows_c, grad_arrived[c + 1])
        elif grad_input:
            rows_c, grad_input[-1] = in_order(rows_c, grad_input[-1])
        grad_input.append(exchange(rows_c).reshape(slots // chunks, width))
        grad_centre = grad_centre + jnp.sum(centre_c, axis=0)
    out_grad_w = lax.psum_scatter(grad_weight_out[None], "dp", scatter_dimension=2, tiled=True)
    arrived = jnp.concatenate(arrived, axis=1)
    grad_weight_in = lax.dot_general(
        arrived.reshape(slots, width),
        grad_preact.reshape(slots, -1),
        (((0,), (0,)), ((), ())),
        preferred_element_type=f32,
    ).astype(low)
    out_grad_w = out_grad_w.astype(f32)
    result, grad_input[-1], grad_weight_in = in_order(result, grad_input[-1], grad_weight_in)
    in_grad = lax.psum_scatter(grad_weight_in[None], "dp", scatter_dimension=1, tiled=True)
    in_grad = in_grad.astype(f32)
    returned = exchange(result).reshape(slots, width)

    grad_after, grad_low, grad_mixed, sums_two = before_attend_back(
        grad_input, chunked_col, after, out_grad, norms, dense
    )

    grad_proj = lax.dot_general(
        mixed, grad_low, (((0,), (0,)), ((), ())), preferred_element_type=f32
    ).astype(low)
    norm_two = jnp.sum(sums_two.reshape(2, 8, width), axis=1)
    norm_two = norm_two.reshape(2, devices, norm_own).transpose(1, 0, 2).reshape(devices, -1)
    mine = jnp.arange(experts)[:, None, None] == lax.axis_index("expert")
    centre_flat = jnp.where(mine, grad_centre.reshape(1, dp, centre_own), 0.0)
    extra = jnp.concatenate([norm_two, centre_flat.reshape(devices, centre_own)], axis=1)
    extra = jnp.pad(extra, ((0, 0), (0, rows_own * LANES - extra.shape[1]))).astype(low)
    extra = extra.reshape(devices * rows_own, LANES)
    each = width // LANES // groups
    wide = each * LANES

    def begin(parts):
        joined = jnp.concatenate(parts, axis=1)
        return joined.reshape(experts, dp, rows_own, joined.shape[1])

    def back_group(g):
        part = attend_back(packed, grad_mixed, mixed, lse, doc_col, doc_row, g * each, each)
        grad = lax.dot_general(
            normed_low, part, (((0,), (0,)), ((), ())), preferred_element_type=f32
        )
        return part, grad.astype(low)

    parts, grads = [], []
    rest = begin([grad_proj, extra])
    for g in range(groups):
        if g == 1:
            rest = sum_over_cores(rest)
            rest, grad_mixed = in_order(rest, grad_mixed)
        if g == groups - 1:
            first = sum_over_cores(begin(grads[: groups // 2]))
            rest = sum_near(rest)
            rest, first, grad_mixed, returned = in_order(rest, first, grad_mixed, returned)
        part, grad = back_group(g)
        grad, grad_mixed = in_order(grad, grad_mixed)
        parts.append(part)
        grads.append(grad)
    first = sum_near(first)
    second = sum_over_cores(begin(grads[groups // 2 :]))
    first, second, grad_after = in_order(first, second, grad_after)
    second = sum_near(second)
    input_grad, sums_one = input_gradient(
        [(g * wide, wide) for g in range(groups)], parts, dense, tokens, norms, grad_after
    )
    rest, first = sum_far(rest), sum_far(first)
    rest, first, second, sums_one, gate = in_order(rest, first, second, sums_one, gate)
    activations = activations_of([returned], slot_col, gate, after)
    second = sum_far(second)
    norm_one = jnp.sum(sums_one.reshape(2, 8, width), axis=1)
    norm_one = norm_one.reshape(2, devices, norm_own).transpose(1, 0, 2).reshape(devices, -1)
    norm_one = lax.all_to_all(norm_one, everywhere, split_axis=0, concat_axis=0, tiled=True)
    norm_one = jnp.sum(norm_one, axis=0).reshape(2, norm_own)

    proj_grad = rest[:, :width]
    extra = rest[:, width:].reshape(-1)
    norm_grad = jnp.concatenate([norm_one, extra[: 2 * norm_own].reshape(2, norm_own)], axis=0)
    centre_grad = extra[2 * norm_own : 2 * norm_own + centre_own].reshape(centroids.shape)
    owned = [first, second]
    qkv_grad = jnp.concatenate(
        [
            half[:, (3 * k + s) * wide : (3 * k + s + 1) * wide]
            for s in range(3)
            for half in owned
            for k in range(groups // 2)
        ],
        axis=1,
    )
    square_sum = (
        jnp.sum(qkv_grad * qkv_grad)
        + jnp.sum(proj_grad * proj_grad)
        + jnp.sum(norm_grad * norm_grad)
        + jnp.sum(centre_grad * centre_grad)
        + jnp.sum(in_grad * in_grad)
        + jnp.sum(out_grad_w * out_grad_w)
    )
    grad_norm = jnp.sqrt(sum_everywhere(square_sum))
    factor = clip_limit / jnp.maximum(grad_norm, clip_limit)
    norm_new = update(norm_params, norm_moment, norm_average, norm_grad, factor, norm_rate)
    qkv_new = update(qkv_weight, qkv_moment, qkv_average, qkv_grad, factor, learn_rate)
    proj_new = update(proj_weight, proj_moment, proj_average, proj_grad, factor, learn_rate)
    centre_new = update(
        centroids, centroid_moment, centroid_average, centre_grad, factor, learn_rate
    )
    in_new = update(expert_in, in_moment, in_average, in_grad, factor, learn_rate)
    out_new = update(expert_out, out_moment, out_average, out_grad_w, factor, learn_rate)
    return (
        activations,
        input_grad,
        grad_norm,
        norm_new[0],
        qkv_new[0],
        proj_new[0],
        centre_new[0],
        in_new[0],
        out_new[0],
        norm_new[1],
        qkv_new[1],
        proj_new[1],
        centre_new[1],
        in_new[1],
        out_new[1],
        norm_new[2],
        qkv_new[2],
        proj_new[2],
        centre_new[2],
        in_new[2],
        out_new[2],
    )


def solution(mesh):
    placed = (
        P(("expert", "dp"), None),
        P(("expert", "dp")),
        P(("expert", "dp"), None),
        P(("expert", "dp"), None),
        P(None, ("expert", "dp")),
        P(("expert", "dp"), None),
        P(("expert", "dp"), None),
        P("expert", "dp"),
        P("expert", "dp", None),
        P("expert", None, "dp"),
        P(None, ("expert", "dp")),
        P(("expert", "dp"), None),
        P(("expert", "dp"), None),
        P("expert", "dp"),
        P("expert", "dp", None),
        P("expert", None, "dp"),
        P(None, ("expert", "dp")),
        P(("expert", "dp"), None),
        P(("expert", "dp"), None),
        P("expert", "dp"),
        P("expert", "dp", None),
        P("expert", None, "dp"),
    )
    return jax.shard_map(
        shards,
        mesh=mesh,
        in_specs=placed,
        out_specs=(
            P(("expert", "dp"), None),
            P(("expert", "dp"), None),
            P(),
            P(None, ("expert", "dp")),
            P(("expert", "dp"), None),
            P(("expert", "dp"), None),
            P("expert", "dp"),
            P("expert", "dp", None),
            P("expert", None, "dp"),
            P(None, ("expert", "dp")),
            P(("expert", "dp"), None),
            P(("expert", "dp"), None),
            P("expert", "dp"),
            P("expert", "dp", None),
            P("expert", None, "dp"),
            P(None, ("expert", "dp")),
            P(("expert", "dp"), None),
            P(("expert", "dp"), None),
            P("expert", "dp"),
            P("expert", "dp", None),
            P("expert", None, "dp"),
        ),
        check_vma=False,
    )
```

```python
import functools
import math

import jax
import jax.numpy as jnp
from jax import lax
from jax.experimental import pallas as pl
from jax.experimental.pallas import tpu as pltpu
from jax.sharding import PartitionSpec as P

HEAD_DIM = 64
SEQ = 1024
LANES = 128
BLOCK = 256

eps = 1e-05
scale_qk = 0.125
momentum_rate = 0.9
learn_rate = 100.0
norm_rate = 500.0
average_rate = 0.9
clip_limit = 1.0
masked_score = -1000000000.0
everywhere = ("expert", "dp")
low = jnp.bfloat16
f32 = jnp.float32

erfc_point = 0.4
erfc_terms = (
    0.11596270714310389,
    0.08090178846816841,
    0.2341610172367065,
    -0.1854824771652721,
    0.35459055762612957,
    -0.10013360714943426,
)


def hint(microseconds):
    return pl.CostEstimate(
        flops=int(microseconds * 1.9e8), bytes_accessed=0, transcendentals=0
    )


def dot_rows(left, right):
    return lax.dot_general(left, right, (((1,), (0,)), ((), ())), preferred_element_type=f32)


def dot_cols(left, right):
    return lax.dot_general(left, right, (((1,), (1,)), ((), ())), preferred_element_type=f32)


def layer_norm(values, norm_gain, norm_bias):
    centre = values - jnp.mean(values, axis=-1, keepdims=True)
    spread = jnp.mean(centre * centre, axis=-1, keepdims=True)
    return centre * lax.rsqrt(spread + eps) * norm_gain + norm_bias


def fill_bias(bias, doc_of_rows, doc_of_cols, rows_are_keys):
    for block in range(0, SEQ, BLOCK):
        rows = lax.broadcasted_iota(jnp.int32, (BLOCK, SEQ), 0) + block
        cols = lax.broadcasted_iota(jnp.int32, (BLOCK, SEQ), 1)
        causal = (rows <= cols) if rows_are_keys else (rows >= cols)
        same = doc_of_rows[block : block + BLOCK, :] == doc_of_cols[...]
        bias[block : block + BLOCK, :] = jnp.where(same & causal, 3.0e38, masked_score)


def in_head(shape, head, axis):
    return lax.broadcasted_iota(jnp.int32, shape, axis) // HEAD_DIM == head


def keep_head(values, head):
    return jnp.where(in_head(values.shape, head, 1), values, jnp.zeros_like(values))


def attend_kernel(q_ref, k_ref, v_ref, doc_col, doc_row, mixed_ref, lse_ref, bias):
    @pl.when(pl.program_id(1) == 0)
    def _():
        fill_bias(bias, doc_col, doc_row, False)

    for block in range(0, SEQ, BLOCK):
        seen = block + BLOCK
        query = q_ref[block:seen, :] * jnp.asarray(scale_qk, low)
        outs, stats = [], []
        for head in range(2):
            scores = dot_cols(keep_head(query, head), k_ref[:seen, :])
            scores = jnp.minimum(scores, bias[block:seen, :seen])
            top = jnp.max(scores, axis=-1, keepdims=True)
            exponent = jnp.exp(scores - top)
            total = jnp.sum(exponent, axis=-1, keepdims=True)
            outs.append(dot_rows(exponent.astype(low), v_ref[:seen, :]) / total)
            stats.append(top + jnp.log(total))
        first = in_head((BLOCK, LANES), 0, 1)
        mixed_ref[block:seen, :] = jnp.where(first, outs[0], outs[1]).astype(low)
        lane = lax.broadcasted_iota(jnp.int32, (BLOCK, LANES), 1)
        both = jnp.where(lane == 0, stats[0], stats[1])
        lse_ref[:, block:seen] = both.T[:8, :]


def attend(packed, doc_col, doc_row):
    count, wide = packed.shape
    width = wide // 3
    pairs = width // LANES

    def part(which):
        return pl.BlockSpec((SEQ, LANES), lambda r, p, w=which: (r, w * pairs + p))

    return pl.pallas_call(
        attend_kernel,
        grid=(count // SEQ, pairs),
        in_specs=[
            part(0),
            part(1),
            part(2),
            pl.BlockSpec((SEQ, 1), lambda r, p: (r, 0)),
            pl.BlockSpec((1, SEQ), lambda r, p: (0, r)),
        ],
        out_specs=[
            pl.BlockSpec((SEQ, LANES), lambda r, p: (r, p)),
            pl.BlockSpec((8, SEQ), lambda r, p: (p, r)),
        ],
        out_shape=[
            jax.ShapeDtypeStruct((count, width), low),
            jax.ShapeDtypeStruct((8 * pairs, count), f32),
        ],
        scratch_shapes=[pltpu.VMEM((SEQ, SEQ), f32)],
        compiler_params=pltpu.CompilerParams(vmem_limit_bytes=48 * 2**20),
        cost_estimate=hint(29),
        name="attend",
    )(packed, packed, packed, doc_col, doc_row)


def attend_back_kernel(
    q_ref, k_ref, v_ref, grad_ref, mixed_ref, lse_ref, doc_col, doc_row, out_ref, bias, grad_q_t
):
    pair = pl.program_id(1)

    @pl.when(pair == 0)
    def _():
        fill_bias(bias, doc_col, doc_row, True)

    wide = out_ref.shape[1] // 3
    place = [pl.ds(pl.multiple_of(s * wide + pair * LANES, LANES), LANES) for s in range(3)]
    query = q_ref[...] * jnp.asarray(scale_qk, low)
    grad = grad_ref[...]
    product = grad.astype(f32) * mixed_ref[...].astype(f32)
    upper = product.astype(low)
    lower = (product - upper.astype(f32)).astype(low)
    chooser = (
        lax.broadcasted_iota(jnp.int32, (8, LANES), 0)
        == lax.broadcasted_iota(jnp.int32, (8, LANES), 1) // HEAD_DIM
    ).astype(low)
    inner = dot_cols(chooser, upper) + dot_cols(chooser, lower)
    key_t = k_ref[...].T
    for block in range(0, SEQ, BLOCK):
        after = block + BLOCK
        key = k_ref[block:after, :]
        value = v_ref[block:after, :]
        grad_k, grad_v = [], []
        for head in range(2):
            scores = dot_cols(keep_head(key, head), query[block:, :])
            scores = jnp.minimum(scores, bias[block:after, block:])
            weights = jnp.exp(scores - lse_ref[head : head + 1, block:])
            grad_w = dot_cols(keep_head(value, head), grad[block:, :])
            grad_s = (weights * (grad_w - inner[head : head + 1, block:])).astype(low)
            grad_v.append(dot_rows(weights.astype(low), grad[block:, :]))
            grad_k.append(dot_rows(grad_s, query[block:, :]))
            rows = slice(head * HEAD_DIM, (head + 1) * HEAD_DIM)
            moved = dot_rows(key_t[rows, block:after], grad_s)
            if block == 0:
                grad_q_t[rows, :] = moved
            else:
                grad_q_t[rows, block:] += moved
        first = in_head((BLOCK, LANES), 0, 1)
        out_ref[block:after, place[1]] = jnp.where(first, grad_k[0], grad_k[1]).astype(low)
        out_ref[block:after, place[2]] = jnp.where(first, grad_v[0], grad_v[1]).astype(low)
    out_ref[:, place[0]] = (grad_q_t[...] * scale_qk).T.astype(low)


def attend_back(packed, grad_mixed, mixed, lse, doc_col, doc_row, first, count):
    tokens, wide = packed.shape
    pairs = wide // 3 // LANES

    def part(which):
        return pl.BlockSpec((SEQ, LANES), lambda r, p, w=which: (r, w * pairs + first + p))

    return pl.pallas_call(
        attend_back_kernel,
        grid=(tokens // SEQ, count),
        in_specs=[
            part(0),
            part(1),
            part(2),
            pl.BlockSpec((SEQ, LANES), lambda r, p: (r, first + p)),
            pl.BlockSpec((SEQ, LANES), lambda r, p: (r, first + p)),
            pl.BlockSpec((8, SEQ), lambda r, p: (first + p, r)),
            pl.BlockSpec((SEQ, 1), lambda r, p: (r, 0)),
            pl.BlockSpec((1, SEQ), lambda r, p: (0, r)),
        ],
        out_specs=pl.BlockSpec((SEQ, 3 * count * LANES), lambda r, p: (r, 0)),
        out_shape=jax.ShapeDtypeStruct((tokens, 3 * count * LANES), low),
        scratch_shapes=[pltpu.VMEM((SEQ, SEQ), f32), pltpu.VMEM((LANES, SEQ), f32)],
        compiler_params=pltpu.CompilerParams(vmem_limit_bytes=48 * 2**20),
        cost_estimate=hint(4.8 * count),
        name="attend_back",
    )(packed, packed, packed, grad_mixed, mixed, lse, doc_col, doc_row)


def norm_parts(values):
    centre = values - jnp.mean(values, axis=-1, keepdims=True)
    spread = jnp.mean(centre * centre, axis=-1, keepdims=True)
    scale = lax.rsqrt(spread + eps)
    return centre * scale, scale


def norm_back(grad, normal, scale, gain):
    moved = grad * gain
    return scale * (
        moved
        - jnp.mean(moved, axis=-1, keepdims=True)
        - normal * jnp.mean(moved * normal, axis=-1, keepdims=True)
    )


def sum_slabs(values):
    return jnp.sum(values.reshape(-1, 8, values.shape[1]), axis=0)


def after_attend_kernel(
    mixed_refs, proj_ref, x_ref, grad_ref, norm_ref, centre_ref, route_ref, slot_ref, outs, sent
):
    after_ref, grad_rows_ref, gate_ref, out_refs = outs[0], outs[1], outs[2], outs[3:]
    step = pl.program_id(0)
    attended = 0.0
    depth = 0
    for mixed in mixed_refs:
        wide = mixed.shape[1]
        attended = attended + dot_rows(mixed[...], proj_ref[depth : depth + wide, :])
        depth += wide
    after = x_ref[...].astype(f32) + attended
    after_ref[...] = after
    normal, _ = norm_parts(after)
    sent_low = (normal * norm_ref[2:3, :] + norm_ref[3:4, :]).astype(low)
    sent[pl.ds(pl.multiple_of(step * BLOCK, BLOCK), BLOCK), :] = sent_low
    experts = centre_ref.shape[0]
    onehot = route_ref[...] == lax.broadcasted_iota(jnp.int32, (BLOCK, experts), 1)
    picked = dot_rows(onehot.astype(low), centre_ref[...])
    gate = jax.nn.sigmoid(jnp.sum(sent_low.astype(f32) * picked, axis=-1, keepdims=True))
    grad_rows_ref[...] = (gate * grad_ref[...].astype(f32)).astype(low)
    gate_ref[...] = jnp.broadcast_to(gate, gate_ref.shape)

    @pl.when(step == pl.num_programs(0) - 1)
    def _():
        base = 0
        for out_ref in out_refs:
            for row in range(0, out_ref.shape[0], BLOCK):
                slots = lax.broadcasted_iota(jnp.int32, (BLOCK, sent.shape[0]), 0) + base
                place = (slots == slot_ref[...]).astype(low)
                out_ref[row : row + BLOCK, :] = dot_rows(place, sent[...]).astype(low)
                base += BLOCK


def after_attend(mixed, proj, tokens, out_grad, norms, centres, routes, slot_row, chunk_rows):
    count, width = tokens.shape
    chunks = len(chunk_rows)
    tile = pl.BlockSpec((BLOCK, width), lambda i: (i, 0))

    def kernel(*refs):
        n = len(mixed)
        after_attend_kernel(refs[:n], *refs[n : n + 7], refs[n + 7 : -1], refs[-1])

    return pl.pallas_call(
        kernel,
        grid=(count // BLOCK,),
        in_specs=[pl.BlockSpec((BLOCK, m.shape[1]), lambda i: (i, 0)) for m in mixed]
        + [
            pl.BlockSpec((width, width), lambda i: (0, 3)),
            tile,
            tile,
            pl.BlockSpec(norms.shape, lambda i: (0, 0)),
            pl.BlockSpec(centres.shape, lambda i: (0, 0)),
            pl.BlockSpec((BLOCK, 1), lambda i: (i, 0)),
            pl.BlockSpec((1, count), lambda i: (0, 0)),
        ],
        out_specs=[tile, tile, pl.BlockSpec((BLOCK, LANES), lambda i: (i, 0))]
        + [pl.BlockSpec((rows, width), lambda i: (0, 0)) for rows in chunk_rows],
        out_shape=[
            jax.ShapeDtypeStruct((count, width), f32),
            jax.ShapeDtypeStruct((count, width), low),
            jax.ShapeDtypeStruct((count, LANES), f32),
        ]
        + [jax.ShapeDtypeStruct((rows, width), low) for rows in chunk_rows],
        scratch_shapes=[pltpu.VMEM((count, width), low)],
        compiler_params=pltpu.CompilerParams(vmem_limit_bytes=48 * 2**20),
        cost_estimate=hint(13),
        name="after_attend",
    )(*mixed, proj, tokens, out_grad, norms, centres, routes, slot_row)


def picked_rows(slot_ref, row_refs):
    base, total = 0, 0.0
    for rows in row_refs:
        slots = lax.broadcasted_iota(jnp.int32, (BLOCK, rows.shape[0]), 1) + base
        place = (slots == slot_ref[...]).astype(low)
        total = total + dot_rows(place, rows[...])
        base += rows.shape[0]
    return total


def before_attend_back_kernel(
    row_refs, slot_ref, after_ref, grad_ref, norm_ref, proj_ref, outs
):
    grad_after_ref, grad_low_ref, grad_mixed_ref, sums_ref = outs
    grad_normed = picked_rows(slot_ref, row_refs)
    normal, scale = norm_parts(after_ref[...])
    grad_after = grad_ref[...].astype(f32) + norm_back(
        grad_normed, normal, scale, norm_ref[2:3, :]
    )
    grad_after_ref[...] = grad_after
    grad_low = grad_after.astype(low)
    grad_low_ref[...] = grad_low
    grad_mixed_ref[...] = dot_cols(grad_low, proj_ref[...]).astype(low)
    sums = jnp.concatenate([sum_slabs(grad_normed * normal), sum_slabs(grad_normed)], axis=0)

    @pl.when(pl.program_id(0) == 0)
    def _():
        sums_ref[...] = sums

    @pl.when(pl.program_id(0) > 0)
    def _():
        sums_ref[...] += sums


def before_attend_back(rows, slot_col, after, out_grad, norms, proj):
    count, width = after.shape
    tile = pl.BlockSpec((BLOCK, width), lambda i: (i, 0))

    def kernel(*refs):
        n = len(rows)
        before_attend_back_kernel(refs[:n], *refs[n : n + 5], refs[n + 5 :])

    return pl.pallas_call(
        kernel,
        grid=(count // BLOCK,),
        in_specs=[pl.BlockSpec(r.shape, lambda i: (0, 0)) for r in rows]
        + [
            pl.BlockSpec((BLOCK, 1), lambda i: (i, 0)),
            tile,
            tile,
            pl.BlockSpec(norms.shape, lambda i: (0, 0)),
            pl.BlockSpec((width, width), lambda i: (0, 3)),
        ],
        out_specs=[tile, tile, tile, pl.BlockSpec((16, width), lambda i: (0, 0))],
        out_shape=[
            jax.ShapeDtypeStruct((count, width), f32),
            jax.ShapeDtypeStruct((count, width), low),
            jax.ShapeDtypeStruct((count, width), low),
            jax.ShapeDtypeStruct((16, width), f32),
        ],
        compiler_params=pltpu.CompilerParams(vmem_limit_bytes=48 * 2**20),
        cost_estimate=hint(12),
        name="before_attend_back",
    )(*rows, slot_col, after, out_grad, norms, proj)


def input_grad_kernel(plan, grad_refs, weight_ref, x_ref, norm_ref, grad_after_ref, outs):
    out_ref, sums_ref = outs
    grad_normed = 0.0
    each = weight_ref.shape[1] // 3
    for grad, (offset, wide) in zip(grad_refs, plan):
        for s in range(3):
            start = s * each + offset
            grad_normed = grad_normed + dot_cols(
                grad[:, s * wide : (s + 1) * wide], weight_ref[:, start : start + wide]
            )
    normal, scale = norm_parts(x_ref[...].astype(f32))
    out_ref[...] = grad_after_ref[...] + norm_back(grad_normed, normal, scale, norm_ref[0:1, :])
    sums = jnp.concatenate([sum_slabs(grad_normed * normal), sum_slabs(grad_normed)], axis=0)

    @pl.when(pl.program_id(0) == 0)
    def _():
        sums_ref[...] = sums

    @pl.when(pl.program_id(0) > 0)
    def _():
        sums_ref[...] += sums


def input_gradient(plan, grads, dense, tokens, norms, grad_after):
    count, width = tokens.shape
    tile = pl.BlockSpec((BLOCK, width), lambda i: (i, 0))

    def kernel(*refs):
        n = len(grads)
        input_grad_kernel(plan, refs[:n], *refs[n : n + 4], refs[n + 4 :])

    return pl.pallas_call(
        kernel,
        grid=(count // BLOCK,),
        in_specs=[pl.BlockSpec((BLOCK, g.shape[1]), lambda i: (i, 0)) for g in grads]
        + [
            pl.BlockSpec((width, 3 * width), lambda i: (0, 0)),
            tile,
            pl.BlockSpec(norms.shape, lambda i: (0, 0)),
            tile,
        ],
        out_specs=[tile, pl.BlockSpec((16, width), lambda i: (0, 0))],
        out_shape=[
            jax.ShapeDtypeStruct((count, width), f32),
            jax.ShapeDtypeStruct((16, width), f32),
        ],
        compiler_params=pltpu.CompilerParams(vmem_limit_bytes=48 * 2**20),
        cost_estimate=hint(14),
        name="input_gradient",
    )(*grads, dense, tokens, norms, grad_after)


def activations_of(rows, slot_col, gate, after):
    count, width = after.shape
    tile = pl.BlockSpec((BLOCK, width), lambda i: (i, 0))

    def kernel(*refs):
        n = len(rows)
        slot_ref, gate_ref, after_ref, out_ref = refs[n:]
        found = picked_rows(slot_ref, refs[:n])
        out_ref[...] = (after_ref[...] + gate_ref[:, :1] * found).astype(low)

    return pl.pallas_call(
        kernel,
        grid=(count // BLOCK,),
        in_specs=[pl.BlockSpec(r.shape, lambda i: (0, 0)) for r in rows]
        + [
            pl.BlockSpec((BLOCK, 1), lambda i: (i, 0)),
            pl.BlockSpec((BLOCK, LANES), lambda i: (i, 0)),
            tile,
        ],
        out_specs=tile,
        out_shape=jax.ShapeDtypeStruct((count, width), low),
        compiler_params=pltpu.CompilerParams(vmem_limit_bytes=48 * 2**20),
        cost_estimate=hint(7.5),
        name="activations_of",
    )(*rows, slot_col, gate, after)


def gelu_and_slope(x):
    point = 1.0 / (1.0 + (erfc_point * math.sqrt(0.5)) * jnp.abs(x))
    bell = jnp.exp(-0.5 * x * x)
    tail = erfc_terms[-1]
    for term in erfc_terms[-2::-1]:
        tail = tail * point + term
    tail = tail * point * bell
    below = jnp.where(x >= 0.0, 1.0 - tail, tail)
    return x * below, below + x * bell * (1.0 / math.sqrt(2.0 * math.pi))


def row_groups(experts, each):
    group = max(g for g in range(1, experts + 1) if experts % g == 0 and g * each <= BLOCK)
    return group, group * each


def expert_kernel(x_ref, in_ref, *rest):
    hidden_ref, slope_ref = rest[-2:]
    experts, each, width = x_ref.shape
    group, size = row_groups(experts, each)
    for e in range(0, experts, group):
        preact = dot_rows(x_ref[e : e + group].reshape(size, width), in_ref[...])
        value, slope = gelu_and_slope(preact)
        hidden_ref[e : e + group] = value.astype(low).reshape(group, each, -1)
        slope_ref[e : e + group] = slope.astype(low).reshape(group, each, -1)


def expert_forward(arrived, weight_in, chunk, chunks, buffer=None, tile=512):
    experts, each, width = arrived.shape
    inner = weight_in.shape[1]
    return pl.pallas_call(
        expert_kernel,
        grid=(inner // tile,),
        in_specs=[
            pl.BlockSpec((experts, each, width), lambda j: (0, 0, 0)),
            pl.BlockSpec((width, tile), lambda j: (0, j)),
        ]
        + ([] if buffer is None else [pl.BlockSpec(memory_space=pl.ANY)]),
        out_specs=[
            pl.BlockSpec((experts, each, tile), lambda j: (0, chunk, j)),
            pl.BlockSpec((experts, each, tile), lambda j: (0, 0, j)),
        ],
        out_shape=[
            jax.ShapeDtypeStruct((experts, chunks * each, inner), low),
            jax.ShapeDtypeStruct((experts, each, inner), low),
        ],
        input_output_aliases={} if buffer is None else {2: 0},
        compiler_params=pltpu.CompilerParams(vmem_limit_bytes=56 * 2**20),
        cost_estimate=hint(21),
        name="expert_forward",
    )(arrived, weight_in, *([] if buffer is None else [buffer]))


def expert_back_kernel(
    grad_ref, slope_ref, in_ref, out_ref, x_ref, result_ref, centre_ref, *rest
):
    grad_preact_ref, grad_rows_ref, grad_centre_ref, strips, grad_logit_ref = rest[-5:]
    step = pl.program_id(0)
    count, size, tile = strips.shape
    each = grad_ref.shape[1]

    @pl.when(step < count)
    def _():
        grad_hidden = dot_cols(grad_ref[...].reshape(size, -1), out_ref[...])
        grad_preact = (grad_hidden * slope_ref[...].reshape(size, tile).astype(f32)).astype(low)
        strips[step] = grad_preact
        grad_preact_ref[...] = grad_preact.reshape(-1, each, tile)

    @pl.when(step == count)
    def _():
        centre = centre_ref[...].astype(f32)
        grad_centre = jnp.zeros(grad_centre_ref.shape, f32)
        group, rows = row_groups(grad_ref.shape[0], each)
        for e in range(0, grad_ref.shape[0], group):
            x = x_ref[e : e + group].reshape(rows, -1).astype(f32)
            gate = jax.nn.sigmoid(jnp.sum(x * centre, axis=-1, keepdims=True))
            grad = grad_ref[e : e + group].reshape(rows, -1).astype(f32)
            moved = grad * result_ref[e : e + group].reshape(rows, -1).astype(f32)
            grad_logit = jnp.sum(moved, axis=-1, keepdims=True) * (1.0 - gate)
            grad_logit_ref[e * each : e * each + rows, :] = jnp.broadcast_to(
                grad_logit, (rows, LANES)
            )
            grad_centre = grad_centre + sum_slabs(grad_logit * x)
        grad_centre_ref[...] = grad_centre

    @pl.when(step >= count)
    def _():
        columns = grad_rows_ref.shape[2]
        start = pl.multiple_of((step - count) * columns, columns)
        centre = centre_ref[:, pl.ds(start, columns)].astype(f32)
        total = grad_logit_ref[:, :1] * centre
        for k in range(count):
            total = total + dot_cols(strips[k], in_ref[:, k * tile : (k + 1) * tile])
        grad_rows_ref[...] = total.astype(low).reshape(-1, each, columns)


def expert_back(
    grad_arrived,
    slope,
    weight_in,
    weight_out,
    arrived,
    result,
    centre,
    chunk,
    chunks,
    buffer=None,
    tile=1024,
    columns=256,
):
    experts, each, width = grad_arrived.shape
    inner = weight_in.shape[1]
    count = inner // tile
    alone = pl.BlockSpec((experts, each, width), lambda j: (0, 0, 0))

    def strip(j):
        return jnp.minimum(j, count - 1)

    def part(j):
        return jnp.maximum(j - count, 0)

    return pl.pallas_call(
        expert_back_kernel,
        grid=(count + width // columns,),
        in_specs=[
            alone,
            pl.BlockSpec((experts, each, tile), lambda j: (0, 0, strip(j))),
            pl.BlockSpec((columns, inner), lambda j: (part(j), 0)),
            pl.BlockSpec((tile, width), lambda j: (strip(j), 0)),
            alone,
            pl.BlockSpec((experts, each, width), lambda j: (0, chunk, 0)),
            pl.BlockSpec((1, width), lambda j: (0, 0)),
        ]
        + ([] if buffer is None else [pl.BlockSpec(memory_space=pl.ANY)]),
        out_specs=[
            pl.BlockSpec((experts, each, tile), lambda j: (0, chunk, strip(j))),
            pl.BlockSpec((experts, each, columns), lambda j: (0, 0, part(j))),
            pl.BlockSpec((8, width), lambda j: (0, 0)),
        ],
        out_shape=[
            jax.ShapeDtypeStruct((experts, chunks * each, inner), low),
            jax.ShapeDtypeStruct((experts, each, width), low),
            jax.ShapeDtypeStruct((8, width), f32),
        ],
        scratch_shapes=[
            pltpu.VMEM((count, experts * each, tile), low),
            pltpu.VMEM((experts * each, LANES), f32),
        ],
        input_output_aliases={} if buffer is None else {7: 0},
        compiler_params=pltpu.CompilerParams(vmem_limit_bytes=58 * 2**20),
        cost_estimate=hint(23),
        name="expert_back",
    )(
        grad_arrived,
        slope,
        weight_in,
        weight_out,
        arrived,
        result,
        centre,
        *([] if buffer is None else [buffer]),
    )


def weight_grads_kernel(chunks, refs):
    x_refs, grad_refs = refs[:chunks], refs[chunks : 2 * chunks]
    grad_preact_ref, hidden_ref, in_out_ref, out_out_ref, turned = refs[2 * chunks :]
    step = pl.program_id(0)
    half = pl.num_programs(0) // 2

    def turn_rows(chunk_refs):
        for c, ref in enumerate(chunk_refs):
            experts, each, width = ref.shape
            group, size = row_groups(experts, each)
            for e in range(0, experts, group):
                turned[c, :, e * each : e * each + size] = (
                    ref[e : e + group].reshape(size, width).T
                )

    pl.when(step == 0)(lambda: turn_rows(x_refs))
    pl.when(step == half)(lambda: turn_rows(grad_refs))

    def multiply(ref, out_ref):
        experts, slots, tile = ref.shape
        each = slots // chunks
        right = [
            ref[:, c * each : (c + 1) * each, :].reshape(experts * each, tile)
            for c in range(chunks)
        ]
        for row in range(0, turned.shape[1], BLOCK):
            rows = slice(row, row + BLOCK)
            total = dot_rows(turned[0, rows, :], right[0])
            for c in range(1, chunks):
                total = total + dot_rows(turned[c, rows, :], right[c])
            out_ref[rows, :] = total.astype(low)

    pl.when(step < half)(lambda: multiply(grad_preact_ref, in_out_ref))
    pl.when(step >= half)(lambda: multiply(hidden_ref, out_out_ref))


def weight_grads(arrived, grad_arrived, grad_preact, hidden, tile=1024):
    chunks = len(arrived)
    experts, each, width = arrived[0].shape
    slots, inner = hidden.shape[1:]
    half = inner // tile
    whole = pl.BlockSpec((experts, each, width), lambda j: (0, 0, 0))

    def first(j):
        return jnp.minimum(j, half - 1)

    def second(j):
        return jnp.maximum(j - half, 0)

    return pl.pallas_call(
        lambda *refs: weight_grads_kernel(chunks, refs),
        grid=(2 * half,),
        in_specs=[whole] * (2 * chunks)
        + [
            pl.BlockSpec((experts, slots, tile), lambda j: (0, 0, first(j))),
            pl.BlockSpec((experts, slots, tile), lambda j: (0, 0, second(j))),
        ],
        out_specs=[
            pl.BlockSpec((width, tile), lambda j: (0, first(j))),
            pl.BlockSpec((width, tile), lambda j: (0, second(j))),
        ],
        out_shape=[jax.ShapeDtypeStruct((width, inner), low)] * 2,
        scratch_shapes=[pltpu.VMEM((chunks, width, experts * each), low)],
        compiler_params=pltpu.CompilerParams(vmem_limit_bytes=58 * 2**20),
        cost_estimate=hint(38),
        name="weight_grads",
    )(*arrived, *grad_arrived, grad_preact, hidden)


def turn_kernel(in_ref, out_ref, square_ref):
    values = in_ref[...].astype(f32)
    out_ref[...] = in_ref[...].T.astype(f32)
    square = sum_slabs(values * values)

    @pl.when(pl.program_id(0) == 0)
    def _():
        square_ref[...] = square

    @pl.when(pl.program_id(0) > 0)
    def _():
        square_ref[...] += square


def turn(values, tile=512):
    rows, columns = values.shape
    turned, square = pl.pallas_call(
        turn_kernel,
        grid=(columns // tile,),
        in_specs=[pl.BlockSpec((rows, tile), lambda j: (0, j))],
        out_specs=[
            pl.BlockSpec((tile, rows), lambda j: (j, 0)),
            pl.BlockSpec((8, tile), lambda j: (0, 0)),
        ],
        out_shape=[
            jax.ShapeDtypeStruct((columns, rows), f32),
            jax.ShapeDtypeStruct((8, tile), f32),
        ],
        cost_estimate=hint(3),
        name="turn",
    )(values)
    return turned, jnp.sum(square)


def swap(values, axis, distance):
    size = lax.axis_size(axis)
    return lax.ppermute(values, axis, [(i, i ^ distance) for i in range(size)])


def sum_halves(parts, axis, bit, at):
    own = (lax.axis_index(axis) // bit) % 2

    def side(which):
        picked = []
        for part in parts:
            shape = part.shape
            halves = part.reshape(shape[:at] + (shape[at] // 2, 2) + shape[at + 1 :])
            picked.append(lax.dynamic_index_in_dim(halves, which, at + 1, keepdims=False))
        return jnp.concatenate(picked, axis=-1)

    return (side(own).astype(f32) + swap(side(1 - own), axis, bit).astype(f32)).astype(low)


def sum_over_cores(parts):
    return sum_halves(parts, "dp", 1, 1)


def sum_over_neighbours(held):
    return sum_halves([held], "expert", 1, 0)


def sum_over_pairs(held, partners, keep):
    experts, dp = lax.axis_size("expert"), lax.axis_size("dp")
    total = lax.dynamic_index_in_dim(held, keep, 0, keepdims=False).astype(f32)
    for offset, (far, near) in enumerate(partners, 1):
        block = lax.dynamic_index_in_dim(held, jnp.bitwise_xor(keep, offset), 0, keepdims=False)
        perm = [
            (e * dp + d, (e ^ far) * dp + (d ^ near)) for e in range(experts) for d in range(dp)
        ]
        total = total + lax.ppermute(block, everywhere, perm).astype(f32)
    return total


def sum_near(held):
    near = held.shape[1]
    held = held.reshape((held.shape[0] // 2, 2 * near) + held.shape[2:]).swapaxes(0, 1)
    partners = [(i // near, i % near * 2) for i in range(1, 2 * near)]
    keep = lax.axis_index("expert") % 2 * near + lax.axis_index("dp") // 2
    return sum_over_pairs(held, partners, keep).astype(low)


def sum_far(held):
    partners = [(2 * i, 0) for i in range(1, held.shape[0])]
    return sum_over_pairs(held, partners, lax.axis_index("expert") // 2)


def sum_across(held):
    partners = [(0, 2 * i) for i in range(1, held.shape[0])]
    return sum_over_pairs(held, partners, lax.axis_index("dp") // 2)


def in_order(*values):
    return lax.optimization_barrier(values)


def sum_everywhere(value):
    held = value.reshape(1, 1)
    for axis in ("dp", "expert"):
        distance = 1
        while distance < lax.axis_size(axis):
            held = held + swap(held, axis, distance)
            distance *= 2
    return held[0, 0]


def update(weight, moment, average, gradient, factor, rate):
    clipped = gradient * factor
    moment_new = momentum_rate * moment + clipped
    weight_new = weight - rate * (clipped + momentum_rate * moment_new)
    average_new = average_rate * average + (1.0 - average_rate) * weight_new
    return (weight_new, moment_new, average_new)


def shards(
    tokens,
    documents,
    routes,
    out_grad,
    norm_params,
    qkv_weight,
    proj_weight,
    centroids,
    expert_in,
    expert_out,
    norm_moment,
    qkv_moment,
    proj_moment,
    centroid_moment,
    in_moment,
    out_moment,
    norm_average,
    qkv_average,
    proj_average,
    centroid_average,
    in_average,
    out_average,
):
    local_tokens, width = tokens.shape
    experts = lax.axis_size("expert")
    dp = lax.axis_size("dp")
    devices = experts * dp
    slot_cap = max(2, 3 * local_tokens // (2 * experts))
    slots = experts * slot_cap
    chunks = 2 if slot_cap % 32 == 0 else 1
    half_cap = slot_cap // chunks
    rows_own = qkv_weight.shape[0]
    norm_own = norm_params.shape[1]
    centre_own = centroids.shape[1]
    groups = 4

    small = jnp.concatenate([norm_params.reshape(-1), centroids.reshape(-1)]).astype(low)
    small = jnp.pad(small, (0, rows_own * LANES - small.shape[0])).reshape(rows_own, LANES)
    dense = jnp.concatenate([qkv_weight.astype(low), proj_weight.astype(low), small], axis=1)
    dense = lax.all_gather(dense, everywhere, axis=0, tiled=True)
    weight_in = lax.all_gather(expert_in.astype(low), "dp", axis=1, tiled=True)[0]
    weight_out = lax.all_gather(expert_out.astype(low), "dp", axis=2, tiled=True)[0]

    small_full = dense[:, 4 * width :].reshape(devices, rows_own * LANES)
    norms = (
        small_full[:, : 4 * norm_own].reshape(devices, 4, norm_own).transpose(1, 0, 2)
    ).reshape(4, width).astype(f32)
    centre_table = small_full[:, 4 * norm_own : 4 * norm_own + centre_own].reshape(experts, width)

    route_ids = routes[:, 0]
    onehot = route_ids[:, None] == jnp.arange(experts, dtype=jnp.int32)[None, :]
    running = jnp.cumsum(onehot.astype(jnp.int32), axis=0)
    within = jnp.sum(running * onehot.astype(jnp.int32), axis=1) - 1
    slot_index = route_ids * slot_cap + within
    chunked = (within // half_cap * experts + route_ids) * half_cap + within % half_cap
    slot_row, slot_col = slot_index[None, :], slot_index[:, None]
    chunked_row, chunked_col = chunked[None, :], chunked[:, None]
    doc_col = documents[:, None]
    doc_row = documents[None, :]

    normed_low = layer_norm(tokens.astype(f32), norms[0], norms[1]).astype(low)
    normed_low, dense = in_order(normed_low, dense)
    packed = jnp.dot(normed_low, dense[:, : 3 * width], preferred_element_type=f32).astype(low)
    mixed, lse = attend(packed, doc_col, doc_row)
    after, grad_rows, gate, *outgoing = after_attend(
        [mixed],
        dense,
        tokens,
        out_grad,
        norms,
        centre_table,
        routes,
        chunked_row,
        [slots // chunks] * chunks,
    )

    def exchange(rows):
        rows = rows.reshape(experts, -1, width)
        return lax.all_to_all(rows, "expert", split_axis=0, concat_axis=0, tiled=True)

    grad_outgoing = []
    for c in range(chunks):
        own = jnp.arange(slots // chunks, dtype=jnp.int32)[:, None] + c * (slots // chunks)
        place = (own == chunked_row).astype(low)
        grad_outgoing.append(jnp.dot(place, grad_rows, preferred_element_type=f32).astype(low))
    arrived, slope, hidden = [], [], None
    for c in range(chunks):
        if c:
            arrived[c - 1], outgoing[c], *grad_outgoing = in_order(
                arrived[c - 1], outgoing[c], *grad_outgoing
            )
        arrived.append(exchange(outgoing[c]))
    for c in range(chunks):
        if c == chunks - 1:
            arrived[c], grad_outgoing[0] = in_order(arrived[c], grad_outgoing[0])
        hidden, slope_c = expert_forward(arrived[c], weight_in, c, chunks, hidden)
        slope.append(slope_c)
        if c == 0 and chunks > 1:
            hidden, grad_outgoing[0] = in_order(hidden, grad_outgoing[0])
    grad_arrived = [exchange(grad_outgoing[0])]
    hidden = hidden.reshape(slots, -1)
    result = jnp.dot(hidden, weight_out, preferred_element_type=f32).astype(low)
    result = result.reshape(experts, slot_cap, width)
    for c in range(1, chunks):
        grad_arrived[c - 1], grad_outgoing[c], result = in_order(
            grad_arrived[c - 1], grad_outgoing[c], result
        )
        grad_arrived.append(exchange(grad_outgoing[c]))
    centre_row = lax.dynamic_slice_in_dim(centre_table, lax.axis_index("expert"), 1, 0)
    grad_preact = None
    grad_input, grad_centre = [], 0.0
    for c in range(chunks):
        last = c == chunks - 1
        grad_preact, rows_c, centre_c = expert_back(
            grad_arrived[c],
            slope[c],
            weight_in,
            weight_out,
            arrived[c],
            result,
            centre_row,
            c,
            chunks,
            grad_preact,
        )
        if not last:
            rows_c, grad_arrived[c + 1] = in_order(rows_c, grad_arrived[c + 1])
        elif grad_input:
            rows_c, grad_input[-1] = in_order(rows_c, grad_input[-1])
        grad_input.append(exchange(rows_c).reshape(slots // chunks, width))
        grad_centre = grad_centre + jnp.sum(centre_c, axis=0)
    if chunks > 1:
        hidden, arrived[0], grad_input[0] = in_order(hidden, arrived[0], grad_input[0])
    grad_in, grad_out_turned = weight_grads(
        arrived, grad_arrived, grad_preact, hidden.reshape(experts, slot_cap, -1)
    )
    result, grad_input[-1], grad_in, grad_out_turned = in_order(
        result, grad_input[-1], grad_in, grad_out_turned
    )
    in_grad = lax.psum_scatter(grad_in[None], "dp", scatter_dimension=1, tiled=True)
    out_turned = lax.psum_scatter(grad_out_turned[None], "dp", scatter_dimension=1, tiled=True)
    in_grad = in_grad.astype(f32)
    in_square = jnp.sum(in_grad * in_grad)
    returned = exchange(result).reshape(slots, width)

    grad_after, grad_low, grad_mixed, sums_two = before_attend_back(
        grad_input, chunked_col, after, out_grad, norms, dense
    )

    grad_proj = lax.dot_general(
        mixed, grad_low, (((0,), (0,)), ((), ())), preferred_element_type=f32
    ).astype(low)
    norm_two = jnp.sum(sums_two.reshape(2, 8, width), axis=1)
    norm_two = norm_two.reshape(2, devices, norm_own).transpose(1, 0, 2).reshape(devices, -1)
    mine = jnp.arange(experts)[:, None, None] == lax.axis_index("expert")
    centre_flat = jnp.where(mine, grad_centre.reshape(1, dp, centre_own), 0.0)
    extra = jnp.concatenate([norm_two, centre_flat.reshape(devices, centre_own)], axis=1)
    extra = jnp.pad(extra, ((0, 0), (0, rows_own * LANES - extra.shape[1]))).astype(low)
    extra = extra.reshape(devices * rows_own, LANES)
    each = width // LANES // groups
    wide = each * LANES

    def by_owner(values):
        return values.reshape(experts, dp, rows_own, values.shape[1])

    def back_group(g):
        part = attend_back(packed, grad_mixed, mixed, lse, doc_col, doc_row, g * each, each)
        grad = lax.dot_general(
            normed_low, part, (((0,), (0,)), ((), ())), preferred_element_type=f32
        )
        return part, grad.astype(low)

    parts, grads = [], []
    rest = by_owner(jnp.concatenate([grad_proj, extra], axis=1))
    for g in range(groups):
        if g == 1:
            rest = sum_over_cores([rest])
            rest, grad_mixed = in_order(rest, grad_mixed)
        if g == groups - 1:
            rest = sum_over_neighbours(rest)
            first = sum_over_cores([by_owner(v) for v in grads[: groups // 2]])
            rest, first, grad_mixed, returned = in_order(rest, first, grad_mixed, returned)
        part, grad = back_group(g)
        grad, grad_mixed = in_order(grad, grad_mixed)
        parts.append(part)
        grads.append(grad)
    second = sum_over_cores([by_owner(v) for v in grads[groups // 2 :]])
    second, first, grad_after = in_order(second, first, grad_after)
    second = sum_near(second)
    first = sum_over_neighbours(first)
    input_grad, sums_one = input_gradient(
        [(g * wide, wide) for g in range(groups)], parts, dense, tokens, norms, grad_after
    )
    first, second, sums_one, gate, out_turned = in_order(
        first, second, sums_one, gate, out_turned
    )
    norm_one = jnp.sum(sums_one.reshape(2, 8, width), axis=1)
    norm_one = norm_one.reshape(2, devices, norm_own).transpose(1, 0, 2).reshape(devices, -1)
    norm_one = lax.all_to_all(norm_one, everywhere, split_axis=0, concat_axis=0, tiled=True)
    norm_one = jnp.sum(norm_one, axis=0).reshape(2, norm_own)
    out_grad_w, out_square = turn(out_turned[0])
    out_grad_w = out_grad_w[None]
    activations = activations_of([returned], slot_col, gate, after)
    second = sum_far(second)
    first = sum_far(jnp.concatenate([rest, first], axis=-1)).astype(low)
    first, second, in_square, out_square, norm_one, activations = in_order(
        first, second, in_square, out_square, norm_one, activations
    )
    first = sum_across(first)

    proj_grad = first[:, :width]
    extra = first[:, width : width + LANES].reshape(-1)
    norm_grad = jnp.concatenate([norm_one, extra[: 2 * norm_own].reshape(2, norm_own)], axis=0)
    centre_grad = extra[2 * norm_own : 2 * norm_own + centre_own].reshape(centroids.shape)
    owned = [first[:, width + LANES :], second]
    qkv_grad = jnp.concatenate(
        [
            half[:, (3 * k + s) * wide : (3 * k + s + 1) * wide]
            for s in range(3)
            for half in owned
            for k in range(groups // 2)
        ],
        axis=1,
    )
    square_sum = (
        jnp.sum(qkv_grad * qkv_grad)
        + jnp.sum(proj_grad * proj_grad)
        + jnp.sum(norm_grad * norm_grad)
        + jnp.sum(centre_grad * centre_grad)
        + in_square
        + out_square
    )
    grad_norm = jnp.sqrt(sum_everywhere(square_sum))
    factor = clip_limit / jnp.maximum(grad_norm, clip_limit)
    norm_new = update(norm_params, norm_moment, norm_average, norm_grad, factor, norm_rate)
    qkv_new = update(qkv_weight, qkv_moment, qkv_average, qkv_grad, factor, learn_rate)
    proj_new = update(proj_weight, proj_moment, proj_average, proj_grad, factor, learn_rate)
    centre_new = update(
        centroids, centroid_moment, centroid_average, centre_grad, factor, learn_rate
    )
    in_new = update(expert_in, in_moment, in_average, in_grad, factor, learn_rate)
    out_new = update(expert_out, out_moment, out_average, out_grad_w, factor, learn_rate)
    return (
        activations,
        input_grad,
        grad_norm,
        norm_new[0],
        qkv_new[0],
        proj_new[0],
        centre_new[0],
        in_new[0],
        out_new[0],
        norm_new[1],
        qkv_new[1],
        proj_new[1],
        centre_new[1],
        in_new[1],
        out_new[1],
        norm_new[2],
        qkv_new[2],
        proj_new[2],
        centre_new[2],
        in_new[2],
        out_new[2],
    )


def solution(mesh):
    placed = (
        P(("expert", "dp"), None),
        P(("expert", "dp")),
        P(("expert", "dp"), None),
        P(("expert", "dp"), None),
        P(None, ("expert", "dp")),
        P(("expert", "dp"), None),
        P(("expert", "dp"), None),
        P("expert", "dp"),
        P("expert", "dp", None),
        P("expert", None, "dp"),
        P(None, ("expert", "dp")),
        P(("expert", "dp"), None),
        P(("expert", "dp"), None),
        P("expert", "dp"),
        P("expert", "dp", None),
        P("expert", None, "dp"),
        P(None, ("expert", "dp")),
        P(("expert", "dp"), None),
        P(("expert", "dp"), None),
        P("expert", "dp"),
        P("expert", "dp", None),
        P("expert", None, "dp"),
    )
    return jax.shard_map(
        shards,
        mesh=mesh,
        in_specs=placed,
        out_specs=(
            P(("expert", "dp"), None),
            P(("expert", "dp"), None),
            P(),
            P(None, ("expert", "dp")),
            P(("expert", "dp"), None),
            P(("expert", "dp"), None),
            P("expert", "dp"),
            P("expert", "dp", None),
            P("expert", None, "dp"),
            P(None, ("expert", "dp")),
            P(("expert", "dp"), None),
            P(("expert", "dp"), None),
            P("expert", "dp"),
            P("expert", "dp", None),
            P("expert", None, "dp"),
            P(None, ("expert", "dp")),
            P(("expert", "dp"), None),
            P(("expert", "dp"), None),
            P("expert", "dp"),
            P("expert", "dp", None),
            P("expert", None, "dp"),
        ),
        check_vma=False,
    )
```

```python
import functools
import math

import jax
import jax.numpy as jnp
from jax import lax
from jax.experimental import pallas as pl
from jax.experimental.pallas import tpu as pltpu
from jax.sharding import PartitionSpec as P

HEAD_DIM = 64
SEQ = 1024
LANES = 128
BLOCK = 256

eps = 1e-05
scale_qk = 0.125
momentum_rate = 0.9
learn_rate = 100.0
norm_rate = 500.0
average_rate = 0.9
clip_limit = 1.0
masked_score = -1000000000.0
everywhere = ("expert", "dp")
low = jnp.bfloat16
f32 = jnp.float32

erfc_point = 0.4
erfc_terms = (
    0.11596270714310389,
    0.08090178846816841,
    0.2341610172367065,
    -0.1854824771652721,
    0.35459055762612957,
    -0.10013360714943426,
)


def hint(microseconds):
    return pl.CostEstimate(
        flops=int(microseconds * 1.9e8), bytes_accessed=0, transcendentals=0
    )


def dot_rows(left, right):
    return lax.dot_general(left, right, (((1,), (0,)), ((), ())), preferred_element_type=f32)


def dot_cols(left, right):
    return lax.dot_general(left, right, (((1,), (1,)), ((), ())), preferred_element_type=f32)


def layer_norm(values, norm_gain, norm_bias):
    centre = values - jnp.mean(values, axis=-1, keepdims=True)
    spread = jnp.mean(centre * centre, axis=-1, keepdims=True)
    return centre * lax.rsqrt(spread + eps) * norm_gain + norm_bias


def fill_bias(bias, doc_of_rows, doc_of_cols, rows_are_keys):
    for block in range(0, SEQ, BLOCK):
        rows = lax.broadcasted_iota(jnp.int32, (BLOCK, SEQ), 0) + block
        cols = lax.broadcasted_iota(jnp.int32, (BLOCK, SEQ), 1)
        causal = (rows <= cols) if rows_are_keys else (rows >= cols)
        same = doc_of_rows[block : block + BLOCK, :] == doc_of_cols[...]
        bias[block : block + BLOCK, :] = jnp.where(same & causal, 3.0e38, masked_score)


def in_head(shape, head, axis):
    return lax.broadcasted_iota(jnp.int32, shape, axis) // HEAD_DIM == head


def keep_head(values, head):
    return jnp.where(in_head(values.shape, head, 1), values, jnp.zeros_like(values))


def attend_kernel(q_ref, k_ref, v_ref, doc_col, doc_row, mixed_ref, lse_ref, bias):
    @pl.when(pl.program_id(1) == 0)
    def _():
        fill_bias(bias, doc_col, doc_row, False)

    for block in range(0, SEQ, BLOCK):
        seen = block + BLOCK
        query = q_ref[block:seen, :] * jnp.asarray(scale_qk, low)
        outs, stats = [], []
        for head in range(2):
            scores = dot_cols(keep_head(query, head), k_ref[:seen, :])
            scores = jnp.minimum(scores, bias[block:seen, :seen])
            top = jnp.max(scores, axis=-1, keepdims=True)
            exponent = jnp.exp(scores - top)
            total = jnp.sum(exponent, axis=-1, keepdims=True)
            outs.append(dot_rows(exponent.astype(low), v_ref[:seen, :]) / total)
            stats.append(top + jnp.log(total))
        first = in_head((BLOCK, LANES), 0, 1)
        mixed_ref[block:seen, :] = jnp.where(first, outs[0], outs[1]).astype(low)
        lane = lax.broadcasted_iota(jnp.int32, (BLOCK, LANES), 1)
        both = jnp.where(lane == 0, stats[0], stats[1])
        lse_ref[:, block:seen] = both.T[:8, :]


def attend(packed, doc_col, doc_row):
    count, wide = packed.shape
    width = wide // 3
    pairs = width // LANES

    def part(which):
        return pl.BlockSpec((SEQ, LANES), lambda r, p, w=which: (r, w * pairs + p))

    return pl.pallas_call(
        attend_kernel,
        grid=(count // SEQ, pairs),
        in_specs=[
            part(0),
            part(1),
            part(2),
            pl.BlockSpec((SEQ, 1), lambda r, p: (r, 0)),
            pl.BlockSpec((1, SEQ), lambda r, p: (0, r)),
        ],
        out_specs=[
            pl.BlockSpec((SEQ, LANES), lambda r, p: (r, p)),
            pl.BlockSpec((8, SEQ), lambda r, p: (p, r)),
        ],
        out_shape=[
            jax.ShapeDtypeStruct((count, width), low),
            jax.ShapeDtypeStruct((8 * pairs, count), f32),
        ],
        scratch_shapes=[pltpu.VMEM((SEQ, SEQ), f32)],
        compiler_params=pltpu.CompilerParams(vmem_limit_bytes=48 * 2**20),
        cost_estimate=hint(29),
        name="attend",
    )(packed, packed, packed, doc_col, doc_row)


def attend_back_kernel(
    q_ref, k_ref, v_ref, grad_ref, mixed_ref, lse_ref, doc_col, doc_row, out_ref, bias, grad_q_t
):
    pair = pl.program_id(1)

    @pl.when(pair == 0)
    def _():
        fill_bias(bias, doc_col, doc_row, True)

    wide = out_ref.shape[1] // 3
    place = [pl.ds(pl.multiple_of(s * wide + pair * LANES, LANES), LANES) for s in range(3)]
    query = q_ref[...] * jnp.asarray(scale_qk, low)
    grad = grad_ref[...]
    product = grad.astype(f32) * mixed_ref[...].astype(f32)
    upper = product.astype(low)
    lower = (product - upper.astype(f32)).astype(low)
    chooser = (
        lax.broadcasted_iota(jnp.int32, (8, LANES), 0)
        == lax.broadcasted_iota(jnp.int32, (8, LANES), 1) // HEAD_DIM
    ).astype(low)
    inner = dot_cols(chooser, upper) + dot_cols(chooser, lower)
    key_t = k_ref[...].T
    for block in range(0, SEQ, BLOCK):
        after = block + BLOCK
        key = k_ref[block:after, :]
        value = v_ref[block:after, :]
        grad_k, grad_v = [], []
        for head in range(2):
            scores = dot_cols(keep_head(key, head), query[block:, :])
            scores = jnp.minimum(scores, bias[block:after, block:])
            weights = jnp.exp(scores - lse_ref[head : head + 1, block:])
            grad_w = dot_cols(keep_head(value, head), grad[block:, :])
            grad_s = (weights * (grad_w - inner[head : head + 1, block:])).astype(low)
            grad_v.append(dot_rows(weights.astype(low), grad[block:, :]))
            grad_k.append(dot_rows(grad_s, query[block:, :]))
            rows = slice(head * HEAD_DIM, (head + 1) * HEAD_DIM)
            moved = dot_rows(key_t[rows, block:after], grad_s)
            if block == 0:
                grad_q_t[rows, :] = moved
            else:
                grad_q_t[rows, block:] += moved
        first = in_head((BLOCK, LANES), 0, 1)
        out_ref[block:after, place[1]] = jnp.where(first, grad_k[0], grad_k[1]).astype(low)
        out_ref[block:after, place[2]] = jnp.where(first, grad_v[0], grad_v[1]).astype(low)
    out_ref[:, place[0]] = (grad_q_t[...] * scale_qk).T.astype(low)


def attend_back(packed, grad_mixed, mixed, lse, doc_col, doc_row, first, count, grad_first):
    tokens, wide = packed.shape
    pairs = wide // 3 // LANES

    def part(which):
        return pl.BlockSpec((SEQ, LANES), lambda r, p, w=which: (r, w * pairs + first + p))

    return pl.pallas_call(
        attend_back_kernel,
        grid=(tokens // SEQ, count),
        in_specs=[
            part(0),
            part(1),
            part(2),
            pl.BlockSpec((SEQ, LANES), lambda r, p: (r, grad_first + p)),
            pl.BlockSpec((SEQ, LANES), lambda r, p: (r, first + p)),
            pl.BlockSpec((8, SEQ), lambda r, p: (first + p, r)),
            pl.BlockSpec((SEQ, 1), lambda r, p: (r, 0)),
            pl.BlockSpec((1, SEQ), lambda r, p: (0, r)),
        ],
        out_specs=pl.BlockSpec((SEQ, 3 * count * LANES), lambda r, p: (r, 0)),
        out_shape=jax.ShapeDtypeStruct((tokens, 3 * count * LANES), low),
        scratch_shapes=[pltpu.VMEM((SEQ, SEQ), f32), pltpu.VMEM((LANES, SEQ), f32)],
        compiler_params=pltpu.CompilerParams(vmem_limit_bytes=48 * 2**20),
        cost_estimate=hint(4.8 * count),
        name="attend_back",
    )(packed, packed, packed, grad_mixed, mixed, lse, doc_col, doc_row)


def norm_parts(values):
    centre = values - jnp.mean(values, axis=-1, keepdims=True)
    spread = jnp.mean(centre * centre, axis=-1, keepdims=True)
    scale = lax.rsqrt(spread + eps)
    return centre * scale, scale


def norm_back(grad, normal, scale, gain):
    moved = grad * gain
    return scale * (
        moved
        - jnp.mean(moved, axis=-1, keepdims=True)
        - normal * jnp.mean(moved * normal, axis=-1, keepdims=True)
    )


def sum_slabs(values):
    return jnp.sum(values.reshape(-1, 8, values.shape[1]), axis=0)


def after_attend_kernel(
    mixed_refs, proj_ref, x_ref, grad_ref, norm_ref, centre_ref, route_ref, slot_ref, outs, sent
):
    after_ref, grad_rows_ref, gate_ref, out_refs = outs[0], outs[1], outs[2], outs[3:]
    step = pl.program_id(0)
    attended = 0.0
    depth = 0
    for mixed in mixed_refs:
        wide = mixed.shape[1]
        attended = attended + dot_rows(mixed[...], proj_ref[depth : depth + wide, :])
        depth += wide
    after = x_ref[...].astype(f32) + attended
    after_ref[...] = after
    normal, _ = norm_parts(after)
    sent_low = (normal * norm_ref[2:3, :] + norm_ref[3:4, :]).astype(low)
    sent[pl.ds(pl.multiple_of(step * BLOCK, BLOCK), BLOCK), :] = sent_low
    experts = centre_ref.shape[0]
    onehot = route_ref[...] == lax.broadcasted_iota(jnp.int32, (BLOCK, experts), 1)
    picked = dot_rows(onehot.astype(low), centre_ref[...])
    gate = jax.nn.sigmoid(jnp.sum(sent_low.astype(f32) * picked, axis=-1, keepdims=True))
    grad_rows_ref[...] = (gate * grad_ref[...].astype(f32)).astype(low)
    gate_ref[...] = jnp.broadcast_to(gate, gate_ref.shape)

    @pl.when(step == pl.num_programs(0) - 1)
    def _():
        base = 0
        for out_ref in out_refs:
            for row in range(0, out_ref.shape[0], BLOCK):
                slots = lax.broadcasted_iota(jnp.int32, (BLOCK, sent.shape[0]), 0) + base
                place = (slots == slot_ref[...]).astype(low)
                out_ref[row : row + BLOCK, :] = dot_rows(place, sent[...]).astype(low)
                base += BLOCK


def after_attend(mixed, proj, tokens, out_grad, norms, centres, routes, slot_row, chunk_rows):
    count, width = tokens.shape
    chunks = len(chunk_rows)
    tile = pl.BlockSpec((BLOCK, width), lambda i: (i, 0))

    def kernel(*refs):
        n = len(mixed)
        after_attend_kernel(refs[:n], *refs[n : n + 7], refs[n + 7 : -1], refs[-1])

    return pl.pallas_call(
        kernel,
        grid=(count // BLOCK,),
        in_specs=[pl.BlockSpec((BLOCK, m.shape[1]), lambda i: (i, 0)) for m in mixed]
        + [
            pl.BlockSpec((width, width), lambda i: (0, 0)),
            tile,
            tile,
            pl.BlockSpec(norms.shape, lambda i: (0, 0)),
            pl.BlockSpec(centres.shape, lambda i: (0, 0)),
            pl.BlockSpec((BLOCK, 1), lambda i: (i, 0)),
            pl.BlockSpec((1, count), lambda i: (0, 0)),
        ],
        out_specs=[tile, tile, pl.BlockSpec((BLOCK, LANES), lambda i: (i, 0))]
        + [pl.BlockSpec((rows, width), lambda i: (0, 0)) for rows in chunk_rows],
        out_shape=[
            jax.ShapeDtypeStruct((count, width), f32),
            jax.ShapeDtypeStruct((count, width), low),
            jax.ShapeDtypeStruct((count, LANES), f32),
        ]
        + [jax.ShapeDtypeStruct((rows, width), low) for rows in chunk_rows],
        scratch_shapes=[pltpu.VMEM((count, width), low)],
        compiler_params=pltpu.CompilerParams(vmem_limit_bytes=48 * 2**20),
        cost_estimate=hint(13),
        name="after_attend",
    )(*mixed, proj, tokens, out_grad, norms, centres, routes, slot_row)


def picked_rows(slot_ref, row_refs):
    base, total = 0, 0.0
    for rows in row_refs:
        slots = lax.broadcasted_iota(jnp.int32, (BLOCK, rows.shape[0]), 1) + base
        place = (slots == slot_ref[...]).astype(low)
        total = total + dot_rows(place, rows[...])
        base += rows.shape[0]
    return total


def before_attend_back_kernel(
    row_refs, slot_ref, after_ref, grad_ref, norm_ref, proj_ref, outs
):
    grad_after_ref, grad_low_ref, grad_mixed_ref, sums_ref = outs
    grad_normed = picked_rows(slot_ref, row_refs)
    normal, scale = norm_parts(after_ref[...])
    grad_after = grad_ref[...].astype(f32) + norm_back(
        grad_normed, normal, scale, norm_ref[2:3, :]
    )
    grad_after_ref[...] = grad_after
    grad_low = grad_after.astype(low)
    grad_low_ref[...] = grad_low
    grad_mixed_ref[...] = dot_cols(grad_low, proj_ref[...]).astype(low)
    sums = jnp.concatenate([sum_slabs(grad_normed * normal), sum_slabs(grad_normed)], axis=0)

    @pl.when(pl.program_id(0) == 0)
    def _():
        sums_ref[...] = sums

    @pl.when(pl.program_id(0) > 0)
    def _():
        sums_ref[...] += sums


def before_attend_back(rows, slot_col, after, out_grad, norms, proj):
    count, width = after.shape
    tile = pl.BlockSpec((BLOCK, width), lambda i: (i, 0))

    def kernel(*refs):
        n = len(rows)
        before_attend_back_kernel(refs[:n], *refs[n : n + 5], refs[n + 5 :])

    return pl.pallas_call(
        kernel,
        grid=(count // BLOCK,),
        in_specs=[pl.BlockSpec(r.shape, lambda i: (0, 0)) for r in rows]
        + [
            pl.BlockSpec((BLOCK, 1), lambda i: (i, 0)),
            tile,
            tile,
            pl.BlockSpec(norms.shape, lambda i: (0, 0)),
            pl.BlockSpec((width, width), lambda i: (0, 0)),
        ],
        out_specs=[tile, tile, tile, pl.BlockSpec((16, width), lambda i: (0, 0))],
        out_shape=[
            jax.ShapeDtypeStruct((count, width), f32),
            jax.ShapeDtypeStruct((count, width), low),
            jax.ShapeDtypeStruct((count, width), low),
            jax.ShapeDtypeStruct((16, width), f32),
        ],
        compiler_params=pltpu.CompilerParams(vmem_limit_bytes=48 * 2**20),
        cost_estimate=hint(12),
        name="before_attend_back",
    )(*rows, slot_col, after, out_grad, norms, proj)


def input_grad_kernel(plan, grad_refs, weight_refs, x_ref, norm_ref, grad_after_ref, outs):
    out_ref, sums_ref = outs
    grad_normed = 0.0
    for grad, (strip, offset, wide) in zip(grad_refs, plan):
        for s in range(3):
            weight = weight_refs[3 * strip + s]
            grad_normed = grad_normed + dot_cols(
                grad[:, s * wide : (s + 1) * wide], weight[:, offset : offset + wide]
            )
    normal, scale = norm_parts(x_ref[...].astype(f32))
    out_ref[...] = grad_after_ref[...] + norm_back(grad_normed, normal, scale, norm_ref[0:1, :])
    sums = jnp.concatenate([sum_slabs(grad_normed * normal), sum_slabs(grad_normed)], axis=0)

    @pl.when(pl.program_id(0) == 0)
    def _():
        sums_ref[...] = sums

    @pl.when(pl.program_id(0) > 0)
    def _():
        sums_ref[...] += sums


def input_gradient(plan, grads, weights, tokens, norms, grad_after):
    count, width = tokens.shape
    tile = pl.BlockSpec((BLOCK, width), lambda i: (i, 0))

    def kernel(*refs):
        n, m = len(grads), len(grads) + len(weights)
        input_grad_kernel(plan, refs[:n], refs[n:m], *refs[m : m + 3], refs[m + 3 :])

    return pl.pallas_call(
        kernel,
        grid=(count // BLOCK,),
        in_specs=[pl.BlockSpec((BLOCK, g.shape[1]), lambda i: (i, 0)) for g in grads]
        + [
            pl.BlockSpec((width, columns), lambda i, block=block: (0, block))
            for _, block, columns in weights
        ]
        + [
            tile,
            pl.BlockSpec(norms.shape, lambda i: (0, 0)),
            tile,
        ],
        out_specs=[tile, pl.BlockSpec((16, width), lambda i: (0, 0))],
        out_shape=[
            jax.ShapeDtypeStruct((count, width), f32),
            jax.ShapeDtypeStruct((16, width), f32),
        ],
        compiler_params=pltpu.CompilerParams(vmem_limit_bytes=48 * 2**20),
        cost_estimate=hint(14),
        name="input_gradient",
    )(*grads, *[array for array, _, _ in weights], tokens, norms, grad_after)


def activations_of(rows, slot_col, gate, after):
    count, width = after.shape
    tile = pl.BlockSpec((BLOCK, width), lambda i: (i, 0))

    def kernel(*refs):
        n = len(rows)
        slot_ref, gate_ref, after_ref, out_ref = refs[n:]
        found = picked_rows(slot_ref, refs[:n])
        out_ref[...] = (after_ref[...] + gate_ref[:, :1] * found).astype(low)

    return pl.pallas_call(
        kernel,
        grid=(count // BLOCK,),
        in_specs=[pl.BlockSpec(r.shape, lambda i: (0, 0)) for r in rows]
        + [
            pl.BlockSpec((BLOCK, 1), lambda i: (i, 0)),
            pl.BlockSpec((BLOCK, LANES), lambda i: (i, 0)),
            tile,
        ],
        out_specs=tile,
        out_shape=jax.ShapeDtypeStruct((count, width), low),
        compiler_params=pltpu.CompilerParams(vmem_limit_bytes=48 * 2**20),
        cost_estimate=hint(7.5),
        name="activations_of",
    )(*rows, slot_col, gate, after)


def gelu_and_slope(x):
    point = 1.0 / (1.0 + (erfc_point * math.sqrt(0.5)) * jnp.abs(x))
    bell = jnp.exp(-0.5 * x * x)
    tail = erfc_terms[-1]
    for term in erfc_terms[-2::-1]:
        tail = tail * point + term
    tail = tail * point * bell
    below = jnp.where(x >= 0.0, 1.0 - tail, tail)
    return x * below, below + x * bell * (1.0 / math.sqrt(2.0 * math.pi))


def row_groups(experts, each):
    group = max(g for g in range(1, experts + 1) if experts % g == 0 and g * each <= BLOCK)
    return group, group * each


def expert_kernel(x_ref, in_ref, *rest):
    hidden_ref, slope_ref = rest[-2:]
    experts, each, width = x_ref.shape
    group, size = row_groups(experts, each)
    for e in range(0, experts, group):
        preact = dot_rows(x_ref[e : e + group].reshape(size, width), in_ref[...])
        value, slope = gelu_and_slope(preact)
        hidden_ref[e : e + group] = value.astype(low).reshape(group, each, -1)
        slope_ref[e : e + group] = slope.astype(low).reshape(group, each, -1)


def expert_forward(arrived, weight_in, chunk, chunks, buffer=None, tile=512):
    experts, each, width = arrived.shape
    inner = weight_in.shape[1]
    return pl.pallas_call(
        expert_kernel,
        grid=(inner // tile,),
        in_specs=[
            pl.BlockSpec((experts, each, width), lambda j: (0, 0, 0)),
            pl.BlockSpec((width, tile), lambda j: (0, j)),
        ]
        + ([] if buffer is None else [pl.BlockSpec(memory_space=pl.ANY)]),
        out_specs=[
            pl.BlockSpec((experts, each, tile), lambda j: (0, chunk, j)),
            pl.BlockSpec((experts, each, tile), lambda j: (0, 0, j)),
        ],
        out_shape=[
            jax.ShapeDtypeStruct((experts, chunks * each, inner), low),
            jax.ShapeDtypeStruct((experts, each, inner), low),
        ],
        input_output_aliases={} if buffer is None else {2: 0},
        compiler_params=pltpu.CompilerParams(vmem_limit_bytes=56 * 2**20),
        cost_estimate=hint(21),
        name="expert_forward",
    )(arrived, weight_in, *([] if buffer is None else [buffer]))


def expert_back_kernel(
    grad_ref, slope_ref, in_ref, out_ref, x_ref, result_ref, centre_ref, *rest
):
    grad_preact_ref, grad_rows_ref, grad_centre_ref, strips, grad_logit_ref = rest[-5:]
    step = pl.program_id(0)
    count, size, tile = strips.shape
    each = grad_ref.shape[1]

    @pl.when(step < count)
    def _():
        grad_hidden = dot_cols(grad_ref[...].reshape(size, -1), out_ref[...])
        grad_preact = (grad_hidden * slope_ref[...].reshape(size, tile).astype(f32)).astype(low)
        strips[step] = grad_preact
        grad_preact_ref[...] = grad_preact.reshape(-1, each, tile)

    @pl.when(step == count)
    def _():
        centre = centre_ref[...].astype(f32)
        grad_centre = jnp.zeros(grad_centre_ref.shape, f32)
        group, rows = row_groups(grad_ref.shape[0], each)
        for e in range(0, grad_ref.shape[0], group):
            x = x_ref[e : e + group].reshape(rows, -1).astype(f32)
            gate = jax.nn.sigmoid(jnp.sum(x * centre, axis=-1, keepdims=True))
            grad = grad_ref[e : e + group].reshape(rows, -1).astype(f32)
            moved = grad * result_ref[e : e + group].reshape(rows, -1).astype(f32)
            grad_logit = jnp.sum(moved, axis=-1, keepdims=True) * (1.0 - gate)
            grad_logit_ref[e * each : e * each + rows, :] = jnp.broadcast_to(
                grad_logit, (rows, LANES)
            )
            grad_centre = grad_centre + sum_slabs(grad_logit * x)
        grad_centre_ref[...] = grad_centre

    @pl.when(step >= count)
    def _():
        columns = grad_rows_ref.shape[2]
        start = pl.multiple_of((step - count) * columns, columns)
        centre = centre_ref[:, pl.ds(start, columns)].astype(f32)
        total = grad_logit_ref[:, :1] * centre
        for k in range(count):
            total = total + dot_cols(strips[k], in_ref[:, k * tile : (k + 1) * tile])
        grad_rows_ref[...] = total.astype(low).reshape(-1, each, columns)


def expert_back(
    grad_arrived,
    slope,
    weight_in,
    weight_out,
    arrived,
    result,
    centre,
    chunk,
    chunks,
    buffer=None,
    tile=1024,
    columns=256,
):
    experts, each, width = grad_arrived.shape
    inner = weight_in.shape[1]
    count = inner // tile
    alone = pl.BlockSpec((experts, each, width), lambda j: (0, 0, 0))

    def strip(j):
        return jnp.minimum(j, count - 1)

    def part(j):
        return jnp.maximum(j - count, 0)

    return pl.pallas_call(
        expert_back_kernel,
        grid=(count + width // columns,),
        in_specs=[
            alone,
            pl.BlockSpec((experts, each, tile), lambda j: (0, 0, strip(j))),
            pl.BlockSpec((columns, inner), lambda j: (part(j), 0)),
            pl.BlockSpec((tile, width), lambda j: (strip(j), 0)),
            alone,
            pl.BlockSpec((experts, each, width), lambda j: (0, chunk, 0)),
            pl.BlockSpec((1, width), lambda j: (0, 0)),
        ]
        + ([] if buffer is None else [pl.BlockSpec(memory_space=pl.ANY)]),
        out_specs=[
            pl.BlockSpec((experts, each, tile), lambda j: (0, chunk, strip(j))),
            pl.BlockSpec((experts, each, columns), lambda j: (0, 0, part(j))),
            pl.BlockSpec((8, width), lambda j: (0, 0)),
        ],
        out_shape=[
            jax.ShapeDtypeStruct((experts, chunks * each, inner), low),
            jax.ShapeDtypeStruct((experts, each, width), low),
            jax.ShapeDtypeStruct((8, width), f32),
        ],
        scratch_shapes=[
            pltpu.VMEM((count, experts * each, tile), low),
            pltpu.VMEM((experts * each, LANES), f32),
        ],
        input_output_aliases={} if buffer is None else {7: 0},
        compiler_params=pltpu.CompilerParams(vmem_limit_bytes=58 * 2**20),
        cost_estimate=hint(23),
        name="expert_back",
    )(
        grad_arrived,
        slope,
        weight_in,
        weight_out,
        arrived,
        result,
        centre,
        *([] if buffer is None else [buffer]),
    )


def weight_grads_kernel(chunks, refs):
    x_refs, grad_refs = refs[:chunks], refs[chunks : 2 * chunks]
    grad_preact_ref, hidden_ref, in_out_ref, out_out_ref, turned = refs[2 * chunks :]
    step = pl.program_id(0)
    half = pl.num_programs(0) // 2

    def turn_rows(chunk_refs):
        for c, ref in enumerate(chunk_refs):
            experts, each, width = ref.shape
            group, size = row_groups(experts, each)
            for e in range(0, experts, group):
                turned[c, :, e * each : e * each + size] = (
                    ref[e : e + group].reshape(size, width).T
                )

    pl.when(step == 0)(lambda: turn_rows(x_refs))
    pl.when(step == half)(lambda: turn_rows(grad_refs))

    def multiply(ref, out_ref):
        experts, slots, tile = ref.shape
        each = slots // chunks
        right = [
            ref[:, c * each : (c + 1) * each, :].reshape(experts * each, tile)
            for c in range(chunks)
        ]
        for row in range(0, turned.shape[1], BLOCK):
            rows = slice(row, row + BLOCK)
            total = dot_rows(turned[0, rows, :], right[0])
            for c in range(1, chunks):
                total = total + dot_rows(turned[c, rows, :], right[c])
            out_ref[rows, :] = total.astype(low)

    pl.when(step < half)(lambda: multiply(grad_preact_ref, in_out_ref))
    pl.when(step >= half)(lambda: multiply(hidden_ref, out_out_ref))


def weight_grads(arrived, grad_arrived, grad_preact, hidden, tile=1024):
    chunks = len(arrived)
    experts, each, width = arrived[0].shape
    slots, inner = hidden.shape[1:]
    half = inner // tile
    whole = pl.BlockSpec((experts, each, width), lambda j: (0, 0, 0))

    def first(j):
        return jnp.minimum(j, half - 1)

    def second(j):
        return jnp.maximum(j - half, 0)

    return pl.pallas_call(
        lambda *refs: weight_grads_kernel(chunks, refs),
        grid=(2 * half,),
        in_specs=[whole] * (2 * chunks)
        + [
            pl.BlockSpec((experts, slots, tile), lambda j: (0, 0, first(j))),
            pl.BlockSpec((experts, slots, tile), lambda j: (0, 0, second(j))),
        ],
        out_specs=[
            pl.BlockSpec((width, tile), lambda j: (0, first(j))),
            pl.BlockSpec((width, tile), lambda j: (0, second(j))),
        ],
        out_shape=[jax.ShapeDtypeStruct((width, inner), low)] * 2,
        scratch_shapes=[pltpu.VMEM((chunks, width, experts * each), low)],
        compiler_params=pltpu.CompilerParams(vmem_limit_bytes=58 * 2**20),
        cost_estimate=hint(38),
        name="weight_grads",
    )(*arrived, *grad_arrived, grad_preact, hidden)


def turn_kernel(in_ref, out_ref, square_ref):
    values = in_ref[...].astype(f32)
    out_ref[...] = in_ref[...].T.astype(f32)
    square = sum_slabs(values * values)

    @pl.when(pl.program_id(0) == 0)
    def _():
        square_ref[...] = square

    @pl.when(pl.program_id(0) > 0)
    def _():
        square_ref[...] += square


def turn(values, tile=512):
    rows, columns = values.shape
    turned, square = pl.pallas_call(
        turn_kernel,
        grid=(columns // tile,),
        in_specs=[pl.BlockSpec((rows, tile), lambda j: (0, j))],
        out_specs=[
            pl.BlockSpec((tile, rows), lambda j: (j, 0)),
            pl.BlockSpec((8, tile), lambda j: (0, 0)),
        ],
        out_shape=[
            jax.ShapeDtypeStruct((columns, rows), f32),
            jax.ShapeDtypeStruct((8, tile), f32),
        ],
        cost_estimate=hint(3),
        name="turn",
    )(values)
    return turned, jnp.sum(square)


def swap(values, axis, distance):
    size = lax.axis_size(axis)
    return lax.ppermute(values, axis, [(i, i ^ distance) for i in range(size)])


def assemble_kernel(me_ref, *refs):
    pieces, out_ref = refs[:-1], refs[-1]
    experts, rows = pieces[0].shape[0], pieces[0].shape[1]
    for t, piece in enumerate(pieces):
        for e in range(experts):
            owner = e * len(pieces) + (me_ref[0] ^ t)
            out_ref[pl.ds(pl.multiple_of(owner * rows, rows), rows), :] = piece[e]


def assemble(pieces):
    experts, rows, columns = pieces[0].shape
    dp = len(pieces)
    return pl.pallas_call(
        assemble_kernel,
        in_specs=[pl.BlockSpec(memory_space=pltpu.SMEM)]
        + [pl.BlockSpec(memory_space=pltpu.VMEM)] * dp,
        out_specs=pl.BlockSpec(memory_space=pltpu.VMEM),
        out_shape=jax.ShapeDtypeStruct((experts * dp * rows, columns), pieces[0].dtype),
        compiler_params=pltpu.CompilerParams(vmem_limit_bytes=32 * 2**20),
        cost_estimate=hint(4),
        name="assemble",
    )(lax.axis_index("dp").astype(jnp.int32).reshape(1), *pieces)


def sum_halves(parts, axis, bit, at):
    own = (lax.axis_index(axis) // bit) % 2

    def side(which):
        picked = []
        for part in parts:
            shape = part.shape
            halves = part.reshape(shape[:at] + (shape[at] // 2, 2) + shape[at + 1 :])
            picked.append(lax.dynamic_index_in_dim(halves, which, at + 1, keepdims=False))
        return jnp.concatenate(picked, axis=-1)

    return (side(own).astype(f32) + swap(side(1 - own), axis, bit).astype(f32)).astype(low)


def sum_over_cores(parts):
    return sum_halves(parts, "dp", 1, 1)


def sum_over_neighbours(held):
    return sum_halves([held], "expert", 1, 0)


def sum_over_pairs(held, partners, keep):
    experts, dp = lax.axis_size("expert"), lax.axis_size("dp")
    total = lax.dynamic_index_in_dim(held, keep, 0, keepdims=False).astype(f32)
    for offset, (far, near) in enumerate(partners, 1):
        block = lax.dynamic_index_in_dim(held, jnp.bitwise_xor(keep, offset), 0, keepdims=False)
        perm = [
            (e * dp + d, (e ^ far) * dp + (d ^ near)) for e in range(experts) for d in range(dp)
        ]
        total = total + lax.ppermute(block, everywhere, perm).astype(f32)
    return total


def sum_near(held):
    near = held.shape[1]
    held = held.reshape((held.shape[0] // 2, 2 * near) + held.shape[2:]).swapaxes(0, 1)
    partners = [(i // near, i % near * 2) for i in range(1, 2 * near)]
    keep = lax.axis_index("expert") % 2 * near + lax.axis_index("dp") // 2
    return sum_over_pairs(held, partners, keep).astype(low)


def sum_far(held):
    partners = [(2 * i, 0) for i in range(1, held.shape[0])]
    return sum_over_pairs(held, partners, lax.axis_index("expert") // 2)


def sum_across(held):
    partners = [(0, 2 * i) for i in range(1, held.shape[0])]
    return sum_over_pairs(held, partners, lax.axis_index("dp") // 2)


def in_order(*values):
    return lax.optimization_barrier(values)


def sum_everywhere(value):
    held = value.reshape(1, 1)
    for axis in ("dp", "expert"):
        distance = 1
        while distance < lax.axis_size(axis):
            held = held + swap(held, axis, distance)
            distance *= 2
    return held[0, 0]


def update(weight, moment, average, gradient, factor, rate):
    clipped = gradient * factor
    moment_new = momentum_rate * moment + clipped
    weight_new = weight - rate * (clipped + momentum_rate * moment_new)
    average_new = average_rate * average + (1.0 - average_rate) * weight_new
    return (weight_new, moment_new, average_new)


def shards(
    tokens,
    documents,
    routes,
    out_grad,
    norm_params,
    qkv_weight,
    proj_weight,
    centroids,
    expert_in,
    expert_out,
    norm_moment,
    qkv_moment,
    proj_moment,
    centroid_moment,
    in_moment,
    out_moment,
    norm_average,
    qkv_average,
    proj_average,
    centroid_average,
    in_average,
    out_average,
):
    local_tokens, width = tokens.shape
    experts = lax.axis_size("expert")
    dp = lax.axis_size("dp")
    devices = experts * dp
    slot_cap = max(2, 3 * local_tokens // (2 * experts))
    slots = experts * slot_cap
    chunks = 2 if slot_cap % 32 == 0 else 1
    half_cap = slot_cap // chunks
    rows_own = qkv_weight.shape[0]
    norm_own = norm_params.shape[1]
    centre_own = centroids.shape[1]
    groups = 4

    strips = 2
    strip = width // strips
    small = jnp.concatenate([norm_params.reshape(-1), centroids.reshape(-1)]).astype(low)
    small = jnp.pad(small, (0, rows_own * LANES - small.shape[0])).reshape(rows_own, LANES)
    qkv_low = qkv_weight.astype(low)
    qkv_own = [
        [qkv_low[:, s * width + h * strip : s * width + (h + 1) * strip] for s in range(3)]
        for h in range(strips)
    ]
    front = jnp.concatenate([*qkv_own[0], small], axis=1)
    later = jnp.concatenate([proj_weight.astype(low), *qkv_own[1]], axis=1)
    later = lax.all_gather(later, everywhere, axis=0, tiled=True)
    in_low, out_low = expert_in.astype(low), expert_out.astype(low)

    route_ids = routes[:, 0]
    onehot = route_ids[:, None] == jnp.arange(experts, dtype=jnp.int32)[None, :]
    running = jnp.cumsum(onehot.astype(jnp.int32), axis=0)
    within = jnp.sum(running * onehot.astype(jnp.int32), axis=1) - 1
    slot_index = route_ids * slot_cap + within
    chunked = (within // half_cap * experts + route_ids) * half_cap + within % half_cap
    slot_row, slot_col = slot_index[None, :], slot_index[:, None]
    chunked_row, chunked_col = chunked[None, :], chunked[:, None]
    doc_col = documents[:, None]
    doc_row = documents[None, :]

    if rows_own % 16:
        front = lax.all_gather(front, everywhere, axis=0, tiled=True)
    else:
        spread = jnp.broadcast_to(front[None], (experts,) + front.shape)
        spread = lax.all_to_all(spread, "expert", split_axis=0, concat_axis=0, tiled=True)
        spread, in_low, out_low, slot_row, slot_col, chunked_row, chunked_col = in_order(
            spread, in_low, out_low, slot_row, slot_col, chunked_row, chunked_col
        )
        pieces = {0: spread}
        distance = dp // 2
        while distance:
            for t in list(pieces):
                pieces[t | distance] = swap(pieces[t], "dp", distance)
            distance //= 2
        front = assemble([pieces[t] for t in range(dp)])
    weight_in = lax.all_gather(in_low, "dp", axis=1, tiled=True)[0]
    weight_out = lax.all_gather(out_low, "dp", axis=2, tiled=True)[0]
    small_full = front[:, 3 * strip :].reshape(devices, rows_own * LANES)
    norms = (
        small_full[:, : 4 * norm_own].reshape(devices, 4, norm_own).transpose(1, 0, 2)
    ).reshape(4, width).astype(f32)
    centre_table = small_full[:, 4 * norm_own : 4 * norm_own + centre_own].reshape(experts, width)

    normed_low = layer_norm(tokens.astype(f32), norms[0], norms[1]).astype(low)
    normed_low, front = in_order(normed_low, front)
    packed, mixed, lse = [], [], []
    for weight in (front[:, : 3 * strip], later[:, width:]):
        packed_h = jnp.dot(normed_low, weight, preferred_element_type=f32).astype(low)
        mixed_h, lse_h = attend(packed_h, doc_col, doc_row)
        packed.append(packed_h)
        mixed.append(mixed_h)
        lse.append(lse_h)
    after, grad_rows, gate, *outgoing = after_attend(
        mixed,
        later,
        tokens,
        out_grad,
        norms,
        centre_table,
        routes,
        chunked_row,
        [slots // chunks] * chunks,
    )

    def exchange(rows):
        rows = rows.reshape(experts, -1, width)
        return lax.all_to_all(rows, "expert", split_axis=0, concat_axis=0, tiled=True)

    grad_outgoing = []
    for c in range(chunks):
        own = jnp.arange(slots // chunks, dtype=jnp.int32)[:, None] + c * (slots // chunks)
        place = (own == chunked_row).astype(low)
        grad_outgoing.append(jnp.dot(place, grad_rows, preferred_element_type=f32).astype(low))
    arrived, slope, hidden = [], [], None
    for c in range(chunks):
        if c:
            arrived[c - 1], outgoing[c], *grad_outgoing = in_order(
                arrived[c - 1], outgoing[c], *grad_outgoing
            )
        arrived.append(exchange(outgoing[c]))
    for c in range(chunks):
        if c == chunks - 1:
            arrived[c], grad_outgoing[0] = in_order(arrived[c], grad_outgoing[0])
        hidden, slope_c = expert_forward(arrived[c], weight_in, c, chunks, hidden)
        slope.append(slope_c)
        if c == 0 and chunks > 1:
            hidden, grad_outgoing[0] = in_order(hidden, grad_outgoing[0])
    grad_arrived = [exchange(grad_outgoing[0])]
    hidden = hidden.reshape(slots, -1)
    result = jnp.dot(hidden, weight_out, preferred_element_type=f32).astype(low)
    result = result.reshape(experts, slot_cap, width)
    for c in range(1, chunks):
        grad_arrived[c - 1], grad_outgoing[c], result = in_order(
            grad_arrived[c - 1], grad_outgoing[c], result
        )
        grad_arrived.append(exchange(grad_outgoing[c]))
    centre_row = lax.dynamic_slice_in_dim(centre_table, lax.axis_index("expert"), 1, 0)
    grad_preact = None
    grad_input, grad_centre = [], 0.0
    for c in range(chunks):
        last = c == chunks - 1
        grad_preact, rows_c, centre_c = expert_back(
            grad_arrived[c],
            slope[c],
            weight_in,
            weight_out,
            arrived[c],
            result,
            centre_row,
            c,
            chunks,
            grad_preact,
        )
        if not last:
            rows_c, grad_arrived[c + 1] = in_order(rows_c, grad_arrived[c + 1])
        elif grad_input:
            rows_c, grad_input[-1] = in_order(rows_c, grad_input[-1])
        grad_input.append(exchange(rows_c).reshape(slots // chunks, width))
        grad_centre = grad_centre + jnp.sum(centre_c, axis=0)
    if chunks > 1:
        hidden, arrived[0], grad_input[0] = in_order(hidden, arrived[0], grad_input[0])
    grad_in, grad_out_turned = weight_grads(
        arrived, grad_arrived, grad_preact, hidden.reshape(experts, slot_cap, -1)
    )
    result, grad_input[-1], grad_in, grad_out_turned = in_order(
        result, grad_input[-1], grad_in, grad_out_turned
    )
    in_grad = lax.psum_scatter(grad_in[None], "dp", scatter_dimension=1, tiled=True)
    out_turned = lax.psum_scatter(grad_out_turned[None], "dp", scatter_dimension=1, tiled=True)
    returned = exchange(result).reshape(slots, width)

    grad_after, grad_low, grad_mixed, sums_two = before_attend_back(
        grad_input, chunked_col, after, out_grad, norms, later
    )

    grad_proj = jnp.concatenate(
        [
            lax.dot_general(m, grad_low, (((0,), (0,)), ((), ())), preferred_element_type=f32)
            for m in mixed
        ],
        axis=0,
    ).astype(low)
    norm_two = jnp.sum(sums_two.reshape(2, 8, width), axis=1)
    norm_two = norm_two.reshape(2, devices, norm_own).transpose(1, 0, 2).reshape(devices, -1)
    mine = jnp.arange(experts)[:, None, None] == lax.axis_index("expert")
    centre_flat = jnp.where(mine, grad_centre.reshape(1, dp, centre_own), 0.0)
    extra = jnp.concatenate([norm_two, centre_flat.reshape(devices, centre_own)], axis=1)
    extra = jnp.pad(extra, ((0, 0), (0, rows_own * LANES - extra.shape[1]))).astype(low)
    extra = extra.reshape(devices * rows_own, LANES)
    each = width // LANES // groups
    wide = each * LANES

    def by_owner(values):
        return values.reshape(experts, dp, rows_own, values.shape[1])

    def back_group(g, *beside):
        h, k = g // (groups // strips), g % (groups // strips)
        part = attend_back(
            packed[h], grad_mixed, mixed[h], lse[h], doc_col, doc_row, k * each, each, g * each
        )
        part, *beside = in_order(part, *beside)
        grad = lax.dot_general(
            normed_low, part, (((0,), (0,)), ((), ())), preferred_element_type=f32
        )
        return part, grad.astype(low), *beside

    parts, grads = [], []
    rest = by_owner(jnp.concatenate([grad_proj, extra], axis=1))
    for g in range(groups):
        if g == 1:
            rest = sum_over_cores([rest])
            rest, grad_mixed = in_order(rest, grad_mixed)
        if g == groups - 1:
            rest = sum_over_neighbours(rest)
            first = sum_over_cores([by_owner(v) for v in grads[: groups // 2]])
            out_grad_w, out_square = turn(out_turned[0])
            rest, first, grad_mixed, returned, out_grad_w, out_square = in_order(
                rest, first, grad_mixed, returned, out_grad_w, out_square
            )
            out_grad_w = out_grad_w[None]
            first = sum_over_neighbours(first)
            part, grad, first = back_group(g, first)
        else:
            part, grad = back_group(g)
        grad, grad_mixed = in_order(grad, grad_mixed)
        parts.append(part)
        grads.append(grad)
    second = sum_over_cores([by_owner(v) for v in grads[groups // 2 :]])
    second, first, grad_after = in_order(second, first, grad_after)
    second = sum_near(second)
    first = sum_far(jnp.concatenate([rest, first], axis=-1)).astype(low)
    per_strip = groups // strips
    weights = [(front, s, strip) for s in range(3)]
    weights += [(later, width // strip + s, strip) for s in range(3)]
    input_grad, sums_one = input_gradient(
        [(g // per_strip, g % per_strip * wide, wide) for g in range(groups)],
        parts,
        weights,
        tokens,
        norms,
        grad_after,
    )
    first, second, sums_one, gate = in_order(first, second, sums_one, gate)
    norm_one = jnp.sum(sums_one.reshape(2, 8, width), axis=1)
    norm_one = norm_one.reshape(2, devices, norm_own).transpose(1, 0, 2).reshape(devices, -1)
    norm_one = lax.all_to_all(norm_one, everywhere, split_axis=0, concat_axis=0, tiled=True)
    norm_one, in_grad = in_order(norm_one, in_grad)
    in_grad = in_grad.astype(f32)
    in_square = jnp.sum(in_grad * in_grad)
    norm_one = jnp.sum(norm_one, axis=0).reshape(2, norm_own)
    activations = activations_of([returned], slot_col, gate, after)
    second = sum_far(second)
    first = sum_across(first)
    first, second, in_square, out_square, norm_one, activations = in_order(
        first, second, in_square, out_square, norm_one, activations
    )

    proj_grad = first[:, :width]
    extra = first[:, width : width + LANES].reshape(-1)
    norm_grad = jnp.concatenate([norm_one, extra[: 2 * norm_own].reshape(2, norm_own)], axis=0)
    centre_grad = extra[2 * norm_own : 2 * norm_own + centre_own].reshape(centroids.shape)
    owned = jnp.concatenate([first[:, width + LANES :], second], axis=1)
    qkv_grad = owned.reshape(rows_own, groups, 3, wide).swapaxes(1, 2).reshape(rows_own, 3 * width)
    square_sum = (
        jnp.sum(owned * owned)
        + jnp.sum(proj_grad * proj_grad)
        + jnp.sum(norm_grad * norm_grad)
        + jnp.sum(centre_grad * centre_grad)
        + in_square
        + out_square
    )
    grad_norm = jnp.sqrt(sum_everywhere(square_sum))
    factor = clip_limit / jnp.maximum(grad_norm, clip_limit)
    norm_new = update(norm_params, norm_moment, norm_average, norm_grad, factor, norm_rate)
    qkv_new = update(qkv_weight, qkv_moment, qkv_average, qkv_grad, factor, learn_rate)
    proj_new = update(proj_weight, proj_moment, proj_average, proj_grad, factor, learn_rate)
    centre_new = update(
        centroids, centroid_moment, centroid_average, centre_grad, factor, learn_rate
    )
    in_new = update(expert_in, in_moment, in_average, in_grad, factor, learn_rate)
    out_new = update(expert_out, out_moment, out_average, out_grad_w, factor, learn_rate)
    return (
        activations,
        input_grad,
        grad_norm,
        norm_new[0],
        qkv_new[0],
        proj_new[0],
        centre_new[0],
        in_new[0],
        out_new[0],
        norm_new[1],
        qkv_new[1],
        proj_new[1],
        centre_new[1],
        in_new[1],
        out_new[1],
        norm_new[2],
        qkv_new[2],
        proj_new[2],
        centre_new[2],
        in_new[2],
        out_new[2],
    )


def solution(mesh):
    placed = (
        P(("expert", "dp"), None),
        P(("expert", "dp")),
        P(("expert", "dp"), None),
        P(("expert", "dp"), None),
        P(None, ("expert", "dp")),
        P(("expert", "dp"), None),
        P(("expert", "dp"), None),
        P("expert", "dp"),
        P("expert", "dp", None),
        P("expert", None, "dp"),
        P(None, ("expert", "dp")),
        P(("expert", "dp"), None),
        P(("expert", "dp"), None),
        P("expert", "dp"),
        P("expert", "dp", None),
        P("expert", None, "dp"),
        P(None, ("expert", "dp")),
        P(("expert", "dp"), None),
        P(("expert", "dp"), None),
        P("expert", "dp"),
        P("expert", "dp", None),
        P("expert", None, "dp"),
    )
    return jax.shard_map(
        shards,
        mesh=mesh,
        in_specs=placed,
        out_specs=(
            P(("expert", "dp"), None),
            P(("expert", "dp"), None),
            P(),
            P(None, ("expert", "dp")),
            P(("expert", "dp"), None),
            P(("expert", "dp"), None),
            P("expert", "dp"),
            P("expert", "dp", None),
            P("expert", None, "dp"),
            P(None, ("expert", "dp")),
            P(("expert", "dp"), None),
            P(("expert", "dp"), None),
            P("expert", "dp"),
            P("expert", "dp", None),
            P("expert", None, "dp"),
            P(None, ("expert", "dp")),
            P(("expert", "dp"), None),
            P(("expert", "dp"), None),
            P("expert", "dp"),
            P("expert", "dp", None),
            P("expert", None, "dp"),
        ),
        check_vma=False,
    )
```

```python
import functools
import math

import jax
import jax.numpy as jnp
from jax import lax
from jax.experimental import pallas as pl
from jax.experimental.pallas import tpu as pltpu
from jax.sharding import PartitionSpec as P

HEAD_DIM = 64
SEQ = 1024
LANES = 128
BLOCK = 256

eps = 1e-05
scale_qk = 0.125
momentum_rate = 0.9
learn_rate = 100.0
norm_rate = 500.0
average_rate = 0.9
clip_limit = 1.0
masked_score = -1000000000.0
everywhere = ("expert", "dp")
low = jnp.bfloat16
f32 = jnp.float32

erfc_point = 0.4
erfc_terms = (
    0.11596270714310389,
    0.08090178846816841,
    0.2341610172367065,
    -0.1854824771652721,
    0.35459055762612957,
    -0.10013360714943426,
)


def hint(microseconds):
    return pl.CostEstimate(
        flops=int(microseconds * 1.9e8), bytes_accessed=0, transcendentals=0
    )


def dot_rows(left, right):
    return lax.dot_general(left, right, (((1,), (0,)), ((), ())), preferred_element_type=f32)


def dot_cols(left, right):
    return lax.dot_general(left, right, (((1,), (1,)), ((), ())), preferred_element_type=f32)


def layer_norm(values, norm_gain, norm_bias):
    centre = values - jnp.mean(values, axis=-1, keepdims=True)
    spread = jnp.mean(centre * centre, axis=-1, keepdims=True)
    return centre * lax.rsqrt(spread + eps) * norm_gain + norm_bias


def fill_bias(bias, doc_of_rows, doc_of_cols, rows_are_keys):
    for block in range(0, SEQ, BLOCK):
        rows = lax.broadcasted_iota(jnp.int32, (BLOCK, SEQ), 0) + block
        cols = lax.broadcasted_iota(jnp.int32, (BLOCK, SEQ), 1)
        causal = (rows <= cols) if rows_are_keys else (rows >= cols)
        same = doc_of_rows[block : block + BLOCK, :] == doc_of_cols[...]
        bias[block : block + BLOCK, :] = jnp.where(same & causal, 3.0e38, masked_score)


def in_head(shape, head, axis):
    return lax.broadcasted_iota(jnp.int32, shape, axis) // HEAD_DIM == head


def keep_head(values, head):
    return jnp.where(in_head(values.shape, head, 1), values, jnp.zeros_like(values))


def attend_kernel(q_ref, k_ref, v_ref, doc_col, doc_row, mixed_ref, lse_ref, bias):
    @pl.when(pl.program_id(1) == 0)
    def _():
        fill_bias(bias, doc_col, doc_row, False)

    def scores_of(block):
        seen = block + BLOCK
        query = q_ref[block:seen, :] * jnp.asarray(scale_qk, low)
        return [dot_cols(keep_head(query, head), k_ref[:seen, :]) for head in range(2)]

    following = scores_of(0)
    for block in range(0, SEQ, BLOCK):
        seen = block + BLOCK
        current = following
        if seen < SEQ:
            following = scores_of(seen)
        weights, outs, stats = [], [], []
        for head in range(2):
            scores = jnp.minimum(current[head], bias[block:seen, :seen])
            top = jnp.max(scores, axis=-1, keepdims=True)
            exponent = jnp.exp(scores - top)
            total = jnp.sum(exponent, axis=-1, keepdims=True)
            weights.append((exponent.astype(low), total))
            stats.append(top + jnp.log(total))
        for exponent, total in weights:
            outs.append(dot_rows(exponent, v_ref[:seen, :]) / total)
        first = in_head((BLOCK, LANES), 0, 1)
        mixed_ref[block:seen, :] = jnp.where(first, outs[0], outs[1]).astype(low)
        lane = lax.broadcasted_iota(jnp.int32, (BLOCK, LANES), 1)
        both = jnp.where(lane == 0, stats[0], stats[1])
        lse_ref[:, block:seen] = both.T[:8, :]


def attend(packed, doc_col, doc_row):
    count, wide = packed.shape
    width = wide // 3
    pairs = width // LANES

    def part(which):
        return pl.BlockSpec((SEQ, LANES), lambda r, p, w=which: (r, w * pairs + p))

    return pl.pallas_call(
        attend_kernel,
        grid=(count // SEQ, pairs),
        in_specs=[
            part(0),
            part(1),
            part(2),
            pl.BlockSpec((SEQ, 1), lambda r, p: (r, 0)),
            pl.BlockSpec((1, SEQ), lambda r, p: (0, r)),
        ],
        out_specs=[
            pl.BlockSpec((SEQ, LANES), lambda r, p: (r, p)),
            pl.BlockSpec((8, SEQ), lambda r, p: (p, r)),
        ],
        out_shape=[
            jax.ShapeDtypeStruct((count, width), low),
            jax.ShapeDtypeStruct((8 * pairs, count), f32),
        ],
        scratch_shapes=[pltpu.VMEM((SEQ, SEQ), f32)],
        compiler_params=pltpu.CompilerParams(vmem_limit_bytes=48 * 2**20),
        cost_estimate=hint(29),
        name="attend",
    )(packed, packed, packed, doc_col, doc_row)


def attend_back_kernel(
    q_ref, k_ref, v_ref, grad_ref, mixed_ref, lse_ref, doc_col, doc_row, out_ref, bias, grad_q_t
):
    pair = pl.program_id(1)

    @pl.when(pair == 0)
    def _():
        fill_bias(bias, doc_col, doc_row, True)

    wide = out_ref.shape[1] // 3
    place = [pl.ds(pl.multiple_of(s * wide + pair * LANES, LANES), LANES) for s in range(3)]
    query = q_ref[...] * jnp.asarray(scale_qk, low)
    grad = grad_ref[...]
    product = grad.astype(f32) * mixed_ref[...].astype(f32)
    upper = product.astype(low)
    lower = (product - upper.astype(f32)).astype(low)
    chooser = (
        lax.broadcasted_iota(jnp.int32, (8, LANES), 0)
        == lax.broadcasted_iota(jnp.int32, (8, LANES), 1) // HEAD_DIM
    ).astype(low)
    inner = dot_cols(chooser, upper) + dot_cols(chooser, lower)
    key_t = k_ref[...].T
    for block in range(0, SEQ, BLOCK):
        after = block + BLOCK
        key = k_ref[block:after, :]
        value = v_ref[block:after, :]
        grad_k, grad_v = [], []
        for head in range(2):
            scores = dot_cols(keep_head(key, head), query[block:, :])
            scores = jnp.minimum(scores, bias[block:after, block:])
            weights = jnp.exp(scores - lse_ref[head : head + 1, block:])
            grad_w = dot_cols(keep_head(value, head), grad[block:, :])
            grad_s = (weights * (grad_w - inner[head : head + 1, block:])).astype(low)
            grad_v.append(dot_rows(weights.astype(low), grad[block:, :]))
            grad_k.append(dot_rows(grad_s, query[block:, :]))
            rows = slice(head * HEAD_DIM, (head + 1) * HEAD_DIM)
            moved = dot_rows(key_t[rows, block:after], grad_s)
            if block == 0:
                grad_q_t[rows, :] = moved
            else:
                grad_q_t[rows, block:] += moved
        first = in_head((BLOCK, LANES), 0, 1)
        out_ref[block:after, place[1]] = jnp.where(first, grad_k[0], grad_k[1]).astype(low)
        out_ref[block:after, place[2]] = jnp.where(first, grad_v[0], grad_v[1]).astype(low)
    out_ref[:, place[0]] = (grad_q_t[...] * scale_qk).T.astype(low)


def attend_back(packed, grad_mixed, mixed, lse, doc_col, doc_row, first, count, grad_first):
    tokens, wide = packed.shape
    pairs = wide // 3 // LANES

    def part(which):
        return pl.BlockSpec((SEQ, LANES), lambda r, p, w=which: (r, w * pairs + first + p))

    return pl.pallas_call(
        attend_back_kernel,
        grid=(tokens // SEQ, count),
        in_specs=[
            part(0),
            part(1),
            part(2),
            pl.BlockSpec((SEQ, LANES), lambda r, p: (r, grad_first + p)),
            pl.BlockSpec((SEQ, LANES), lambda r, p: (r, first + p)),
            pl.BlockSpec((8, SEQ), lambda r, p: (first + p, r)),
            pl.BlockSpec((SEQ, 1), lambda r, p: (r, 0)),
            pl.BlockSpec((1, SEQ), lambda r, p: (0, r)),
        ],
        out_specs=pl.BlockSpec((SEQ, 3 * count * LANES), lambda r, p: (r, 0)),
        out_shape=jax.ShapeDtypeStruct((tokens, 3 * count * LANES), low),
        scratch_shapes=[pltpu.VMEM((SEQ, SEQ), f32), pltpu.VMEM((LANES, SEQ), f32)],
        compiler_params=pltpu.CompilerParams(vmem_limit_bytes=48 * 2**20),
        cost_estimate=hint(4.8 * count),
        name="attend_back",
    )(packed, packed, packed, grad_mixed, mixed, lse, doc_col, doc_row)


def norm_parts(values):
    centre = values - jnp.mean(values, axis=-1, keepdims=True)
    spread = jnp.mean(centre * centre, axis=-1, keepdims=True)
    scale = lax.rsqrt(spread + eps)
    return centre * scale, scale


def norm_back(grad, normal, scale, gain):
    moved = grad * gain
    return scale * (
        moved
        - jnp.mean(moved, axis=-1, keepdims=True)
        - normal * jnp.mean(moved * normal, axis=-1, keepdims=True)
    )


def sum_slabs(values):
    return jnp.sum(values.reshape(-1, 8, values.shape[1]), axis=0)


def after_attend_kernel(
    mixed_refs, proj_ref, x_ref, grad_ref, norm_ref, centre_ref, route_ref, slot_ref, outs, sent
):
    after_ref, grad_rows_ref, gate_ref, out_refs = outs[0], outs[1], outs[2], outs[3:]
    step = pl.program_id(0)
    attended = 0.0
    depth = 0
    for mixed in mixed_refs:
        wide = mixed.shape[1]
        attended = attended + dot_rows(mixed[...], proj_ref[depth : depth + wide, :])
        depth += wide
    after = x_ref[...].astype(f32) + attended
    after_ref[...] = after
    normal, _ = norm_parts(after)
    sent_low = (normal * norm_ref[2:3, :] + norm_ref[3:4, :]).astype(low)
    sent[pl.ds(pl.multiple_of(step * BLOCK, BLOCK), BLOCK), :] = sent_low
    experts = centre_ref.shape[0]
    onehot = route_ref[...] == lax.broadcasted_iota(jnp.int32, (BLOCK, experts), 1)
    picked = dot_rows(onehot.astype(low), centre_ref[...])
    gate = jax.nn.sigmoid(jnp.sum(sent_low.astype(f32) * picked, axis=-1, keepdims=True))
    grad_rows_ref[...] = (gate * grad_ref[...].astype(f32)).astype(low)
    gate_ref[...] = jnp.broadcast_to(gate, gate_ref.shape)

    @pl.when(step == pl.num_programs(0) - 1)
    def _():
        base = 0
        for out_ref in out_refs:
            for row in range(0, out_ref.shape[0], BLOCK):
                slots = lax.broadcasted_iota(jnp.int32, (BLOCK, sent.shape[0]), 0) + base
                place = (slots == slot_ref[...]).astype(low)
                out_ref[row : row + BLOCK, :] = dot_rows(place, sent[...]).astype(low)
                base += BLOCK


def after_attend(mixed, proj, tokens, out_grad, norms, centres, routes, slot_row, chunk_rows):
    count, width = tokens.shape
    chunks = len(chunk_rows)
    tile = pl.BlockSpec((BLOCK, width), lambda i: (i, 0))

    def kernel(*refs):
        n = len(mixed)
        after_attend_kernel(refs[:n], *refs[n : n + 7], refs[n + 7 : -1], refs[-1])

    return pl.pallas_call(
        kernel,
        grid=(count // BLOCK,),
        in_specs=[pl.BlockSpec((BLOCK, m.shape[1]), lambda i: (i, 0)) for m in mixed]
        + [
            pl.BlockSpec((width, width), lambda i: (0, 0)),
            tile,
            tile,
            pl.BlockSpec(norms.shape, lambda i: (0, 0)),
            pl.BlockSpec(centres.shape, lambda i: (0, 0)),
            pl.BlockSpec((BLOCK, 1), lambda i: (i, 0)),
            pl.BlockSpec((1, count), lambda i: (0, 0)),
        ],
        out_specs=[tile, tile, pl.BlockSpec((BLOCK, LANES), lambda i: (i, 0))]
        + [pl.BlockSpec((rows, width), lambda i: (0, 0)) for rows in chunk_rows],
        out_shape=[
            jax.ShapeDtypeStruct((count, width), f32),
            jax.ShapeDtypeStruct((count, width), low),
            jax.ShapeDtypeStruct((count, LANES), f32),
        ]
        + [jax.ShapeDtypeStruct((rows, width), low) for rows in chunk_rows],
        scratch_shapes=[pltpu.VMEM((count, width), low)],
        compiler_params=pltpu.CompilerParams(vmem_limit_bytes=48 * 2**20),
        cost_estimate=hint(13),
        name="after_attend",
    )(*mixed, proj, tokens, out_grad, norms, centres, routes, slot_row)


def picked_rows(slot_ref, row_refs):
    base, total = 0, 0.0
    for rows in row_refs:
        slots = lax.broadcasted_iota(jnp.int32, (BLOCK, rows.shape[0]), 1) + base
        place = (slots == slot_ref[...]).astype(low)
        total = total + dot_rows(place, rows[...])
        base += rows.shape[0]
    return total


def before_attend_back_kernel(
    row_refs, slot_ref, after_ref, grad_ref, norm_ref, proj_ref, outs
):
    grad_after_ref, grad_low_ref, grad_mixed_ref, sums_ref = outs
    grad_normed = picked_rows(slot_ref, row_refs)
    normal, scale = norm_parts(after_ref[...])
    grad_after = grad_ref[...].astype(f32) + norm_back(
        grad_normed, normal, scale, norm_ref[2:3, :]
    )
    grad_after_ref[...] = grad_after
    grad_low = grad_after.astype(low)
    grad_low_ref[...] = grad_low
    grad_mixed_ref[...] = dot_cols(grad_low, proj_ref[...]).astype(low)
    sums = jnp.concatenate([sum_slabs(grad_normed * normal), sum_slabs(grad_normed)], axis=0)

    @pl.when(pl.program_id(0) == 0)
    def _():
        sums_ref[...] = sums

    @pl.when(pl.program_id(0) > 0)
    def _():
        sums_ref[...] += sums


def before_attend_back(rows, slot_col, after, out_grad, norms, proj):
    count, width = after.shape
    tile = pl.BlockSpec((BLOCK, width), lambda i: (i, 0))

    def kernel(*refs):
        n = len(rows)
        before_attend_back_kernel(refs[:n], *refs[n : n + 5], refs[n + 5 :])

    return pl.pallas_call(
        kernel,
        grid=(count // BLOCK,),
        in_specs=[pl.BlockSpec(r.shape, lambda i: (0, 0)) for r in rows]
        + [
            pl.BlockSpec((BLOCK, 1), lambda i: (i, 0)),
            tile,
            tile,
            pl.BlockSpec(norms.shape, lambda i: (0, 0)),
            pl.BlockSpec((width, width), lambda i: (0, 0)),
        ],
        out_specs=[tile, tile, tile, pl.BlockSpec((16, width), lambda i: (0, 0))],
        out_shape=[
            jax.ShapeDtypeStruct((count, width), f32),
            jax.ShapeDtypeStruct((count, width), low),
            jax.ShapeDtypeStruct((count, width), low),
            jax.ShapeDtypeStruct((16, width), f32),
        ],
        compiler_params=pltpu.CompilerParams(vmem_limit_bytes=48 * 2**20),
        cost_estimate=hint(12),
        name="before_attend_back",
    )(*rows, slot_col, after, out_grad, norms, proj)


def input_grad_kernel(plan, grad_refs, weight_refs, x_ref, norm_ref, grad_after_ref, outs):
    out_ref, sums_ref = outs
    grad_normed = 0.0
    for grad, (strip, offset, wide) in zip(grad_refs, plan):
        for s in range(3):
            weight = weight_refs[3 * strip + s]
            grad_normed = grad_normed + dot_cols(
                grad[:, s * wide : (s + 1) * wide], weight[:, offset : offset + wide]
            )
    normal, scale = norm_parts(x_ref[...].astype(f32))
    out_ref[...] = grad_after_ref[...] + norm_back(grad_normed, normal, scale, norm_ref[0:1, :])
    sums = jnp.concatenate([sum_slabs(grad_normed * normal), sum_slabs(grad_normed)], axis=0)

    @pl.when(pl.program_id(0) == 0)
    def _():
        sums_ref[...] = sums

    @pl.when(pl.program_id(0) > 0)
    def _():
        sums_ref[...] += sums


def input_gradient(plan, grads, weights, tokens, norms, grad_after):
    count, width = tokens.shape
    tile = pl.BlockSpec((BLOCK, width), lambda i: (i, 0))

    def kernel(*refs):
        n, m = len(grads), len(grads) + len(weights)
        input_grad_kernel(plan, refs[:n], refs[n:m], *refs[m : m + 3], refs[m + 3 :])

    return pl.pallas_call(
        kernel,
        grid=(count // BLOCK,),
        in_specs=[pl.BlockSpec((BLOCK, g.shape[1]), lambda i: (i, 0)) for g in grads]
        + [
            pl.BlockSpec((width, columns), lambda i, block=block: (0, block))
            for _, block, columns in weights
        ]
        + [
            tile,
            pl.BlockSpec(norms.shape, lambda i: (0, 0)),
            tile,
        ],
        out_specs=[tile, pl.BlockSpec((16, width), lambda i: (0, 0))],
        out_shape=[
            jax.ShapeDtypeStruct((count, width), f32),
            jax.ShapeDtypeStruct((16, width), f32),
        ],
        compiler_params=pltpu.CompilerParams(vmem_limit_bytes=48 * 2**20),
        cost_estimate=hint(14),
        name="input_gradient",
    )(*grads, *[array for array, _, _ in weights], tokens, norms, grad_after)


def activations_of(rows, slot_col, gate, after):
    count, width = after.shape
    tile = pl.BlockSpec((BLOCK, width), lambda i: (i, 0))

    def kernel(*refs):
        n = len(rows)
        slot_ref, gate_ref, after_ref, out_ref = refs[n:]
        found = picked_rows(slot_ref, refs[:n])
        out_ref[...] = (after_ref[...] + gate_ref[:, :1] * found).astype(low)

    return pl.pallas_call(
        kernel,
        grid=(count // BLOCK,),
        in_specs=[pl.BlockSpec(r.shape, lambda i: (0, 0)) for r in rows]
        + [
            pl.BlockSpec((BLOCK, 1), lambda i: (i, 0)),
            pl.BlockSpec((BLOCK, LANES), lambda i: (i, 0)),
            tile,
        ],
        out_specs=tile,
        out_shape=jax.ShapeDtypeStruct((count, width), low),
        compiler_params=pltpu.CompilerParams(vmem_limit_bytes=48 * 2**20),
        cost_estimate=hint(7.5),
        name="activations_of",
    )(*rows, slot_col, gate, after)


def gelu_and_slope(x):
    point = 1.0 / (1.0 + (erfc_point * math.sqrt(0.5)) * jnp.abs(x))
    bell = jnp.exp(-0.5 * x * x)
    tail = erfc_terms[-1]
    for term in erfc_terms[-2::-1]:
        tail = tail * point + term
    tail = tail * point * bell
    below = jnp.where(x >= 0.0, 1.0 - tail, tail)
    return x * below, below + x * bell * (1.0 / math.sqrt(2.0 * math.pi))


def row_groups(experts, each):
    group = max(g for g in range(1, experts + 1) if experts % g == 0 and g * each <= BLOCK)
    return group, group * each


def expert_kernel(x_ref, in_ref, *rest):
    hidden_ref, slope_ref = rest[-2:]
    experts, each, width = x_ref.shape
    group, size = row_groups(experts, each)
    for e in range(0, experts, group):
        preact = dot_rows(x_ref[e : e + group].reshape(size, width), in_ref[...])
        value, slope = gelu_and_slope(preact)
        hidden_ref[e : e + group] = value.astype(low).reshape(group, each, -1)
        slope_ref[e : e + group] = slope.astype(low).reshape(group, each, -1)


def expert_forward(arrived, weight_in, chunk, chunks, buffer=None, tile=512):
    experts, each, width = arrived.shape
    inner = weight_in.shape[1]
    return pl.pallas_call(
        expert_kernel,
        grid=(inner // tile,),
        in_specs=[
            pl.BlockSpec((experts, each, width), lambda j: (0, 0, 0)),
            pl.BlockSpec((width, tile), lambda j: (0, j)),
        ]
        + ([] if buffer is None else [pl.BlockSpec(memory_space=pl.ANY)]),
        out_specs=[
            pl.BlockSpec((experts, each, tile), lambda j: (0, chunk, j)),
            pl.BlockSpec((experts, each, tile), lambda j: (0, 0, j)),
        ],
        out_shape=[
            jax.ShapeDtypeStruct((experts, chunks * each, inner), low),
            jax.ShapeDtypeStruct((experts, each, inner), low),
        ],
        input_output_aliases={} if buffer is None else {2: 0},
        compiler_params=pltpu.CompilerParams(vmem_limit_bytes=56 * 2**20),
        cost_estimate=hint(21),
        name="expert_forward",
    )(arrived, weight_in, *([] if buffer is None else [buffer]))


def expert_back_kernel(
    grad_ref, slope_ref, in_ref, out_ref, x_ref, result_ref, centre_ref, *rest
):
    grad_preact_ref, grad_rows_ref, grad_centre_ref, strips, grad_logit_ref = rest[-5:]
    step = pl.program_id(0)
    count, size, tile = strips.shape
    each = grad_ref.shape[1]

    @pl.when(step < count)
    def _():
        grad_hidden = dot_cols(grad_ref[...].reshape(size, -1), out_ref[...])
        grad_preact = (grad_hidden * slope_ref[...].reshape(size, tile).astype(f32)).astype(low)
        strips[step] = grad_preact
        grad_preact_ref[...] = grad_preact.reshape(-1, each, tile)

    @pl.when(step == count)
    def _():
        centre = centre_ref[...].astype(f32)
        grad_centre = jnp.zeros(grad_centre_ref.shape, f32)
        group, rows = row_groups(grad_ref.shape[0], each)
        for e in range(0, grad_ref.shape[0], group):
            x = x_ref[e : e + group].reshape(rows, -1).astype(f32)
            gate = jax.nn.sigmoid(jnp.sum(x * centre, axis=-1, keepdims=True))
            grad = grad_ref[e : e + group].reshape(rows, -1).astype(f32)
            moved = grad * result_ref[e : e + group].reshape(rows, -1).astype(f32)
            grad_logit = jnp.sum(moved, axis=-1, keepdims=True) * (1.0 - gate)
            grad_logit_ref[e * each : e * each + rows, :] = jnp.broadcast_to(
                grad_logit, (rows, LANES)
            )
            grad_centre = grad_centre + sum_slabs(grad_logit * x)
        grad_centre_ref[...] = grad_centre

    @pl.when(step >= count)
    def _():
        columns = grad_rows_ref.shape[2]
        start = pl.multiple_of((step - count) * columns, columns)
        centre = centre_ref[:, pl.ds(start, columns)].astype(f32)
        total = grad_logit_ref[:, :1] * centre
        for k in range(count):
            total = total + dot_cols(strips[k], in_ref[:, k * tile : (k + 1) * tile])
        grad_rows_ref[...] = total.astype(low).reshape(-1, each, columns)


def expert_back(
    grad_arrived,
    slope,
    weight_in,
    weight_out,
    arrived,
    result,
    centre,
    chunk,
    chunks,
    buffer=None,
    tile=1024,
    columns=256,
):
    experts, each, width = grad_arrived.shape
    inner = weight_in.shape[1]
    count = inner // tile
    alone = pl.BlockSpec((experts, each, width), lambda j: (0, 0, 0))

    def strip(j):
        return jnp.minimum(j, count - 1)

    def part(j):
        return jnp.maximum(j - count, 0)

    return pl.pallas_call(
        expert_back_kernel,
        grid=(count + width // columns,),
        in_specs=[
            alone,
            pl.BlockSpec((experts, each, tile), lambda j: (0, 0, strip(j))),
            pl.BlockSpec((columns, inner), lambda j: (part(j), 0)),
            pl.BlockSpec((tile, width), lambda j: (strip(j), 0)),
            alone,
            pl.BlockSpec((experts, each, width), lambda j: (0, chunk, 0)),
            pl.BlockSpec((1, width), lambda j: (0, 0)),
        ]
        + ([] if buffer is None else [pl.BlockSpec(memory_space=pl.ANY)]),
        out_specs=[
            pl.BlockSpec((experts, each, tile), lambda j: (0, chunk, strip(j))),
            pl.BlockSpec((experts, each, columns), lambda j: (0, 0, part(j))),
            pl.BlockSpec((8, width), lambda j: (0, 0)),
        ],
        out_shape=[
            jax.ShapeDtypeStruct((experts, chunks * each, inner), low),
            jax.ShapeDtypeStruct((experts, each, width), low),
            jax.ShapeDtypeStruct((8, width), f32),
        ],
        scratch_shapes=[
            pltpu.VMEM((count, experts * each, tile), low),
            pltpu.VMEM((experts * each, LANES), f32),
        ],
        input_output_aliases={} if buffer is None else {7: 0},
        compiler_params=pltpu.CompilerParams(vmem_limit_bytes=58 * 2**20),
        cost_estimate=hint(23),
        name="expert_back",
    )(
        grad_arrived,
        slope,
        weight_in,
        weight_out,
        arrived,
        result,
        centre,
        *([] if buffer is None else [buffer]),
    )


def weight_grads_kernel(chunks, refs):
    x_refs, grad_refs = refs[:chunks], refs[chunks : 2 * chunks]
    grad_preact_ref, hidden_ref, in_out_ref, out_out_ref, turned = refs[2 * chunks :]
    step = pl.program_id(0)
    half = pl.num_programs(0) // 2

    def turn_rows(chunk_refs):
        for c, ref in enumerate(chunk_refs):
            experts, each, width = ref.shape
            group, size = row_groups(experts, each)
            for e in range(0, experts, group):
                turned[c, :, e * each : e * each + size] = (
                    ref[e : e + group].reshape(size, width).T
                )

    pl.when(step == 0)(lambda: turn_rows(x_refs))
    pl.when(step == half)(lambda: turn_rows(grad_refs))

    def multiply(ref, out_ref):
        experts, slots, tile = ref.shape
        each = slots // chunks
        right = [
            ref[:, c * each : (c + 1) * each, :].reshape(experts * each, tile)
            for c in range(chunks)
        ]
        for row in range(0, turned.shape[1], BLOCK):
            rows = slice(row, row + BLOCK)
            total = dot_rows(turned[0, rows, :], right[0])
            for c in range(1, chunks):
                total = total + dot_rows(turned[c, rows, :], right[c])
            out_ref[rows, :] = total.astype(low)

    pl.when(step < half)(lambda: multiply(grad_preact_ref, in_out_ref))
    pl.when(step >= half)(lambda: multiply(hidden_ref, out_out_ref))


def weight_grads(arrived, grad_arrived, grad_preact, hidden, tile=1024):
    chunks = len(arrived)
    experts, each, width = arrived[0].shape
    slots, inner = hidden.shape[1:]
    half = inner // tile
    whole = pl.BlockSpec((experts, each, width), lambda j: (0, 0, 0))

    def first(j):
        return jnp.minimum(j, half - 1)

    def second(j):
        return jnp.maximum(j - half, 0)

    return pl.pallas_call(
        lambda *refs: weight_grads_kernel(chunks, refs),
        grid=(2 * half,),
        in_specs=[whole] * (2 * chunks)
        + [
            pl.BlockSpec((experts, slots, tile), lambda j: (0, 0, first(j))),
            pl.BlockSpec((experts, slots, tile), lambda j: (0, 0, second(j))),
        ],
        out_specs=[
            pl.BlockSpec((width, tile), lambda j: (0, first(j))),
            pl.BlockSpec((width, tile), lambda j: (0, second(j))),
        ],
        out_shape=[jax.ShapeDtypeStruct((width, inner), low)] * 2,
        scratch_shapes=[pltpu.VMEM((chunks, width, experts * each), low)],
        compiler_params=pltpu.CompilerParams(vmem_limit_bytes=58 * 2**20),
        cost_estimate=hint(38),
        name="weight_grads",
    )(*arrived, *grad_arrived, grad_preact, hidden)


def update(weight, moment, average, gradient, factor, rate):
    clipped = gradient * factor
    moment_new = momentum_rate * moment + clipped
    weight_new = weight - rate * (clipped + momentum_rate * moment_new)
    average_new = average_rate * average + (1.0 - average_rate) * weight_new
    return (weight_new, moment_new, average_new)


def step_kernel(factor_ref, *refs):
    inputs, outputs = refs[:8], refs[8:]
    factor = factor_ref[0]
    for which in range(2):
        weight, moment, average, gradient = inputs[4 * which : 4 * which + 4]
        gradient = gradient[...] if which == 0 else gradient[...].T
        stepped = update(
            weight[0], moment[0], average[0], gradient.astype(f32), factor, learn_rate
        )
        for out, value in zip(outputs[3 * which : 3 * which + 3], stepped):
            out[0] = value


def step_experts(factor, first, second, tile=256):
    rows, columns = first[0].shape[1:]
    along = pl.BlockSpec((1, rows, tile), lambda j: (0, 0, j))
    down = pl.BlockSpec((1, tile, rows), lambda j: (0, j, 0))
    gradient = pl.BlockSpec((rows, tile), lambda j: (0, j))
    return pl.pallas_call(
        step_kernel,
        grid=(columns // tile,),
        in_specs=[pl.BlockSpec(memory_space=pltpu.SMEM)]
        + [along] * 3
        + [gradient]
        + [down] * 3
        + [gradient],
        out_specs=[along] * 3 + [down] * 3,
        out_shape=[jax.ShapeDtypeStruct(first[0].shape, f32)] * 3
        + [jax.ShapeDtypeStruct(second[0].shape, f32)] * 3,
        compiler_params=pltpu.CompilerParams(vmem_limit_bytes=48 * 2**20),
        cost_estimate=hint(20),
        name="step_experts",
    )(factor.reshape(1), *first, *second)


def swap(values, axis, distance):
    size = lax.axis_size(axis)
    return lax.ppermute(values, axis, [(i, i ^ distance) for i in range(size)])


def assemble_kernel(me_ref, *refs):
    pieces, out_ref = refs[:-1], refs[-1]
    experts, rows = pieces[0].shape[0], pieces[0].shape[1]
    for t, piece in enumerate(pieces):
        for e in range(experts):
            owner = e * len(pieces) + (me_ref[0] ^ t)
            out_ref[pl.ds(pl.multiple_of(owner * rows, rows), rows), :] = piece[e]


def assemble(pieces):
    experts, rows, columns = pieces[0].shape
    dp = len(pieces)
    return pl.pallas_call(
        assemble_kernel,
        in_specs=[pl.BlockSpec(memory_space=pltpu.SMEM)]
        + [pl.BlockSpec(memory_space=pltpu.VMEM)] * dp,
        out_specs=pl.BlockSpec(memory_space=pltpu.VMEM),
        out_shape=jax.ShapeDtypeStruct((experts * dp * rows, columns), pieces[0].dtype),
        compiler_params=pltpu.CompilerParams(vmem_limit_bytes=32 * 2**20),
        cost_estimate=hint(4),
        name="assemble",
    )(lax.axis_index("dp").astype(jnp.int32).reshape(1), *pieces)


def sum_halves(parts, axis, bit, at):
    own = (lax.axis_index(axis) // bit) % 2

    def side(which):
        picked = []
        for part in parts:
            shape = part.shape
            halves = part.reshape(shape[:at] + (shape[at] // 2, 2) + shape[at + 1 :])
            picked.append(lax.dynamic_index_in_dim(halves, which, at + 1, keepdims=False))
        return jnp.concatenate(picked, axis=-1)

    return (side(own).astype(f32) + swap(side(1 - own), axis, bit).astype(f32)).astype(low)


def sum_over_cores(parts):
    return sum_halves(parts, "dp", 1, 1)


def sum_over_neighbours(held):
    return sum_halves([held], "expert", 1, 0)


def sum_over_pairs(held, partners, keep, *beside):
    experts, dp = lax.axis_size("expert"), lax.axis_size("dp")
    total = lax.dynamic_index_in_dim(held, keep, 0, keepdims=False).astype(f32)
    received = []
    for offset, (far, near) in enumerate(partners, 1):
        block = lax.dynamic_index_in_dim(held, jnp.bitwise_xor(keep, offset), 0, keepdims=False)
        perm = [
            (e * dp + d, (e ^ far) * dp + (d ^ near)) for e in range(experts) for d in range(dp)
        ]
        received.append(lax.ppermute(block, everywhere, perm))
    if beside:
        moved = in_order(*received, *beside)
        received, beside = moved[: len(received)], moved[len(received) :]
    for block in received:
        total = total + block.astype(f32)
    return (total, *beside) if beside else total


def sum_near(held):
    near = held.shape[1]
    held = held.reshape((held.shape[0] // 2, 2 * near) + held.shape[2:]).swapaxes(0, 1)
    partners = [(i // near, i % near * 2) for i in range(1, 2 * near)]
    keep = lax.axis_index("expert") % 2 * near + lax.axis_index("dp") // 2
    return sum_over_pairs(held, partners, keep).astype(low)


def sum_far(held, *beside):
    partners = [(2 * i, 0) for i in range(1, held.shape[0])]
    return sum_over_pairs(held, partners, lax.axis_index("expert") // 2, *beside)


def sum_across(held):
    partners = [(0, 2 * i) for i in range(1, held.shape[0])]
    return sum_over_pairs(held, partners, lax.axis_index("dp") // 2)


def in_order(*values):
    return lax.optimization_barrier(values)


def sum_everywhere(value):
    held = value.reshape(1, 1)
    for axis in ("dp", "expert"):
        distance = 1
        while distance < lax.axis_size(axis):
            held = held + swap(held, axis, distance)
            distance *= 2
    return held[0, 0]


def shards(
    tokens,
    documents,
    routes,
    out_grad,
    norm_params,
    qkv_weight,
    proj_weight,
    centroids,
    expert_in,
    expert_out,
    norm_moment,
    qkv_moment,
    proj_moment,
    centroid_moment,
    in_moment,
    out_moment,
    norm_average,
    qkv_average,
    proj_average,
    centroid_average,
    in_average,
    out_average,
):
    local_tokens, width = tokens.shape
    experts = lax.axis_size("expert")
    dp = lax.axis_size("dp")
    devices = experts * dp
    slot_cap = max(2, 3 * local_tokens // (2 * experts))
    slots = experts * slot_cap
    chunks = 2 if slot_cap % 32 == 0 else 1
    half_cap = slot_cap // chunks
    rows_own = qkv_weight.shape[0]
    norm_own = norm_params.shape[1]
    centre_own = centroids.shape[1]
    groups = 4

    strips = 2
    strip = width // strips
    small = jnp.concatenate([norm_params.reshape(-1), centroids.reshape(-1)]).astype(low)
    small = jnp.pad(small, (0, rows_own * LANES - small.shape[0])).reshape(rows_own, LANES)
    qkv_low = qkv_weight.astype(low)
    qkv_own = [
        [qkv_low[:, s * width + h * strip : s * width + (h + 1) * strip] for s in range(3)]
        for h in range(strips)
    ]
    front = jnp.concatenate([*qkv_own[0], small], axis=1)
    later = jnp.concatenate([proj_weight.astype(low), *qkv_own[1]], axis=1)
    later = lax.all_gather(later, everywhere, axis=0, tiled=True)
    in_low, out_low = expert_in.astype(low), expert_out.astype(low)

    route_ids = routes[:, 0]
    onehot = route_ids[:, None] == jnp.arange(experts, dtype=jnp.int32)[None, :]
    running = jnp.cumsum(onehot.astype(jnp.int32), axis=0)
    within = jnp.sum(running * onehot.astype(jnp.int32), axis=1) - 1
    slot_index = route_ids * slot_cap + within
    chunked = (within // half_cap * experts + route_ids) * half_cap + within % half_cap
    slot_row, slot_col = slot_index[None, :], slot_index[:, None]
    chunked_row, chunked_col = chunked[None, :], chunked[:, None]
    doc_col = documents[:, None]
    doc_row = documents[None, :]

    if rows_own % 16:
        front = lax.all_gather(front, everywhere, axis=0, tiled=True)
    else:
        spread = jnp.broadcast_to(front[None], (experts,) + front.shape)
        spread = lax.all_to_all(spread, "expert", split_axis=0, concat_axis=0, tiled=True)
        spread, in_low, out_low, slot_row, slot_col, chunked_row, chunked_col = in_order(
            spread, in_low, out_low, slot_row, slot_col, chunked_row, chunked_col
        )
        pieces = {0: spread}
        distance = dp // 2
        while distance:
            for t in list(pieces):
                pieces[t | distance] = swap(pieces[t], "dp", distance)
            distance //= 2
        front = assemble([pieces[t] for t in range(dp)])
    weight_in = lax.all_gather(in_low, "dp", axis=1, tiled=True)[0]
    weight_out = lax.all_gather(out_low, "dp", axis=2, tiled=True)[0]
    small_full = front[:, 3 * strip :].reshape(devices, rows_own * LANES)
    norms = (
        small_full[:, : 4 * norm_own].reshape(devices, 4, norm_own).transpose(1, 0, 2)
    ).reshape(4, width).astype(f32)
    centre_table = small_full[:, 4 * norm_own : 4 * norm_own + centre_own].reshape(experts, width)

    normed_low = layer_norm(tokens.astype(f32), norms[0], norms[1]).astype(low)
    normed_low, front = in_order(normed_low, front)
    packed, mixed, lse = [], [], []
    for weight in (front[:, : 3 * strip], later[:, width:]):
        packed_h = jnp.dot(normed_low, weight, preferred_element_type=f32).astype(low)
        mixed_h, lse_h = attend(packed_h, doc_col, doc_row)
        packed.append(packed_h)
        mixed.append(mixed_h)
        lse.append(lse_h)
    after, grad_rows, gate, *outgoing = after_attend(
        mixed,
        later,
        tokens,
        out_grad,
        norms,
        centre_table,
        routes,
        chunked_row,
        [slots // chunks] * chunks,
    )

    def exchange(rows):
        rows = rows.reshape(experts, -1, width)
        return lax.all_to_all(rows, "expert", split_axis=0, concat_axis=0, tiled=True)

    grad_outgoing = []
    for c in range(chunks):
        own = jnp.arange(slots // chunks, dtype=jnp.int32)[:, None] + c * (slots // chunks)
        place = (own == chunked_row).astype(low)
        grad_outgoing.append(jnp.dot(place, grad_rows, preferred_element_type=f32).astype(low))
    arrived, slope, hidden = [], [], None
    for c in range(chunks):
        if c:
            arrived[c - 1], outgoing[c], *grad_outgoing = in_order(
                arrived[c - 1], outgoing[c], *grad_outgoing
            )
        arrived.append(exchange(outgoing[c]))
    for c in range(chunks):
        if c == chunks - 1:
            arrived[c], grad_outgoing[0] = in_order(arrived[c], grad_outgoing[0])
        hidden, slope_c = expert_forward(arrived[c], weight_in, c, chunks, hidden)
        slope.append(slope_c)
        if c == 0 and chunks > 1:
            hidden, grad_outgoing[0] = in_order(hidden, grad_outgoing[0])
    grad_arrived = [exchange(grad_outgoing[0])]
    hidden = hidden.reshape(slots, -1)
    result = jnp.dot(hidden, weight_out, preferred_element_type=f32).astype(low)
    result = result.reshape(experts, slot_cap, width)
    for c in range(1, chunks):
        grad_arrived[c - 1], grad_outgoing[c], result = in_order(
            grad_arrived[c - 1], grad_outgoing[c], result
        )
        grad_arrived.append(exchange(grad_outgoing[c]))
    centre_row = lax.dynamic_slice_in_dim(centre_table, lax.axis_index("expert"), 1, 0)
    grad_preact = None
    grad_input, grad_centre = [], 0.0
    for c in range(chunks):
        last = c == chunks - 1
        grad_preact, rows_c, centre_c = expert_back(
            grad_arrived[c],
            slope[c],
            weight_in,
            weight_out,
            arrived[c],
            result,
            centre_row,
            c,
            chunks,
            grad_preact,
        )
        if not last:
            rows_c, grad_arrived[c + 1] = in_order(rows_c, grad_arrived[c + 1])
        elif grad_input:
            rows_c, grad_input[-1] = in_order(rows_c, grad_input[-1])
        grad_input.append(exchange(rows_c).reshape(slots // chunks, width))
        grad_centre = grad_centre + jnp.sum(centre_c, axis=0)
    if chunks > 1:
        hidden, arrived[0], grad_input[0] = in_order(hidden, arrived[0], grad_input[0])
    grad_in, grad_out_turned = weight_grads(
        arrived, grad_arrived, grad_preact, hidden.reshape(experts, slot_cap, -1)
    )
    result, grad_input[-1], grad_in, grad_out_turned = in_order(
        result, grad_input[-1], grad_in, grad_out_turned
    )
    in_grad = lax.psum_scatter(grad_in[None], "dp", scatter_dimension=1, tiled=True)
    out_turned = lax.psum_scatter(grad_out_turned[None], "dp", scatter_dimension=1, tiled=True)
    returned = exchange(result).reshape(slots, width)

    grad_after, grad_low, grad_mixed, sums_two = before_attend_back(
        grad_input, chunked_col, after, out_grad, norms, later
    )

    grad_proj = jnp.concatenate(
        [
            lax.dot_general(m, grad_low, (((0,), (0,)), ((), ())), preferred_element_type=f32)
            for m in mixed
        ],
        axis=0,
    ).astype(low)
    norm_two = jnp.sum(sums_two.reshape(2, 8, width), axis=1)
    norm_two = norm_two.reshape(2, devices, norm_own).transpose(1, 0, 2).reshape(devices, -1)
    mine = jnp.arange(experts)[:, None, None] == lax.axis_index("expert")
    centre_flat = jnp.where(mine, grad_centre.reshape(1, dp, centre_own), 0.0)
    extra = jnp.concatenate([norm_two, centre_flat.reshape(devices, centre_own)], axis=1)
    extra = jnp.pad(extra, ((0, 0), (0, rows_own * LANES - extra.shape[1]))).astype(low)
    extra = extra.reshape(devices * rows_own, LANES)
    each = width // LANES // groups
    wide = each * LANES

    def by_owner(values):
        return values.reshape(experts, dp, rows_own, values.shape[1])

    def back_group(g, *beside):
        h, k = g // (groups // strips), g % (groups // strips)
        part = attend_back(
            packed[h], grad_mixed, mixed[h], lse[h], doc_col, doc_row, k * each, each, g * each
        )
        part, *beside = in_order(part, *beside)
        grad = lax.dot_general(
            normed_low, part, (((0,), (0,)), ((), ())), preferred_element_type=f32
        )
        return part, grad.astype(low), *beside

    parts, grads = [], []
    rest = by_owner(jnp.concatenate([grad_proj, extra], axis=1))
    for g in range(groups):
        if g == 1:
            rest = sum_over_cores([rest])
            rest, grad_mixed = in_order(rest, grad_mixed)
        if g == groups - 1:
            rest = sum_over_neighbours(rest)
            first = sum_over_cores([by_owner(v) for v in grads[: groups // 2]])
            rest, first, grad_mixed, returned = in_order(rest, first, grad_mixed, returned)
            first = sum_over_neighbours(first)
            part, grad, first = back_group(g, first)
        else:
            part, grad = back_group(g)
        grad, grad_mixed = in_order(grad, grad_mixed)
        parts.append(part)
        grads.append(grad)
    second = sum_over_cores([by_owner(v) for v in grads[groups // 2 :]])
    second, first, grad_after = in_order(second, first, grad_after)
    second = sum_near(second)
    first = sum_far(jnp.concatenate([rest, first], axis=-1)).astype(low)
    per_strip = groups // strips
    weights = [(front, s, strip) for s in range(3)]
    weights += [(later, width // strip + s, strip) for s in range(3)]
    input_grad, sums_one = input_gradient(
        [(g // per_strip, g % per_strip * wide, wide) for g in range(groups)],
        parts,
        weights,
        tokens,
        norms,
        grad_after,
    )
    first, second, sums_one, gate = in_order(first, second, sums_one, gate)
    norm_one = jnp.sum(sums_one.reshape(2, 8, width), axis=1)
    norm_one = norm_one.reshape(2, devices, norm_own).transpose(1, 0, 2).reshape(devices, -1)
    norm_one = lax.all_to_all(norm_one, everywhere, split_axis=0, concat_axis=0, tiled=True)
    norm_one, in_grad, out_turned = in_order(norm_one, in_grad, out_turned)
    in_square = jnp.sum(jnp.square(in_grad.astype(f32)))
    out_square = jnp.sum(jnp.square(out_turned.astype(f32)))
    activations = activations_of([returned], slot_col, gate, after)
    norm_one = jnp.sum(norm_one, axis=0).reshape(2, norm_own)
    second, activations, in_square, out_square = sum_far(
        second, activations, in_square, out_square
    )
    first = sum_across(first)
    first, second, in_square, out_square, norm_one, activations = in_order(
        first, second, in_square, out_square, norm_one, activations
    )

    proj_grad = first[:, :width]
    extra = first[:, width : width + LANES].reshape(-1)
    norm_grad = jnp.concatenate([norm_one, extra[: 2 * norm_own].reshape(2, norm_own)], axis=0)
    centre_grad = extra[2 * norm_own : 2 * norm_own + centre_own].reshape(centroids.shape)
    owned = jnp.concatenate([first[:, width + LANES :], second], axis=1)
    qkv_grad = owned.reshape(rows_own, groups, 3, wide).swapaxes(1, 2).reshape(rows_own, 3 * width)
    square_sum = (
        jnp.sum(owned * owned)
        + jnp.sum(proj_grad * proj_grad)
        + jnp.sum(norm_grad * norm_grad)
        + jnp.sum(centre_grad * centre_grad)
        + in_square
        + out_square
    )
    grad_norm = jnp.sqrt(sum_everywhere(square_sum))
    factor = clip_limit / jnp.maximum(grad_norm, clip_limit)
    norm_new = update(norm_params, norm_moment, norm_average, norm_grad, factor, norm_rate)
    qkv_new = update(qkv_weight, qkv_moment, qkv_average, qkv_grad, factor, learn_rate)
    proj_new = update(proj_weight, proj_moment, proj_average, proj_grad, factor, learn_rate)
    centre_new = update(
        centroids, centroid_moment, centroid_average, centre_grad, factor, learn_rate
    )
    stepped = step_experts(
        factor,
        (expert_in, in_moment, in_average, in_grad[0]),
        (expert_out, out_moment, out_average, out_turned[0]),
    )
    in_new, out_new = stepped[:3], stepped[3:]
    return (
        activations,
        input_grad,
        grad_norm,
        norm_new[0],
        qkv_new[0],
        proj_new[0],
        centre_new[0],
        in_new[0],
        out_new[0],
        norm_new[1],
        qkv_new[1],
        proj_new[1],
        centre_new[1],
        in_new[1],
        out_new[1],
        norm_new[2],
        qkv_new[2],
        proj_new[2],
        centre_new[2],
        in_new[2],
        out_new[2],
    )


def solution(mesh):
    placed = (
        P(("expert", "dp"), None),
        P(("expert", "dp")),
        P(("expert", "dp"), None),
        P(("expert", "dp"), None),
        P(None, ("expert", "dp")),
        P(("expert", "dp"), None),
        P(("expert", "dp"), None),
        P("expert", "dp"),
        P("expert", "dp", None),
        P("expert", None, "dp"),
        P(None, ("expert", "dp")),
        P(("expert", "dp"), None),
        P(("expert", "dp"), None),
        P("expert", "dp"),
        P("expert", "dp", None),
        P("expert", None, "dp"),
        P(None, ("expert", "dp")),
        P(("expert", "dp"), None),
        P(("expert", "dp"), None),
        P("expert", "dp"),
        P("expert", "dp", None),
        P("expert", None, "dp"),
    )
    return jax.shard_map(
        shards,
        mesh=mesh,
        in_specs=placed,
        out_specs=(
            P(("expert", "dp"), None),
            P(("expert", "dp"), None),
            P(),
            P(None, ("expert", "dp")),
            P(("expert", "dp"), None),
            P(("expert", "dp"), None),
            P("expert", "dp"),
            P("expert", "dp", None),
            P("expert", None, "dp"),
            P(None, ("expert", "dp")),
            P(("expert", "dp"), None),
            P(("expert", "dp"), None),
            P("expert", "dp"),
            P("expert", "dp", None),
            P("expert", None, "dp"),
            P(None, ("expert", "dp")),
            P(("expert", "dp"), None),
            P(("expert", "dp"), None),
            P("expert", "dp"),
            P("expert", "dp", None),
            P("expert", None, "dp"),
        ),
        check_vma=False,
    )
```

```python
import functools
import math

import jax
import jax.numpy as jnp
from jax import lax
from jax.experimental import pallas as pl
from jax.experimental.pallas import tpu as pltpu
from jax.sharding import PartitionSpec as P

HEAD_DIM = 64
SEQ = 1024
LANES = 128
BLOCK = 256

eps = 1e-05
scale_qk = 0.125
momentum_rate = 0.9
learn_rate = 100.0
norm_rate = 500.0
average_rate = 0.9
clip_limit = 1.0
masked_score = -1000000000.0
everywhere = ("expert", "dp")
low = jnp.bfloat16
f32 = jnp.float32

erfc_point = 0.4
erfc_terms = (
    0.11596270714310389,
    0.08090178846816841,
    0.2341610172367065,
    -0.1854824771652721,
    0.35459055762612957,
    -0.10013360714943426,
)


def hint(microseconds):
    return pl.CostEstimate(
        flops=int(microseconds * 1.9e8), bytes_accessed=0, transcendentals=0
    )


def dot_rows(left, right):
    return lax.dot_general(left, right, (((1,), (0,)), ((), ())), preferred_element_type=f32)


def dot_cols(left, right):
    return lax.dot_general(left, right, (((1,), (1,)), ((), ())), preferred_element_type=f32)


def fill_bias(bias, doc_of_rows, doc_of_cols, rows_are_keys):
    for block in range(0, SEQ, BLOCK):
        rows = lax.broadcasted_iota(jnp.int32, (BLOCK, SEQ), 0) + block
        cols = lax.broadcasted_iota(jnp.int32, (BLOCK, SEQ), 1)
        causal = (rows <= cols) if rows_are_keys else (rows >= cols)
        same = doc_of_rows[block : block + BLOCK, :] == doc_of_cols[...]
        bias[block : block + BLOCK, :] = jnp.where(same & causal, 3.0e38, masked_score)


def in_head(shape, head, axis):
    return lax.broadcasted_iota(jnp.int32, shape, axis) // HEAD_DIM == head


def keep_head(values, head):
    return jnp.where(in_head(values.shape, head, 1), values, jnp.zeros_like(values))


def attend_kernel(q_ref, k_ref, v_ref, doc_col, doc_row, mixed_ref, lse_ref, bias):
    @pl.when(pl.program_id(1) == 0)
    def _():
        fill_bias(bias, doc_col, doc_row, False)

    def scores_of(block):
        seen = block + BLOCK
        query = q_ref[block:seen, :] * jnp.asarray(scale_qk, low)
        return [dot_cols(keep_head(query, head), k_ref[:seen, :]) for head in range(2)]

    following = scores_of(0)
    for block in range(0, SEQ, BLOCK):
        seen = block + BLOCK
        current = following
        if seen < SEQ:
            following = scores_of(seen)
        weights, outs, stats = [], [], []
        for head in range(2):
            scores = jnp.minimum(current[head], bias[block:seen, :seen])
            top = jnp.max(scores, axis=-1, keepdims=True)
            exponent = jnp.exp(scores - top)
            total = jnp.sum(exponent, axis=-1, keepdims=True)
            weights.append((exponent.astype(low), total))
            stats.append(top + jnp.log(total))
        for exponent, total in weights:
            outs.append(dot_rows(exponent, v_ref[:seen, :]) / total)
        first = in_head((BLOCK, LANES), 0, 1)
        mixed_ref[block:seen, :] = jnp.where(first, outs[0], outs[1]).astype(low)
        lane = lax.broadcasted_iota(jnp.int32, (BLOCK, LANES), 1)
        both = jnp.where(lane == 0, stats[0], stats[1])
        lse_ref[:, block:seen] = both.T[:8, :]


def attend(packed, doc_col, doc_row):
    count, wide = packed.shape
    width = wide // 3
    pairs = width // LANES

    def part(which):
        return pl.BlockSpec((SEQ, LANES), lambda r, p, w=which: (r, w * pairs + p))

    return pl.pallas_call(
        attend_kernel,
        grid=(count // SEQ, pairs),
        in_specs=[
            part(0),
            part(1),
            part(2),
            pl.BlockSpec((SEQ, 1), lambda r, p: (r, 0)),
            pl.BlockSpec((1, SEQ), lambda r, p: (0, r)),
        ],
        out_specs=[
            pl.BlockSpec((SEQ, LANES), lambda r, p: (r, p)),
            pl.BlockSpec((8, SEQ), lambda r, p: (p, r)),
        ],
        out_shape=[
            jax.ShapeDtypeStruct((count, width), low),
            jax.ShapeDtypeStruct((8 * pairs, count), f32),
        ],
        scratch_shapes=[pltpu.VMEM((SEQ, SEQ), f32)],
        compiler_params=pltpu.CompilerParams(vmem_limit_bytes=48 * 2**20),
        cost_estimate=hint(29),
        name="attend",
    )(packed, packed, packed, doc_col, doc_row)


def attend_back_kernel(
    q_ref, k_ref, v_ref, grad_ref, mixed_ref, lse_ref, doc_col, doc_row, out_ref, bias, grad_q_t
):
    pair = pl.program_id(1)

    @pl.when(pair == 0)
    def _():
        fill_bias(bias, doc_col, doc_row, True)

    wide = out_ref.shape[1] // 3
    place = [pl.ds(pl.multiple_of(s * wide + pair * LANES, LANES), LANES) for s in range(3)]
    query = q_ref[...] * jnp.asarray(scale_qk, low)
    grad = grad_ref[...]
    product = grad.astype(f32) * mixed_ref[...].astype(f32)
    upper = product.astype(low)
    lower = (product - upper.astype(f32)).astype(low)
    chooser = (
        lax.broadcasted_iota(jnp.int32, (8, LANES), 0)
        == lax.broadcasted_iota(jnp.int32, (8, LANES), 1) // HEAD_DIM
    ).astype(low)
    inner = dot_cols(chooser, upper) + dot_cols(chooser, lower)
    key_t = k_ref[...].T
    def products(block):
        after = block + BLOCK
        return [
            (
                dot_cols(keep_head(k_ref[block:after, :], head), query[block:, :]),
                dot_cols(keep_head(v_ref[block:after, :], head), grad[block:, :]),
            )
            for head in range(2)
        ]

    following = products(0)
    for block in range(0, SEQ, BLOCK):
        after = block + BLOCK
        current = following
        if after < SEQ:
            following = products(after)
        factors = []
        for head in range(2):
            scores, grad_w = current[head]
            scores = jnp.minimum(scores, bias[block:after, block:])
            weights = jnp.exp(scores - lse_ref[head : head + 1, block:])
            grad_s = (weights * (grad_w - inner[head : head + 1, block:])).astype(low)
            factors.append((weights.astype(low), grad_s))
        grad_k, grad_v = [], []
        for head in range(2):
            weights, grad_s = factors[head]
            grad_v.append(dot_rows(weights, grad[block:, :]))
            grad_k.append(dot_rows(grad_s, query[block:, :]))
            rows = slice(head * HEAD_DIM, (head + 1) * HEAD_DIM)
            moved = dot_rows(key_t[rows, block:after], grad_s)
            if block == 0:
                grad_q_t[rows, :] = moved
            else:
                grad_q_t[rows, block:] += moved
        first = in_head((BLOCK, LANES), 0, 1)
        out_ref[block:after, place[1]] = jnp.where(first, grad_k[0], grad_k[1]).astype(low)
        out_ref[block:after, place[2]] = jnp.where(first, grad_v[0], grad_v[1]).astype(low)
    out_ref[:, place[0]] = (grad_q_t[...] * scale_qk).T.astype(low)


def attend_back(packed, grad_mixed, mixed, lse, doc_col, doc_row, first, count, grad_first):
    tokens, wide = packed.shape
    pairs = wide // 3 // LANES

    def part(which):
        return pl.BlockSpec((SEQ, LANES), lambda r, p, w=which: (r, w * pairs + first + p))

    return pl.pallas_call(
        attend_back_kernel,
        grid=(tokens // SEQ, count),
        in_specs=[
            part(0),
            part(1),
            part(2),
            pl.BlockSpec((SEQ, LANES), lambda r, p: (r, grad_first + p)),
            pl.BlockSpec((SEQ, LANES), lambda r, p: (r, first + p)),
            pl.BlockSpec((8, SEQ), lambda r, p: (first + p, r)),
            pl.BlockSpec((SEQ, 1), lambda r, p: (r, 0)),
            pl.BlockSpec((1, SEQ), lambda r, p: (0, r)),
        ],
        out_specs=pl.BlockSpec((SEQ, 3 * count * LANES), lambda r, p: (r, 0)),
        out_shape=jax.ShapeDtypeStruct((tokens, 3 * count * LANES), low),
        scratch_shapes=[pltpu.VMEM((SEQ, SEQ), f32), pltpu.VMEM((LANES, SEQ), f32)],
        compiler_params=pltpu.CompilerParams(vmem_limit_bytes=48 * 2**20),
        cost_estimate=hint(4.8 * count),
        name="attend_back",
    )(packed, packed, packed, grad_mixed, mixed, lse, doc_col, doc_row)


def norm_parts(values):
    centre = values - jnp.mean(values, axis=-1, keepdims=True)
    spread = jnp.mean(centre * centre, axis=-1, keepdims=True)
    scale = lax.rsqrt(spread + eps)
    return centre * scale, scale


def norm_back(grad, normal, scale, gain):
    moved = grad * gain
    return scale * (
        moved
        - jnp.mean(moved, axis=-1, keepdims=True)
        - normal * jnp.mean(moved * normal, axis=-1, keepdims=True)
    )


def sum_slabs(values):
    return jnp.sum(values.reshape(-1, 8, values.shape[1]), axis=0)


def after_attend_kernel(
    mixed_refs, proj_ref, x_ref, grad_ref, norm_ref, centre_ref, route_ref, slot_ref, outs, sent
):
    after_ref, grad_rows_ref, gate_ref, out_refs = outs[0], outs[1], outs[2], outs[3:]
    step = pl.program_id(0)
    attended = 0.0
    depth = 0
    for mixed in mixed_refs:
        wide = mixed.shape[1]
        attended = attended + dot_rows(mixed[...], proj_ref[depth : depth + wide, :])
        depth += wide
    after = x_ref[...].astype(f32) + attended
    after_ref[...] = after
    normal, _ = norm_parts(after)
    sent_low = (normal * norm_ref[2:3, :] + norm_ref[3:4, :]).astype(low)
    sent[pl.ds(pl.multiple_of(step * BLOCK, BLOCK), BLOCK), :] = sent_low
    experts = centre_ref.shape[0]
    onehot = route_ref[...] == lax.broadcasted_iota(jnp.int32, (BLOCK, experts), 1)
    picked = dot_rows(onehot.astype(low), centre_ref[...])
    gate = jax.nn.sigmoid(jnp.sum(sent_low.astype(f32) * picked, axis=-1, keepdims=True))
    grad_rows_ref[...] = (gate * grad_ref[...].astype(f32)).astype(low)
    gate_ref[...] = jnp.broadcast_to(gate, gate_ref.shape)

    @pl.when(step == pl.num_programs(0) - 1)
    def _():
        base = 0
        for out_ref in out_refs:
            for row in range(0, out_ref.shape[0], BLOCK):
                slots = lax.broadcasted_iota(jnp.int32, (BLOCK, sent.shape[0]), 0) + base
                place = (slots == slot_ref[...]).astype(low)
                out_ref[row : row + BLOCK, :] = dot_rows(place, sent[...]).astype(low)
                base += BLOCK


def after_attend(mixed, proj, tokens, out_grad, norms, centres, routes, slot_row, chunk_rows):
    count, width = tokens.shape
    chunks = len(chunk_rows)
    tile = pl.BlockSpec((BLOCK, width), lambda i: (i, 0))

    def kernel(*refs):
        n = len(mixed)
        after_attend_kernel(refs[:n], *refs[n : n + 7], refs[n + 7 : -1], refs[-1])

    return pl.pallas_call(
        kernel,
        grid=(count // BLOCK,),
        in_specs=[pl.BlockSpec((BLOCK, m.shape[1]), lambda i: (i, 0)) for m in mixed]
        + [
            pl.BlockSpec((width, width), lambda i: (0, 0)),
            tile,
            tile,
            pl.BlockSpec(norms.shape, lambda i: (0, 0)),
            pl.BlockSpec(centres.shape, lambda i: (0, 0)),
            pl.BlockSpec((BLOCK, 1), lambda i: (i, 0)),
            pl.BlockSpec((1, count), lambda i: (0, 0)),
        ],
        out_specs=[tile, tile, pl.BlockSpec((BLOCK, LANES), lambda i: (i, 0))]
        + [pl.BlockSpec((rows, width), lambda i: (0, 0)) for rows in chunk_rows],
        out_shape=[
            jax.ShapeDtypeStruct((count, width), f32),
            jax.ShapeDtypeStruct((count, width), low),
            jax.ShapeDtypeStruct((count, LANES), f32),
        ]
        + [jax.ShapeDtypeStruct((rows, width), low) for rows in chunk_rows],
        scratch_shapes=[pltpu.VMEM((count, width), low)],
        compiler_params=pltpu.CompilerParams(vmem_limit_bytes=48 * 2**20),
        cost_estimate=hint(13),
        name="after_attend",
    )(*mixed, proj, tokens, out_grad, norms, centres, routes, slot_row)


def picked_rows(slot_ref, row_refs):
    base, total = 0, 0.0
    for rows in row_refs:
        slots = lax.broadcasted_iota(jnp.int32, (BLOCK, rows.shape[0]), 1) + base
        place = (slots == slot_ref[...]).astype(low)
        total = total + dot_rows(place, rows[...])
        base += rows.shape[0]
    return total


def before_attend_back_kernel(
    row_refs, slot_ref, after_ref, grad_ref, norm_ref, proj_ref, outs
):
    grad_after_ref, grad_low_ref, grad_mixed_ref, sums_ref = outs
    grad_normed = picked_rows(slot_ref, row_refs)
    normal, scale = norm_parts(after_ref[...])
    grad_after = grad_ref[...].astype(f32) + norm_back(
        grad_normed, normal, scale, norm_ref[2:3, :]
    )
    grad_after_ref[...] = grad_after
    grad_low = grad_after.astype(low)
    grad_low_ref[...] = grad_low
    grad_mixed_ref[...] = dot_cols(grad_low, proj_ref[...]).astype(low)
    sums = jnp.concatenate([sum_slabs(grad_normed * normal), sum_slabs(grad_normed)], axis=0)

    @pl.when(pl.program_id(0) == 0)
    def _():
        sums_ref[...] = sums

    @pl.when(pl.program_id(0) > 0)
    def _():
        sums_ref[...] += sums


def before_attend_back(rows, slot_col, after, out_grad, norms, proj):
    count, width = after.shape
    tile = pl.BlockSpec((BLOCK, width), lambda i: (i, 0))

    def kernel(*refs):
        n = len(rows)
        before_attend_back_kernel(refs[:n], *refs[n : n + 5], refs[n + 5 :])

    return pl.pallas_call(
        kernel,
        grid=(count // BLOCK,),
        in_specs=[pl.BlockSpec(r.shape, lambda i: (0, 0)) for r in rows]
        + [
            pl.BlockSpec((BLOCK, 1), lambda i: (i, 0)),
            tile,
            tile,
            pl.BlockSpec(norms.shape, lambda i: (0, 0)),
            pl.BlockSpec((width, width), lambda i: (0, 0)),
        ],
        out_specs=[tile, tile, tile, pl.BlockSpec((16, width), lambda i: (0, 0))],
        out_shape=[
            jax.ShapeDtypeStruct((count, width), f32),
            jax.ShapeDtypeStruct((count, width), low),
            jax.ShapeDtypeStruct((count, width), low),
            jax.ShapeDtypeStruct((16, width), f32),
        ],
        compiler_params=pltpu.CompilerParams(vmem_limit_bytes=48 * 2**20),
        cost_estimate=hint(12),
        name="before_attend_back",
    )(*rows, slot_col, after, out_grad, norms, proj)


def input_grad_kernel(plan, grad_refs, weight_refs, x_ref, norm_ref, grad_after_ref, outs):
    out_ref, sums_ref = outs
    grad_normed = 0.0
    for grad, (strip, offset, wide) in zip(grad_refs, plan):
        for s in range(3):
            weight = weight_refs[3 * strip + s]
            grad_normed = grad_normed + dot_cols(
                grad[:, s * wide : (s + 1) * wide], weight[:, offset : offset + wide]
            )
    normal, scale = norm_parts(x_ref[...].astype(f32))
    out_ref[...] = grad_after_ref[...] + norm_back(grad_normed, normal, scale, norm_ref[0:1, :])
    sums = jnp.concatenate([sum_slabs(grad_normed * normal), sum_slabs(grad_normed)], axis=0)

    @pl.when(pl.program_id(0) == 0)
    def _():
        sums_ref[...] = sums

    @pl.when(pl.program_id(0) > 0)
    def _():
        sums_ref[...] += sums


def input_gradient(plan, grads, weights, tokens, norms, grad_after):
    count, width = tokens.shape
    tile = pl.BlockSpec((BLOCK, width), lambda i: (i, 0))

    def kernel(*refs):
        n, m = len(grads), len(grads) + len(weights)
        input_grad_kernel(plan, refs[:n], refs[n:m], *refs[m : m + 3], refs[m + 3 :])

    return pl.pallas_call(
        kernel,
        grid=(count // BLOCK,),
        in_specs=[pl.BlockSpec((BLOCK, g.shape[1]), lambda i: (i, 0)) for g in grads]
        + [
            pl.BlockSpec((width, columns), lambda i, block=block: (0, block))
            for _, block, columns in weights
        ]
        + [
            tile,
            pl.BlockSpec(norms.shape, lambda i: (0, 0)),
            tile,
        ],
        out_specs=[tile, pl.BlockSpec((16, width), lambda i: (0, 0))],
        out_shape=[
            jax.ShapeDtypeStruct((count, width), f32),
            jax.ShapeDtypeStruct((16, width), f32),
        ],
        compiler_params=pltpu.CompilerParams(vmem_limit_bytes=48 * 2**20),
        cost_estimate=hint(14),
        name="input_gradient",
    )(*grads, *[array for array, _, _ in weights], tokens, norms, grad_after)


def activations_of(rows, slot_col, gate, after):
    count, width = after.shape
    tile = pl.BlockSpec((BLOCK, width), lambda i: (i, 0))

    def kernel(*refs):
        n = len(rows)
        slot_ref, gate_ref, after_ref, out_ref = refs[n:]
        found = picked_rows(slot_ref, refs[:n])
        out_ref[...] = (after_ref[...] + gate_ref[:, :1] * found).astype(low)

    return pl.pallas_call(
        kernel,
        grid=(count // BLOCK,),
        in_specs=[pl.BlockSpec(r.shape, lambda i: (0, 0)) for r in rows]
        + [
            pl.BlockSpec((BLOCK, 1), lambda i: (i, 0)),
            pl.BlockSpec((BLOCK, LANES), lambda i: (i, 0)),
            tile,
        ],
        out_specs=tile,
        out_shape=jax.ShapeDtypeStruct((count, width), low),
        compiler_params=pltpu.CompilerParams(vmem_limit_bytes=48 * 2**20),
        cost_estimate=hint(7.5),
        name="activations_of",
    )(*rows, slot_col, gate, after)


def gelu_and_slope(x):
    point = 1.0 / (1.0 + (erfc_point * math.sqrt(0.5)) * jnp.abs(x))
    bell = jnp.exp(-0.5 * x * x)
    tail = erfc_terms[-1]
    for term in erfc_terms[-2::-1]:
        tail = tail * point + term
    tail = tail * point * bell
    below = jnp.where(x >= 0.0, 1.0 - tail, tail)
    return x * below, below + x * bell * (1.0 / math.sqrt(2.0 * math.pi))


def row_groups(experts, each):
    group = max(g for g in range(1, experts + 1) if experts % g == 0 and g * each <= BLOCK)
    return group, group * each


def expert_kernel(x_ref, in_ref, *rest):
    hidden_ref, slope_ref = rest[-2:]
    experts, each, width = x_ref.shape
    group, size = row_groups(experts, each)
    for e in range(0, experts, group):
        preact = dot_rows(x_ref[e : e + group].reshape(size, width), in_ref[...])
        value, slope = gelu_and_slope(preact)
        hidden_ref[e : e + group] = value.astype(low).reshape(group, each, -1)
        slope_ref[e : e + group] = slope.astype(low).reshape(group, each, -1)


def expert_forward(arrived, weight_in, chunk, chunks, buffer=None, tile=512):
    experts, each, width = arrived.shape
    inner = weight_in.shape[1]
    return pl.pallas_call(
        expert_kernel,
        grid=(inner // tile,),
        in_specs=[
            pl.BlockSpec((experts, each, width), lambda j: (0, 0, 0)),
            pl.BlockSpec((width, tile), lambda j: (0, j)),
        ]
        + ([] if buffer is None else [pl.BlockSpec(memory_space=pl.ANY)]),
        out_specs=[
            pl.BlockSpec((experts, each, tile), lambda j: (0, chunk, j)),
            pl.BlockSpec((experts, each, tile), lambda j: (0, 0, j)),
        ],
        out_shape=[
            jax.ShapeDtypeStruct((experts, chunks * each, inner), low),
            jax.ShapeDtypeStruct((experts, each, inner), low),
        ],
        input_output_aliases={} if buffer is None else {2: 0},
        compiler_params=pltpu.CompilerParams(vmem_limit_bytes=56 * 2**20),
        cost_estimate=hint(21),
        name="expert_forward",
    )(arrived, weight_in, *([] if buffer is None else [buffer]))


def expert_back_kernel(
    grad_ref, slope_ref, in_ref, out_ref, x_ref, result_ref, centre_ref, *rest
):
    grad_preact_ref, grad_rows_ref, grad_centre_ref, strips, grad_logit_ref = rest[-5:]
    step = pl.program_id(0)
    count, size, tile = strips.shape
    each = grad_ref.shape[1]

    @pl.when(step < count)
    def _():
        grad_hidden = dot_cols(grad_ref[...].reshape(size, -1), out_ref[...])
        grad_preact = (grad_hidden * slope_ref[...].reshape(size, tile).astype(f32)).astype(low)
        strips[step] = grad_preact
        grad_preact_ref[...] = grad_preact.reshape(-1, each, tile)

    @pl.when(step == count)
    def _():
        centre = centre_ref[...].astype(f32)
        grad_centre = jnp.zeros(grad_centre_ref.shape, f32)
        group, rows = row_groups(grad_ref.shape[0], each)
        for e in range(0, grad_ref.shape[0], group):
            x = x_ref[e : e + group].reshape(rows, -1).astype(f32)
            gate = jax.nn.sigmoid(jnp.sum(x * centre, axis=-1, keepdims=True))
            grad = grad_ref[e : e + group].reshape(rows, -1).astype(f32)
            moved = grad * result_ref[e : e + group].reshape(rows, -1).astype(f32)
            grad_logit = jnp.sum(moved, axis=-1, keepdims=True) * (1.0 - gate)
            grad_logit_ref[e * each : e * each + rows, :] = jnp.broadcast_to(
                grad_logit, (rows, LANES)
            )
            grad_centre = grad_centre + sum_slabs(grad_logit * x)
        grad_centre_ref[...] = grad_centre

    @pl.when(step >= count)
    def _():
        columns = grad_rows_ref.shape[2]
        start = pl.multiple_of((step - count) * columns, columns)
        centre = centre_ref[:, pl.ds(start, columns)].astype(f32)
        total = grad_logit_ref[:, :1] * centre
        for k in range(count):
            total = total + dot_cols(strips[k], in_ref[:, k * tile : (k + 1) * tile])
        grad_rows_ref[...] = total.astype(low).reshape(-1, each, columns)


def expert_back(
    grad_arrived,
    slope,
    weight_in,
    weight_out,
    arrived,
    result,
    centre,
    chunk,
    chunks,
    buffer=None,
    tile=1024,
    columns=256,
):
    experts, each, width = grad_arrived.shape
    inner = weight_in.shape[1]
    count = inner // tile
    alone = pl.BlockSpec((experts, each, width), lambda j: (0, 0, 0))

    def strip(j):
        return jnp.minimum(j, count - 1)

    def part(j):
        return jnp.maximum(j - count, 0)

    return pl.pallas_call(
        expert_back_kernel,
        grid=(count + width // columns,),
        in_specs=[
            alone,
            pl.BlockSpec((experts, each, tile), lambda j: (0, 0, strip(j))),
            pl.BlockSpec((columns, inner), lambda j: (part(j), 0)),
            pl.BlockSpec((tile, width), lambda j: (strip(j), 0)),
            alone,
            pl.BlockSpec((experts, each, width), lambda j: (0, chunk, 0)),
            pl.BlockSpec((1, width), lambda j: (0, 0)),
        ]
        + ([] if buffer is None else [pl.BlockSpec(memory_space=pl.ANY)]),
        out_specs=[
            pl.BlockSpec((experts, each, tile), lambda j: (0, chunk, strip(j))),
            pl.BlockSpec((experts, each, columns), lambda j: (0, 0, part(j))),
            pl.BlockSpec((8, width), lambda j: (0, 0)),
        ],
        out_shape=[
            jax.ShapeDtypeStruct((experts, chunks * each, inner), low),
            jax.ShapeDtypeStruct((experts, each, width), low),
            jax.ShapeDtypeStruct((8, width), f32),
        ],
        scratch_shapes=[
            pltpu.VMEM((count, experts * each, tile), low),
            pltpu.VMEM((experts * each, LANES), f32),
        ],
        input_output_aliases={} if buffer is None else {7: 0},
        compiler_params=pltpu.CompilerParams(vmem_limit_bytes=58 * 2**20),
        cost_estimate=hint(23),
        name="expert_back",
    )(
        grad_arrived,
        slope,
        weight_in,
        weight_out,
        arrived,
        result,
        centre,
        *([] if buffer is None else [buffer]),
    )


def weight_grads_kernel(chunks, refs):
    x_refs, grad_refs = refs[:chunks], refs[chunks : 2 * chunks]
    grad_preact_ref, hidden_ref, in_out_ref, out_out_ref, turned = refs[2 * chunks :]
    step = pl.program_id(0)
    half = pl.num_programs(0) // 2

    def turn_rows(chunk_refs):
        for c, ref in enumerate(chunk_refs):
            experts, each, width = ref.shape
            group, size = row_groups(experts, each)
            for e in range(0, experts, group):
                turned[c, :, e * each : e * each + size] = (
                    ref[e : e + group].reshape(size, width).T
                )

    pl.when(step == 0)(lambda: turn_rows(x_refs))
    pl.when(step == half)(lambda: turn_rows(grad_refs))

    def multiply(ref, out_ref):
        experts, slots, tile = ref.shape
        each = slots // chunks
        right = [
            ref[:, c * each : (c + 1) * each, :].reshape(experts * each, tile)
            for c in range(chunks)
        ]
        for row in range(0, turned.shape[1], BLOCK):
            rows = slice(row, row + BLOCK)
            total = dot_rows(turned[0, rows, :], right[0])
            for c in range(1, chunks):
                total = total + dot_rows(turned[c, rows, :], right[c])
            out_ref[rows, :] = total.astype(low)

    pl.when(step < half)(lambda: multiply(grad_preact_ref, in_out_ref))
    pl.when(step >= half)(lambda: multiply(hidden_ref, out_out_ref))


def weight_grads(arrived, grad_arrived, grad_preact, hidden, tile=1024):
    chunks = len(arrived)
    experts, each, width = arrived[0].shape
    slots, inner = hidden.shape[1:]
    half = inner // tile
    whole = pl.BlockSpec((experts, each, width), lambda j: (0, 0, 0))

    def first(j):
        return jnp.minimum(j, half - 1)

    def second(j):
        return jnp.maximum(j - half, 0)

    return pl.pallas_call(
        lambda *refs: weight_grads_kernel(chunks, refs),
        grid=(2 * half,),
        in_specs=[whole] * (2 * chunks)
        + [
            pl.BlockSpec((experts, slots, tile), lambda j: (0, 0, first(j))),
            pl.BlockSpec((experts, slots, tile), lambda j: (0, 0, second(j))),
        ],
        out_specs=[
            pl.BlockSpec((width, tile), lambda j: (0, first(j))),
            pl.BlockSpec((width, tile), lambda j: (0, second(j))),
        ],
        out_shape=[jax.ShapeDtypeStruct((width, inner), low)] * 2,
        scratch_shapes=[pltpu.VMEM((chunks, width, experts * each), low)],
        compiler_params=pltpu.CompilerParams(vmem_limit_bytes=58 * 2**20),
        cost_estimate=hint(38),
        name="weight_grads",
    )(*arrived, *grad_arrived, grad_preact, hidden)


def update(weight, moment, average, gradient, factor, rate):
    clipped = gradient * factor
    moment_new = momentum_rate * moment + clipped
    weight_new = weight - rate * (clipped + momentum_rate * moment_new)
    average_new = average_rate * average + (1.0 - average_rate) * weight_new
    return (weight_new, moment_new, average_new)


def step_kernel(factor_ref, *refs):
    inputs, outputs = refs[:8], refs[8:]
    factor = factor_ref[0]
    for which in range(2):
        weight, moment, average, gradient = inputs[4 * which : 4 * which + 4]
        gradient = gradient[...] if which == 0 else gradient[...].T
        stepped = update(
            weight[0], moment[0], average[0], gradient.astype(f32), factor, learn_rate
        )
        for out, value in zip(outputs[3 * which : 3 * which + 3], stepped):
            out[0] = value


def step_experts(factor, first, second, tile=1024):
    rows, columns = first[0].shape[1:]
    along = pl.BlockSpec((1, rows, tile), lambda j: (0, 0, j))
    down = pl.BlockSpec((1, tile, rows), lambda j: (0, j, 0))
    gradient = pl.BlockSpec((rows, tile), lambda j: (0, j))
    return pl.pallas_call(
        step_kernel,
        grid=(columns // tile,),
        in_specs=[pl.BlockSpec(memory_space=pltpu.SMEM)]
        + [along] * 3
        + [gradient]
        + [down] * 3
        + [gradient],
        out_specs=[along] * 3 + [down] * 3,
        out_shape=[jax.ShapeDtypeStruct(first[0].shape, f32)] * 3
        + [jax.ShapeDtypeStruct(second[0].shape, f32)] * 3,
        compiler_params=pltpu.CompilerParams(vmem_limit_bytes=48 * 2**20),
        cost_estimate=hint(20),
        name="step_experts",
    )(factor.reshape(1), *first, *second)


def swap(values, axis, distance):
    size = lax.axis_size(axis)
    return lax.ppermute(values, axis, [(i, i ^ distance) for i in range(size)])


def assemble_kernel(me_ref, *refs):
    pieces, out_ref = refs[:-1], refs[-1]
    experts, rows = pieces[0].shape[0], pieces[0].shape[1]
    for t, piece in enumerate(pieces):
        for e in range(experts):
            owner = e * len(pieces) + (me_ref[0] ^ t)
            out_ref[pl.ds(pl.multiple_of(owner * rows, rows), rows), :] = piece[e]


def assemble(pieces):
    experts, rows, columns = pieces[0].shape
    dp = len(pieces)
    return pl.pallas_call(
        assemble_kernel,
        in_specs=[pl.BlockSpec(memory_space=pltpu.SMEM)]
        + [pl.BlockSpec(memory_space=pltpu.VMEM)] * dp,
        out_specs=pl.BlockSpec(memory_space=pltpu.VMEM),
        out_shape=jax.ShapeDtypeStruct((experts * dp * rows, columns), pieces[0].dtype),
        compiler_params=pltpu.CompilerParams(vmem_limit_bytes=32 * 2**20),
        cost_estimate=hint(4),
        name="assemble",
    )(lax.axis_index("dp").astype(jnp.int32).reshape(1), *pieces)


def sum_halves(parts, axis, bit, at):
    own = (lax.axis_index(axis) // bit) % 2

    def side(which):
        picked = []
        for part in parts:
            shape = part.shape
            halves = part.reshape(shape[:at] + (shape[at] // 2, 2) + shape[at + 1 :])
            picked.append(lax.dynamic_index_in_dim(halves, which, at + 1, keepdims=False))
        return jnp.concatenate(picked, axis=-1)

    return (side(own).astype(f32) + swap(side(1 - own), axis, bit).astype(f32)).astype(low)


def sum_over_cores(parts):
    return sum_halves(parts, "dp", 1, 1)


def sum_over_neighbours(held):
    return sum_halves([held], "expert", 1, 0)


def sum_over_pairs(held, partners, keep, *beside):
    experts, dp = lax.axis_size("expert"), lax.axis_size("dp")
    total = lax.dynamic_index_in_dim(held, keep, 0, keepdims=False).astype(f32)
    received = []
    for offset, (far, near) in enumerate(partners, 1):
        block = lax.dynamic_index_in_dim(held, jnp.bitwise_xor(keep, offset), 0, keepdims=False)
        perm = [
            (e * dp + d, (e ^ far) * dp + (d ^ near)) for e in range(experts) for d in range(dp)
        ]
        received.append(lax.ppermute(block, everywhere, perm))
    if beside:
        moved = in_order(*received, *beside)
        received, beside = moved[: len(received)], moved[len(received) :]
    for block in received:
        total = total + block.astype(f32)
    return (total, *beside) if beside else total


def sum_near(held):
    near = held.shape[1]
    held = held.reshape((held.shape[0] // 2, 2 * near) + held.shape[2:]).swapaxes(0, 1)
    partners = [(i // near, i % near * 2) for i in range(1, 2 * near)]
    keep = lax.axis_index("expert") % 2 * near + lax.axis_index("dp") // 2
    return sum_over_pairs(held, partners, keep).astype(low)


def sum_far(held, *beside):
    partners = [(2 * i, 0) for i in range(1, held.shape[0])]
    return sum_over_pairs(held, partners, lax.axis_index("expert") // 2, *beside)


def sum_across(held):
    partners = [(0, 2 * i) for i in range(1, held.shape[0])]
    return sum_over_pairs(held, partners, lax.axis_index("dp") // 2)


def in_order(*values):
    return lax.optimization_barrier(values)


def sum_everywhere(value):
    held = value.reshape(1, 1)
    for axis in ("dp", "expert"):
        distance = 1
        while distance < lax.axis_size(axis):
            held = held + swap(held, axis, distance)
            distance *= 2
    return held[0, 0]


def shards(
    tokens,
    documents,
    routes,
    out_grad,
    norm_params,
    qkv_weight,
    proj_weight,
    centroids,
    expert_in,
    expert_out,
    norm_moment,
    qkv_moment,
    proj_moment,
    centroid_moment,
    in_moment,
    out_moment,
    norm_average,
    qkv_average,
    proj_average,
    centroid_average,
    in_average,
    out_average,
):
    local_tokens, width = tokens.shape
    experts = lax.axis_size("expert")
    dp = lax.axis_size("dp")
    devices = experts * dp
    slot_cap = max(2, 3 * local_tokens // (2 * experts))
    slots = experts * slot_cap
    chunks = 2 if slot_cap % 32 == 0 else 1
    half_cap = slot_cap // chunks
    rows_own = qkv_weight.shape[0]
    norm_own = norm_params.shape[1]
    centre_own = centroids.shape[1]
    groups = 4

    strips = 2
    strip = width // strips
    small = jnp.concatenate([norm_params.reshape(-1), centroids.reshape(-1)]).astype(low)
    small = jnp.pad(small, (0, rows_own * LANES - small.shape[0])).reshape(rows_own, LANES)
    qkv_low = qkv_weight.astype(low)
    qkv_own = [
        [qkv_low[:, s * width + h * strip : s * width + (h + 1) * strip] for s in range(3)]
        for h in range(strips)
    ]
    front = jnp.concatenate([*qkv_own[0], small], axis=1)
    later = jnp.concatenate([proj_weight.astype(low), *qkv_own[1]], axis=1)
    later = lax.all_gather(later, everywhere, axis=0, tiled=True)
    in_low, out_low = expert_in.astype(low), expert_out.astype(low)

    route_ids = routes[:, 0]
    onehot = route_ids[:, None] == jnp.arange(experts, dtype=jnp.int32)[None, :]
    running = jnp.cumsum(onehot.astype(jnp.int32), axis=0)
    within = jnp.sum(running * onehot.astype(jnp.int32), axis=1) - 1
    slot_index = route_ids * slot_cap + within
    chunked = (within // half_cap * experts + route_ids) * half_cap + within % half_cap
    slot_row, slot_col = slot_index[None, :], slot_index[:, None]
    chunked_row, chunked_col = chunked[None, :], chunked[:, None]
    doc_col = documents[:, None]
    doc_row = documents[None, :]

    normal_one, _ = norm_parts(tokens.astype(f32))
    if rows_own % 16:
        front = lax.all_gather(front, everywhere, axis=0, tiled=True)
    else:
        spread = jnp.broadcast_to(front[None], (experts,) + front.shape)
        spread = lax.all_to_all(spread, "expert", split_axis=0, concat_axis=0, tiled=True)
        spread, normal_one, in_low, out_low, slot_row, slot_col, chunked_row, chunked_col = in_order(
            spread, normal_one, in_low, out_low, slot_row, slot_col, chunked_row, chunked_col
        )
        pieces = {0: spread}
        distance = dp // 2
        while distance:
            for t in list(pieces):
                pieces[t | distance] = swap(pieces[t], "dp", distance)
            distance //= 2
        front = assemble([pieces[t] for t in range(dp)])
    weight_in = lax.all_gather(in_low, "dp", axis=1, tiled=True)[0]
    weight_out = lax.all_gather(out_low, "dp", axis=2, tiled=True)[0]
    small_full = front[:, 3 * strip :].reshape(devices, rows_own * LANES)
    norms = (
        small_full[:, : 4 * norm_own].reshape(devices, 4, norm_own).transpose(1, 0, 2)
    ).reshape(4, width).astype(f32)
    centre_table = small_full[:, 4 * norm_own : 4 * norm_own + centre_own].reshape(experts, width)

    normed_low = (normal_one * norms[0] + norms[1]).astype(low)
    normed_low, front = in_order(normed_low, front)
    packed, mixed, lse = [], [], []
    for weight in (front[:, : 3 * strip], later[:, width:]):
        packed_h = jnp.dot(normed_low, weight, preferred_element_type=f32).astype(low)
        mixed_h, lse_h = attend(packed_h, doc_col, doc_row)
        packed.append(packed_h)
        mixed.append(mixed_h)
        lse.append(lse_h)
    after, grad_rows, gate, *outgoing = after_attend(
        mixed,
        later,
        tokens,
        out_grad,
        norms,
        centre_table,
        routes,
        chunked_row,
        [slots // chunks] * chunks,
    )

    def exchange(rows):
        rows = rows.reshape(experts, -1, width)
        return lax.all_to_all(rows, "expert", split_axis=0, concat_axis=0, tiled=True)

    grad_outgoing = []
    for c in range(chunks):
        own = jnp.arange(slots // chunks, dtype=jnp.int32)[:, None] + c * (slots // chunks)
        place = (own == chunked_row).astype(low)
        grad_outgoing.append(jnp.dot(place, grad_rows, preferred_element_type=f32).astype(low))
    arrived, slope, hidden = [], [], None
    for c in range(chunks):
        if c:
            arrived[c - 1], outgoing[c], *grad_outgoing = in_order(
                arrived[c - 1], outgoing[c], *grad_outgoing
            )
        arrived.append(exchange(outgoing[c]))
    for c in range(chunks):
        if c == chunks - 1:
            arrived[c], grad_outgoing[0] = in_order(arrived[c], grad_outgoing[0])
        hidden, slope_c = expert_forward(arrived[c], weight_in, c, chunks, hidden)
        slope.append(slope_c)
        if c == 0 and chunks > 1:
            hidden, grad_outgoing[0] = in_order(hidden, grad_outgoing[0])
    grad_arrived = [exchange(grad_outgoing[0])]
    hidden = hidden.reshape(slots, -1)
    result = jnp.dot(hidden, weight_out, preferred_element_type=f32).astype(low)
    result = result.reshape(experts, slot_cap, width)
    for c in range(1, chunks):
        grad_arrived[c - 1], grad_outgoing[c], result = in_order(
            grad_arrived[c - 1], grad_outgoing[c], result
        )
        grad_arrived.append(exchange(grad_outgoing[c]))
    centre_row = lax.dynamic_slice_in_dim(centre_table, lax.axis_index("expert"), 1, 0)
    grad_preact = None
    grad_input, grad_centre = [], 0.0
    for c in range(chunks):
        last = c == chunks - 1
        grad_preact, rows_c, centre_c = expert_back(
            grad_arrived[c],
            slope[c],
            weight_in,
            weight_out,
            arrived[c],
            result,
            centre_row,
            c,
            chunks,
            grad_preact,
        )
        if not last:
            rows_c, grad_arrived[c + 1] = in_order(rows_c, grad_arrived[c + 1])
        elif grad_input:
            rows_c, grad_input[-1] = in_order(rows_c, grad_input[-1])
        grad_input.append(exchange(rows_c).reshape(slots // chunks, width))
        grad_centre = grad_centre + jnp.sum(centre_c, axis=0)
    if chunks > 1:
        hidden, arrived[0], grad_input[0] = in_order(hidden, arrived[0], grad_input[0])
    grad_in, grad_out_turned = weight_grads(
        arrived, grad_arrived, grad_preact, hidden.reshape(experts, slot_cap, -1)
    )
    result, grad_input[-1], grad_in, grad_out_turned = in_order(
        result, grad_input[-1], grad_in, grad_out_turned
    )
    in_grad = lax.psum_scatter(grad_in[None], "dp", scatter_dimension=1, tiled=True)
    out_turned = lax.psum_scatter(grad_out_turned[None], "dp", scatter_dimension=1, tiled=True)
    returned = exchange(result).reshape(slots, width)

    grad_after, grad_low, grad_mixed, sums_two = before_attend_back(
        grad_input, chunked_col, after, out_grad, norms, later
    )

    grad_proj = jnp.concatenate(
        [
            lax.dot_general(m, grad_low, (((0,), (0,)), ((), ())), preferred_element_type=f32)
            for m in mixed
        ],
        axis=0,
    ).astype(low)
    norm_two = jnp.sum(sums_two.reshape(2, 8, width), axis=1)
    norm_two = norm_two.reshape(2, devices, norm_own).transpose(1, 0, 2).reshape(devices, -1)
    mine = jnp.arange(experts)[:, None, None] == lax.axis_index("expert")
    centre_flat = jnp.where(mine, grad_centre.reshape(1, dp, centre_own), 0.0)
    extra = jnp.concatenate([norm_two, centre_flat.reshape(devices, centre_own)], axis=1)
    extra = jnp.pad(extra, ((0, 0), (0, rows_own * LANES - extra.shape[1]))).astype(low)
    extra = extra.reshape(devices * rows_own, LANES)
    each = width // LANES // groups
    wide = each * LANES

    def by_owner(values):
        return values.reshape(experts, dp, rows_own, values.shape[1])

    def back_group(g, *beside):
        h, k = g // (groups // strips), g % (groups // strips)
        part = attend_back(
            packed[h], grad_mixed, mixed[h], lse[h], doc_col, doc_row, k * each, each, g * each
        )
        part, *beside = in_order(part, *beside)
        grad = lax.dot_general(
            normed_low, part, (((0,), (0,)), ((), ())), preferred_element_type=f32
        )
        return part, grad.astype(low), *beside

    parts, grads = [], []
    rest = by_owner(jnp.concatenate([grad_proj, extra], axis=1))
    for g in range(groups):
        if g == 1:
            rest = sum_over_cores([rest])
            rest, grad_mixed = in_order(rest, grad_mixed)
        if g == groups - 1:
            rest = sum_over_neighbours(rest)
            first = sum_over_cores([by_owner(v) for v in grads[: groups // 2]])
            rest, first, grad_mixed, returned = in_order(rest, first, grad_mixed, returned)
            first = sum_over_neighbours(first)
            part, grad, first = back_group(g, first)
        else:
            part, grad = back_group(g)
        grad, grad_mixed = in_order(grad, grad_mixed)
        parts.append(part)
        grads.append(grad)
    second = sum_over_cores([by_owner(v) for v in grads[groups // 2 :]])
    second, first, grad_after = in_order(second, first, grad_after)
    second = sum_near(second)
    first = sum_far(jnp.concatenate([rest, first], axis=-1)).astype(low)
    per_strip = groups // strips
    weights = [(front, s, strip) for s in range(3)]
    weights += [(later, width // strip + s, strip) for s in range(3)]
    input_grad, sums_one = input_gradient(
        [(g // per_strip, g % per_strip * wide, wide) for g in range(groups)],
        parts,
        weights,
        tokens,
        norms,
        grad_after,
    )
    first, second, sums_one, gate = in_order(first, second, sums_one, gate)
    norm_one = jnp.sum(sums_one.reshape(2, 8, width), axis=1)
    norm_one = norm_one.reshape(2, devices, norm_own).transpose(1, 0, 2).reshape(devices, -1)
    norm_one = lax.all_to_all(norm_one, everywhere, split_axis=0, concat_axis=0, tiled=True)
    norm_one, in_grad, out_turned = in_order(norm_one, in_grad, out_turned)
    in_square = jnp.sum(jnp.square(in_grad.astype(f32)))
    out_square = jnp.sum(jnp.square(out_turned.astype(f32)))
    activations = activations_of([returned], slot_col, gate, after)
    norm_one = jnp.sum(norm_one, axis=0).reshape(2, norm_own)
    second, activations, in_square, out_square = sum_far(
        second, activations, in_square, out_square
    )
    first = sum_across(first)
    first, second, in_square, out_square, norm_one, activations = in_order(
        first, second, in_square, out_square, norm_one, activations
    )

    proj_grad = first[:, :width]
    extra = first[:, width : width + LANES].reshape(-1)
    norm_grad = jnp.concatenate([norm_one, extra[: 2 * norm_own].reshape(2, norm_own)], axis=0)
    centre_grad = extra[2 * norm_own : 2 * norm_own + centre_own].reshape(centroids.shape)
    owned = jnp.concatenate([first[:, width + LANES :], second], axis=1)
    qkv_grad = owned.reshape(rows_own, groups, 3, wide).swapaxes(1, 2).reshape(rows_own, 3 * width)
    square_sum = (
        jnp.sum(owned * owned)
        + jnp.sum(proj_grad * proj_grad)
        + jnp.sum(norm_grad * norm_grad)
        + jnp.sum(centre_grad * centre_grad)
        + in_square
        + out_square
    )
    grad_norm = jnp.sqrt(sum_everywhere(square_sum))
    factor = clip_limit / jnp.maximum(grad_norm, clip_limit)
    norm_new = update(norm_params, norm_moment, norm_average, norm_grad, factor, norm_rate)
    qkv_new = update(qkv_weight, qkv_moment, qkv_average, qkv_grad, factor, learn_rate)
    proj_new = update(proj_weight, proj_moment, proj_average, proj_grad, factor, learn_rate)
    centre_new = update(
        centroids, centroid_moment, centroid_average, centre_grad, factor, learn_rate
    )
    stepped = step_experts(
        factor,
        (expert_in, in_moment, in_average, in_grad[0]),
        (expert_out, out_moment, out_average, out_turned[0]),
    )
    in_new, out_new = stepped[:3], stepped[3:]
    return (
        activations,
        input_grad,
        grad_norm,
        norm_new[0],
        qkv_new[0],
        proj_new[0],
        centre_new[0],
        in_new[0],
        out_new[0],
        norm_new[1],
        qkv_new[1],
        proj_new[1],
        centre_new[1],
        in_new[1],
        out_new[1],
        norm_new[2],
        qkv_new[2],
        proj_new[2],
        centre_new[2],
        in_new[2],
        out_new[2],
    )


def solution(mesh):
    placed = (
        P(("expert", "dp"), None),
        P(("expert", "dp")),
        P(("expert", "dp"), None),
        P(("expert", "dp"), None),
        P(None, ("expert", "dp")),
        P(("expert", "dp"), None),
        P(("expert", "dp"), None),
        P("expert", "dp"),
        P("expert", "dp", None),
        P("expert", None, "dp"),
        P(None, ("expert", "dp")),
        P(("expert", "dp"), None),
        P(("expert", "dp"), None),
        P("expert", "dp"),
        P("expert", "dp", None),
        P("expert", None, "dp"),
        P(None, ("expert", "dp")),
        P(("expert", "dp"), None),
        P(("expert", "dp"), None),
        P("expert", "dp"),
        P("expert", "dp", None),
        P("expert", None, "dp"),
    )
    return jax.shard_map(
        shards,
        mesh=mesh,
        in_specs=placed,
        out_specs=(
            P(("expert", "dp"), None),
            P(("expert", "dp"), None),
            P(),
            P(None, ("expert", "dp")),
            P(("expert", "dp"), None),
            P(("expert", "dp"), None),
            P("expert", "dp"),
            P("expert", "dp", None),
            P("expert", None, "dp"),
            P(None, ("expert", "dp")),
            P(("expert", "dp"), None),
            P(("expert", "dp"), None),
            P("expert", "dp"),
            P("expert", "dp", None),
            P("expert", None, "dp"),
            P(None, ("expert", "dp")),
            P(("expert", "dp"), None),
            P(("expert", "dp"), None),
            P("expert", "dp"),
            P("expert", "dp", None),
            P("expert", None, "dp"),
        ),
        check_vma=False,
    )
```

```python
import functools
import math

import jax
import jax.numpy as jnp
from jax import lax
from jax.experimental import pallas as pl
from jax.experimental.pallas import tpu as pltpu
from jax.sharding import PartitionSpec as P

HEAD_DIM = 64
SEQ = 1024
LANES = 128
BLOCK = 256

eps = 1e-05
scale_qk = 0.125
momentum_rate = 0.9
learn_rate = 100.0
norm_rate = 500.0
average_rate = 0.9
clip_limit = 1.0
masked_score = -1000000000.0
everywhere = ("expert", "dp")
low = jnp.bfloat16
f32 = jnp.float32

erfc_point = 0.4
erfc_terms = (
    0.11596270714310389,
    0.08090178846816841,
    0.2341610172367065,
    -0.1854824771652721,
    0.35459055762612957,
    -0.10013360714943426,
)


def hint(microseconds):
    return pl.CostEstimate(
        flops=int(microseconds * 1.9e8), bytes_accessed=0, transcendentals=0
    )


def dot_rows(left, right):
    return lax.dot_general(left, right, (((1,), (0,)), ((), ())), preferred_element_type=f32)


def dot_cols(left, right):
    return lax.dot_general(left, right, (((1,), (1,)), ((), ())), preferred_element_type=f32)


def fill_bias(bias, doc_of_rows, doc_of_cols, rows_are_keys):
    for block in range(0, SEQ, BLOCK):
        rows = lax.broadcasted_iota(jnp.int32, (BLOCK, SEQ), 0) + block
        cols = lax.broadcasted_iota(jnp.int32, (BLOCK, SEQ), 1)
        causal = (rows <= cols) if rows_are_keys else (rows >= cols)
        same = doc_of_rows[block : block + BLOCK, :] == doc_of_cols[...]
        bias[block : block + BLOCK, :] = jnp.where(same & causal, 3.0e38, masked_score)


def in_head(shape, head, axis):
    return lax.broadcasted_iota(jnp.int32, shape, axis) // HEAD_DIM == head


def keep_head(values, head):
    return jnp.where(in_head(values.shape, head, 1), values, jnp.zeros_like(values))


def attend_kernel(q_ref, k_ref, v_ref, doc_col, doc_row, mixed_ref, lse_ref, bias):
    @pl.when(pl.program_id(1) == 0)
    def _():
        fill_bias(bias, doc_col, doc_row, False)

    def scores_of(block):
        seen = block + BLOCK
        query = q_ref[block:seen, :] * jnp.asarray(scale_qk, low)
        return [dot_cols(keep_head(query, head), k_ref[:seen, :]) for head in range(2)]

    following = scores_of(0)
    for block in range(0, SEQ, BLOCK):
        seen = block + BLOCK
        current = following
        if seen < SEQ:
            following = scores_of(seen)
        weights, outs, stats = [], [], []
        for head in range(2):
            scores = jnp.minimum(current[head], bias[block:seen, :seen])
            top = jnp.max(scores, axis=-1, keepdims=True)
            exponent = jnp.exp(scores - top)
            total = jnp.sum(exponent, axis=-1, keepdims=True)
            weights.append((exponent.astype(low), total))
            stats.append(top + jnp.log(total))
        for exponent, total in weights:
            outs.append(dot_rows(exponent, v_ref[:seen, :]) / total)
        first = in_head((BLOCK, LANES), 0, 1)
        mixed_ref[block:seen, :] = jnp.where(first, outs[0], outs[1]).astype(low)
        lane = lax.broadcasted_iota(jnp.int32, (BLOCK, LANES), 1)
        both = jnp.where(lane == 0, stats[0], stats[1])
        lse_ref[:, block:seen] = both.T[:8, :]


def attend(packed, doc_col, doc_row):
    count, wide = packed.shape
    width = wide // 3
    pairs = width // LANES

    def part(which):
        return pl.BlockSpec((SEQ, LANES), lambda r, p, w=which: (r, w * pairs + p))

    return pl.pallas_call(
        attend_kernel,
        grid=(count // SEQ, pairs),
        in_specs=[
            part(0),
            part(1),
            part(2),
            pl.BlockSpec((SEQ, 1), lambda r, p: (r, 0)),
            pl.BlockSpec((1, SEQ), lambda r, p: (0, r)),
        ],
        out_specs=[
            pl.BlockSpec((SEQ, LANES), lambda r, p: (r, p)),
            pl.BlockSpec((8, SEQ), lambda r, p: (p, r)),
        ],
        out_shape=[
            jax.ShapeDtypeStruct((count, width), low),
            jax.ShapeDtypeStruct((8 * pairs, count), f32),
        ],
        scratch_shapes=[pltpu.VMEM((SEQ, SEQ), f32)],
        compiler_params=pltpu.CompilerParams(vmem_limit_bytes=48 * 2**20),
        cost_estimate=hint(29),
        name="attend",
    )(packed, packed, packed, doc_col, doc_row)


def attend_back_kernel(
    q_ref, k_ref, v_ref, grad_ref, mixed_ref, lse_ref, doc_col, doc_row, out_ref, bias, grad_q_t
):
    pair = pl.program_id(1)

    @pl.when(pair == 0)
    def _():
        fill_bias(bias, doc_col, doc_row, True)

    wide = out_ref.shape[1] // 3
    place = [pl.ds(pl.multiple_of(s * wide + pair * LANES, LANES), LANES) for s in range(3)]
    query = q_ref[...] * jnp.asarray(scale_qk, low)
    grad = grad_ref[...]
    product = grad.astype(f32) * mixed_ref[...].astype(f32)
    upper = product.astype(low)
    lower = (product - upper.astype(f32)).astype(low)
    chooser = (
        lax.broadcasted_iota(jnp.int32, (8, LANES), 0)
        == lax.broadcasted_iota(jnp.int32, (8, LANES), 1) // HEAD_DIM
    ).astype(low)
    inner = dot_cols(chooser, upper) + dot_cols(chooser, lower)
    key_t = k_ref[...].T
    def products(block):
        after = block + BLOCK
        return [
            (
                dot_cols(keep_head(k_ref[block:after, :], head), query[block:, :]),
                dot_cols(keep_head(v_ref[block:after, :], head), grad[block:, :]),
            )
            for head in range(2)
        ]

    following = products(0)
    for block in range(0, SEQ, BLOCK):
        after = block + BLOCK
        current = following
        if after < SEQ:
            following = products(after)
        factors = []
        for head in range(2):
            scores, grad_w = current[head]
            scores = jnp.minimum(scores, bias[block:after, block:])
            weights = jnp.exp(scores - lse_ref[head : head + 1, block:])
            grad_s = (weights * (grad_w - inner[head : head + 1, block:])).astype(low)
            factors.append((weights.astype(low), grad_s))
        grad_k, grad_v = [], []
        for head in range(2):
            weights, grad_s = factors[head]
            grad_v.append(dot_rows(weights, grad[block:, :]))
            grad_k.append(dot_rows(grad_s, query[block:, :]))
            rows = slice(head * HEAD_DIM, (head + 1) * HEAD_DIM)
            moved = dot_rows(key_t[rows, block:after], grad_s)
            if block == 0:
                grad_q_t[rows, :] = moved
            else:
                grad_q_t[rows, block:] += moved
        first = in_head((BLOCK, LANES), 0, 1)
        out_ref[block:after, place[1]] = jnp.where(first, grad_k[0], grad_k[1]).astype(low)
        out_ref[block:after, place[2]] = jnp.where(first, grad_v[0], grad_v[1]).astype(low)
    out_ref[:, place[0]] = (grad_q_t[...] * scale_qk).T.astype(low)


def attend_back(packed, grad_mixed, mixed, lse, doc_col, doc_row, first, count, grad_first):
    tokens, wide = packed.shape
    pairs = wide // 3 // LANES

    def part(which):
        return pl.BlockSpec((SEQ, LANES), lambda r, p, w=which: (r, w * pairs + first + p))

    return pl.pallas_call(
        attend_back_kernel,
        grid=(tokens // SEQ, count),
        in_specs=[
            part(0),
            part(1),
            part(2),
            pl.BlockSpec((SEQ, LANES), lambda r, p: (r, grad_first + p)),
            pl.BlockSpec((SEQ, LANES), lambda r, p: (r, first + p)),
            pl.BlockSpec((8, SEQ), lambda r, p: (first + p, r)),
            pl.BlockSpec((SEQ, 1), lambda r, p: (r, 0)),
            pl.BlockSpec((1, SEQ), lambda r, p: (0, r)),
        ],
        out_specs=pl.BlockSpec((SEQ, 3 * count * LANES), lambda r, p: (r, 0)),
        out_shape=jax.ShapeDtypeStruct((tokens, 3 * count * LANES), low),
        scratch_shapes=[pltpu.VMEM((SEQ, SEQ), f32), pltpu.VMEM((LANES, SEQ), f32)],
        compiler_params=pltpu.CompilerParams(vmem_limit_bytes=48 * 2**20),
        cost_estimate=hint(4.8 * count),
        name="attend_back",
    )(packed, packed, packed, grad_mixed, mixed, lse, doc_col, doc_row)


def norm_parts(values):
    centre = values - jnp.mean(values, axis=-1, keepdims=True)
    spread = jnp.mean(centre * centre, axis=-1, keepdims=True)
    scale = lax.rsqrt(spread + eps)
    return centre * scale, scale


def norm_back(grad, normal, scale, gain):
    moved = grad * gain
    return scale * (
        moved
        - jnp.mean(moved, axis=-1, keepdims=True)
        - normal * jnp.mean(moved * normal, axis=-1, keepdims=True)
    )


def sum_slabs(values):
    return jnp.sum(values.reshape(-1, 8, values.shape[1]), axis=0)


def after_attend_kernel(
    mixed_refs, proj_ref, x_ref, grad_ref, norm_ref, centre_ref, route_ref, slot_ref, outs, sent
):
    after_ref, grad_rows_ref, gate_ref, out_refs = outs[0], outs[1], outs[2], outs[3:]
    step = pl.program_id(0)
    attended = 0.0
    depth = 0
    for mixed in mixed_refs:
        wide = mixed.shape[1]
        attended = attended + dot_rows(mixed[...], proj_ref[depth : depth + wide, :])
        depth += wide
    after = x_ref[...].astype(f32) + attended
    after_ref[...] = after
    normal, _ = norm_parts(after)
    sent_low = (normal * norm_ref[2:3, :] + norm_ref[3:4, :]).astype(low)
    sent[pl.ds(pl.multiple_of(step * BLOCK, BLOCK), BLOCK), :] = sent_low
    experts = centre_ref.shape[0]
    onehot = route_ref[...] == lax.broadcasted_iota(jnp.int32, (BLOCK, experts), 1)
    picked = dot_rows(onehot.astype(low), centre_ref[...])
    gate = jax.nn.sigmoid(jnp.sum(sent_low.astype(f32) * picked, axis=-1, keepdims=True))
    grad_rows_ref[...] = (gate * grad_ref[...].astype(f32)).astype(low)
    gate_ref[...] = jnp.broadcast_to(gate, gate_ref.shape)

    @pl.when(step == pl.num_programs(0) - 1)
    def _():
        base = 0
        for out_ref in out_refs:
            for row in range(0, out_ref.shape[0], BLOCK):
                slots = lax.broadcasted_iota(jnp.int32, (BLOCK, sent.shape[0]), 0) + base
                place = (slots == slot_ref[...]).astype(low)
                out_ref[row : row + BLOCK, :] = dot_rows(place, sent[...]).astype(low)
                base += BLOCK


def after_attend(mixed, proj, tokens, out_grad, norms, centres, routes, slot_row, chunk_rows):
    count, width = tokens.shape
    chunks = len(chunk_rows)
    tile = pl.BlockSpec((BLOCK, width), lambda i: (i, 0))

    def kernel(*refs):
        n = len(mixed)
        after_attend_kernel(refs[:n], *refs[n : n + 7], refs[n + 7 : -1], refs[-1])

    return pl.pallas_call(
        kernel,
        grid=(count // BLOCK,),
        in_specs=[pl.BlockSpec((BLOCK, m.shape[1]), lambda i: (i, 0)) for m in mixed]
        + [
            pl.BlockSpec((width, width), lambda i: (0, 0)),
            tile,
            tile,
            pl.BlockSpec(norms.shape, lambda i: (0, 0)),
            pl.BlockSpec(centres.shape, lambda i: (0, 0)),
            pl.BlockSpec((BLOCK, 1), lambda i: (i, 0)),
            pl.BlockSpec((1, count), lambda i: (0, 0)),
        ],
        out_specs=[tile, tile, pl.BlockSpec((BLOCK, LANES), lambda i: (i, 0))]
        + [pl.BlockSpec((rows, width), lambda i: (0, 0)) for rows in chunk_rows],
        out_shape=[
            jax.ShapeDtypeStruct((count, width), f32),
            jax.ShapeDtypeStruct((count, width), low),
            jax.ShapeDtypeStruct((count, LANES), f32),
        ]
        + [jax.ShapeDtypeStruct((rows, width), low) for rows in chunk_rows],
        scratch_shapes=[pltpu.VMEM((count, width), low)],
        compiler_params=pltpu.CompilerParams(vmem_limit_bytes=48 * 2**20),
        cost_estimate=hint(13),
        name="after_attend",
    )(*mixed, proj, tokens, out_grad, norms, centres, routes, slot_row)


def picked_rows(slot_ref, row_refs):
    base, total = 0, 0.0
    for rows in row_refs:
        slots = lax.broadcasted_iota(jnp.int32, (BLOCK, rows.shape[0]), 1) + base
        place = (slots == slot_ref[...]).astype(low)
        total = total + dot_rows(place, rows[...])
        base += rows.shape[0]
    return total


def before_attend_back_kernel(
    row_refs, slot_ref, after_ref, grad_ref, norm_ref, proj_ref, outs
):
    grad_after_ref, grad_low_ref, grad_mixed_ref, sums_ref = outs
    grad_normed = picked_rows(slot_ref, row_refs)
    normal, scale = norm_parts(after_ref[...])
    grad_after = grad_ref[...].astype(f32) + norm_back(
        grad_normed, normal, scale, norm_ref[2:3, :]
    )
    grad_after_ref[...] = grad_after
    grad_low = grad_after.astype(low)
    grad_low_ref[...] = grad_low
    grad_mixed_ref[...] = dot_cols(grad_low, proj_ref[...]).astype(low)
    sums = jnp.concatenate([sum_slabs(grad_normed * normal), sum_slabs(grad_normed)], axis=0)

    @pl.when(pl.program_id(0) == 0)
    def _():
        sums_ref[...] = sums

    @pl.when(pl.program_id(0) > 0)
    def _():
        sums_ref[...] += sums


def before_attend_back(rows, slot_col, after, out_grad, norms, proj):
    count, width = after.shape
    tile = pl.BlockSpec((BLOCK, width), lambda i: (i, 0))

    def kernel(*refs):
        n = len(rows)
        before_attend_back_kernel(refs[:n], *refs[n : n + 5], refs[n + 5 :])

    return pl.pallas_call(
        kernel,
        grid=(count // BLOCK,),
        in_specs=[pl.BlockSpec(r.shape, lambda i: (0, 0)) for r in rows]
        + [
            pl.BlockSpec((BLOCK, 1), lambda i: (i, 0)),
            tile,
            tile,
            pl.BlockSpec(norms.shape, lambda i: (0, 0)),
            pl.BlockSpec((width, width), lambda i: (0, 0)),
        ],
        out_specs=[tile, tile, tile, pl.BlockSpec((16, width), lambda i: (0, 0))],
        out_shape=[
            jax.ShapeDtypeStruct((count, width), f32),
            jax.ShapeDtypeStruct((count, width), low),
            jax.ShapeDtypeStruct((count, width), low),
            jax.ShapeDtypeStruct((16, width), f32),
        ],
        compiler_params=pltpu.CompilerParams(vmem_limit_bytes=48 * 2**20),
        cost_estimate=hint(12),
        name="before_attend_back",
    )(*rows, slot_col, after, out_grad, norms, proj)


def input_grad_kernel(plan, grad_refs, weight_refs, x_ref, norm_ref, grad_after_ref, outs):
    out_ref, sums_ref = outs
    grad_normed = 0.0
    for grad, (strip, offset, wide) in zip(grad_refs, plan):
        for s in range(3):
            weight = weight_refs[3 * strip + s]
            grad_normed = grad_normed + dot_cols(
                grad[:, s * wide : (s + 1) * wide], weight[:, offset : offset + wide]
            )
    normal, scale = norm_parts(x_ref[...].astype(f32))
    out_ref[...] = grad_after_ref[...] + norm_back(grad_normed, normal, scale, norm_ref[0:1, :])
    sums = jnp.concatenate([sum_slabs(grad_normed * normal), sum_slabs(grad_normed)], axis=0)

    @pl.when(pl.program_id(0) == 0)
    def _():
        sums_ref[...] = sums

    @pl.when(pl.program_id(0) > 0)
    def _():
        sums_ref[...] += sums


def input_gradient(plan, grads, weights, tokens, norms, grad_after):
    count, width = tokens.shape
    tile = pl.BlockSpec((BLOCK, width), lambda i: (i, 0))

    def kernel(*refs):
        n, m = len(grads), len(grads) + len(weights)
        input_grad_kernel(plan, refs[:n], refs[n:m], *refs[m : m + 3], refs[m + 3 :])

    return pl.pallas_call(
        kernel,
        grid=(count // BLOCK,),
        in_specs=[pl.BlockSpec((BLOCK, g.shape[1]), lambda i: (i, 0)) for g in grads]
        + [
            pl.BlockSpec((width, columns), lambda i, block=block: (0, block))
            for _, block, columns in weights
        ]
        + [
            tile,
            pl.BlockSpec(norms.shape, lambda i: (0, 0)),
            tile,
        ],
        out_specs=[tile, pl.BlockSpec((16, width), lambda i: (0, 0))],
        out_shape=[
            jax.ShapeDtypeStruct((count, width), f32),
            jax.ShapeDtypeStruct((16, width), f32),
        ],
        compiler_params=pltpu.CompilerParams(vmem_limit_bytes=48 * 2**20),
        cost_estimate=hint(14),
        name="input_gradient",
    )(*grads, *[array for array, _, _ in weights], tokens, norms, grad_after)


def activations_of(rows, slot_col, gate, after):
    count, width = after.shape
    tile = pl.BlockSpec((BLOCK, width), lambda i: (i, 0))

    def kernel(*refs):
        n = len(rows)
        slot_ref, gate_ref, after_ref, out_ref = refs[n:]
        found = picked_rows(slot_ref, refs[:n])
        out_ref[...] = (after_ref[...] + gate_ref[:, :1] * found).astype(low)

    return pl.pallas_call(
        kernel,
        grid=(count // BLOCK,),
        in_specs=[pl.BlockSpec(r.shape, lambda i: (0, 0)) for r in rows]
        + [
            pl.BlockSpec((BLOCK, 1), lambda i: (i, 0)),
            pl.BlockSpec((BLOCK, LANES), lambda i: (i, 0)),
            tile,
        ],
        out_specs=tile,
        out_shape=jax.ShapeDtypeStruct((count, width), low),
        compiler_params=pltpu.CompilerParams(vmem_limit_bytes=48 * 2**20),
        cost_estimate=hint(7.5),
        name="activations_of",
    )(*rows, slot_col, gate, after)


def gelu_and_slope(x):
    point = 1.0 / (1.0 + (erfc_point * math.sqrt(0.5)) * jnp.abs(x))
    bell = jnp.exp(-0.5 * x * x)
    tail = erfc_terms[-1]
    for term in erfc_terms[-2::-1]:
        tail = tail * point + term
    tail = tail * point * bell
    below = jnp.where(x >= 0.0, 1.0 - tail, tail)
    return x * below, below + x * bell * (1.0 / math.sqrt(2.0 * math.pi))


def row_groups(experts, each):
    group = max(g for g in range(1, experts + 1) if experts % g == 0 and g * each <= BLOCK)
    return group, group * each


def expert_kernel(x_ref, in_ref, *rest):
    hidden_ref, slope_ref = rest[-2:]
    experts, each, width = x_ref.shape
    group, size = row_groups(experts, each)
    for e in range(0, experts, group):
        preact = dot_rows(x_ref[e : e + group].reshape(size, width), in_ref[...])
        value, slope = gelu_and_slope(preact)
        hidden_ref[e : e + group] = value.astype(low).reshape(group, each, -1)
        slope_ref[e : e + group] = slope.astype(low).reshape(group, each, -1)


def expert_forward(arrived, weight_in, chunk, chunks, buffer=None, tile=512):
    experts, each, width = arrived.shape
    inner = weight_in.shape[1]
    return pl.pallas_call(
        expert_kernel,
        grid=(inner // tile,),
        in_specs=[
            pl.BlockSpec((experts, each, width), lambda j: (0, 0, 0)),
            pl.BlockSpec((width, tile), lambda j: (0, j)),
        ]
        + ([] if buffer is None else [pl.BlockSpec(memory_space=pl.ANY)]),
        out_specs=[
            pl.BlockSpec((experts, each, tile), lambda j: (0, chunk, j)),
            pl.BlockSpec((experts, each, tile), lambda j: (0, 0, j)),
        ],
        out_shape=[
            jax.ShapeDtypeStruct((experts, chunks * each, inner), low),
            jax.ShapeDtypeStruct((experts, each, inner), low),
        ],
        input_output_aliases={} if buffer is None else {2: 0},
        compiler_params=pltpu.CompilerParams(vmem_limit_bytes=56 * 2**20),
        cost_estimate=hint(21),
        name="expert_forward",
    )(arrived, weight_in, *([] if buffer is None else [buffer]))


def expert_back_kernel(
    grad_ref, slope_ref, in_ref, out_ref, x_ref, result_ref, centre_ref, *rest
):
    grad_preact_ref, grad_rows_ref, grad_centre_ref, strips, grad_logit_ref = rest[-5:]
    step = pl.program_id(0)
    count, size, tile = strips.shape
    each = grad_ref.shape[1]

    @pl.when(step < count)
    def _():
        grad_hidden = dot_cols(grad_ref[...].reshape(size, -1), out_ref[...])
        grad_preact = (grad_hidden * slope_ref[...].reshape(size, tile).astype(f32)).astype(low)
        strips[step] = grad_preact
        grad_preact_ref[...] = grad_preact.reshape(-1, each, tile)

    @pl.when(step == count)
    def _():
        centre = centre_ref[...].astype(f32)
        grad_centre = jnp.zeros(grad_centre_ref.shape, f32)
        group, rows = row_groups(grad_ref.shape[0], each)
        for e in range(0, grad_ref.shape[0], group):
            x = x_ref[e : e + group].reshape(rows, -1).astype(f32)
            gate = jax.nn.sigmoid(jnp.sum(x * centre, axis=-1, keepdims=True))
            grad = grad_ref[e : e + group].reshape(rows, -1).astype(f32)
            moved = grad * result_ref[e : e + group].reshape(rows, -1).astype(f32)
            grad_logit = jnp.sum(moved, axis=-1, keepdims=True) * (1.0 - gate)
            grad_logit_ref[e * each : e * each + rows, :] = jnp.broadcast_to(
                grad_logit, (rows, LANES)
            )
            grad_centre = grad_centre + sum_slabs(grad_logit * x)
        grad_centre_ref[...] = grad_centre

    @pl.when(step >= count)
    def _():
        columns = grad_rows_ref.shape[2]
        start = pl.multiple_of((step - count) * columns, columns)
        centre = centre_ref[:, pl.ds(start, columns)].astype(f32)
        total = grad_logit_ref[:, :1] * centre
        for k in range(count):
            total = total + dot_cols(strips[k], in_ref[:, k * tile : (k + 1) * tile])
        grad_rows_ref[...] = total.astype(low).reshape(-1, each, columns)


def expert_back(
    grad_arrived,
    slope,
    weight_in,
    weight_out,
    arrived,
    result,
    centre,
    chunk,
    chunks,
    buffer=None,
    tile=1024,
    columns=256,
):
    experts, each, width = grad_arrived.shape
    inner = weight_in.shape[1]
    count = inner // tile
    alone = pl.BlockSpec((experts, each, width), lambda j: (0, 0, 0))

    def strip(j):
        return jnp.minimum(j, count - 1)

    def part(j):
        return jnp.maximum(j - count, 0)

    return pl.pallas_call(
        expert_back_kernel,
        grid=(count + width // columns,),
        in_specs=[
            alone,
            pl.BlockSpec((experts, each, tile), lambda j: (0, 0, strip(j))),
            pl.BlockSpec((columns, inner), lambda j: (part(j), 0)),
            pl.BlockSpec((tile, width), lambda j: (strip(j), 0)),
            alone,
            pl.BlockSpec((experts, each, width), lambda j: (0, chunk, 0)),
            pl.BlockSpec((1, width), lambda j: (0, 0)),
        ]
        + ([] if buffer is None else [pl.BlockSpec(memory_space=pl.ANY)]),
        out_specs=[
            pl.BlockSpec((experts, each, tile), lambda j: (0, chunk, strip(j))),
            pl.BlockSpec((experts, each, columns), lambda j: (0, 0, part(j))),
            pl.BlockSpec((8, width), lambda j: (0, 0)),
        ],
        out_shape=[
            jax.ShapeDtypeStruct((experts, chunks * each, inner), low),
            jax.ShapeDtypeStruct((experts, each, width), low),
            jax.ShapeDtypeStruct((8, width), f32),
        ],
        scratch_shapes=[
            pltpu.VMEM((count, experts * each, tile), low),
            pltpu.VMEM((experts * each, LANES), f32),
        ],
        input_output_aliases={} if buffer is None else {7: 0},
        compiler_params=pltpu.CompilerParams(vmem_limit_bytes=58 * 2**20),
        cost_estimate=hint(23),
        name="expert_back",
    )(
        grad_arrived,
        slope,
        weight_in,
        weight_out,
        arrived,
        result,
        centre,
        *([] if buffer is None else [buffer]),
    )


def weight_grads_kernel(chunks, refs):
    x_refs, grad_refs = refs[:chunks], refs[chunks : 2 * chunks]
    grad_preact_ref, hidden_ref, in_out_ref, out_out_ref, turned = refs[2 * chunks :]
    step = pl.program_id(0)
    half = pl.num_programs(0) // 2

    def turn_rows(chunk_refs):
        for c, ref in enumerate(chunk_refs):
            experts, each, width = ref.shape
            group, size = row_groups(experts, each)
            for e in range(0, experts, group):
                turned[c, :, e * each : e * each + size] = (
                    ref[e : e + group].reshape(size, width).T
                )

    pl.when(step == 0)(lambda: turn_rows(x_refs))
    pl.when(step == half)(lambda: turn_rows(grad_refs))

    def multiply(ref, out_ref):
        experts, slots, tile = ref.shape
        each = slots // chunks
        right = [
            ref[:, c * each : (c + 1) * each, :].reshape(experts * each, tile)
            for c in range(chunks)
        ]
        for row in range(0, turned.shape[1], BLOCK):
            rows = slice(row, row + BLOCK)
            total = dot_rows(turned[0, rows, :], right[0])
            for c in range(1, chunks):
                total = total + dot_rows(turned[c, rows, :], right[c])
            out_ref[rows, :] = total.astype(low)

    pl.when(step < half)(lambda: multiply(grad_preact_ref, in_out_ref))
    pl.when(step >= half)(lambda: multiply(hidden_ref, out_out_ref))


def weight_grads(arrived, grad_arrived, grad_preact, hidden, tile=1024):
    chunks = len(arrived)
    experts, each, width = arrived[0].shape
    slots, inner = hidden.shape[1:]
    half = inner // tile
    whole = pl.BlockSpec((experts, each, width), lambda j: (0, 0, 0))

    def first(j):
        return jnp.minimum(j, half - 1)

    def second(j):
        return jnp.maximum(j - half, 0)

    return pl.pallas_call(
        lambda *refs: weight_grads_kernel(chunks, refs),
        grid=(2 * half,),
        in_specs=[whole] * (2 * chunks)
        + [
            pl.BlockSpec((experts, slots, tile), lambda j: (0, 0, first(j))),
            pl.BlockSpec((experts, slots, tile), lambda j: (0, 0, second(j))),
        ],
        out_specs=[
            pl.BlockSpec((width, tile), lambda j: (0, first(j))),
            pl.BlockSpec((width, tile), lambda j: (0, second(j))),
        ],
        out_shape=[jax.ShapeDtypeStruct((width, inner), low)] * 2,
        scratch_shapes=[pltpu.VMEM((chunks, width, experts * each), low)],
        compiler_params=pltpu.CompilerParams(vmem_limit_bytes=58 * 2**20),
        cost_estimate=hint(38),
        name="weight_grads",
    )(*arrived, *grad_arrived, grad_preact, hidden)


def update(weight, moment, average, gradient, factor, rate):
    clipped = gradient * factor
    moment_new = momentum_rate * moment + clipped
    weight_new = weight - rate * (clipped + momentum_rate * moment_new)
    average_new = average_rate * average + (1.0 - average_rate) * weight_new
    return (weight_new, moment_new, average_new)


def step_kernel(factor_ref, *refs):
    inputs, outputs = refs[:8], refs[8:]
    factor = factor_ref[0]
    for which in range(2):
        weight, moment, average, gradient = inputs[4 * which : 4 * which + 4]
        gradient = gradient[...] if which == 0 else gradient[...].T
        stepped = update(
            weight[0], moment[0], average[0], gradient.astype(f32), factor, learn_rate
        )
        for out, value in zip(outputs[3 * which : 3 * which + 3], stepped):
            out[0] = value


def step_experts(factor, first, second, tile=1024):
    rows, columns = first[0].shape[1:]
    along = pl.BlockSpec((1, rows, tile), lambda j: (0, 0, j))
    down = pl.BlockSpec((1, tile, rows), lambda j: (0, j, 0))
    gradient = pl.BlockSpec((rows, tile), lambda j: (0, j))
    return pl.pallas_call(
        step_kernel,
        grid=(columns // tile,),
        in_specs=[pl.BlockSpec(memory_space=pltpu.SMEM)]
        + [along] * 3
        + [gradient]
        + [down] * 3
        + [gradient],
        out_specs=[along] * 3 + [down] * 3,
        out_shape=[jax.ShapeDtypeStruct(first[0].shape, f32)] * 3
        + [jax.ShapeDtypeStruct(second[0].shape, f32)] * 3,
        compiler_params=pltpu.CompilerParams(vmem_limit_bytes=48 * 2**20),
        cost_estimate=hint(20),
        name="step_experts",
    )(factor.reshape(1), *first, *second)


def swap(values, axis, distance):
    size = lax.axis_size(axis)
    return lax.ppermute(values, axis, [(i, i ^ distance) for i in range(size)])


def assemble_kernel(me_ref, *refs):
    pieces, out_ref = refs[:-1], refs[-1]
    experts, rows = pieces[0].shape[0], pieces[0].shape[1]
    for t, piece in enumerate(pieces):
        for e in range(experts):
            owner = e * len(pieces) + (me_ref[0] ^ t)
            out_ref[pl.ds(pl.multiple_of(owner * rows, rows), rows), :] = piece[e]


def assemble(pieces):
    experts, rows, columns = pieces[0].shape
    dp = len(pieces)
    return pl.pallas_call(
        assemble_kernel,
        in_specs=[pl.BlockSpec(memory_space=pltpu.SMEM)]
        + [pl.BlockSpec(memory_space=pltpu.VMEM)] * dp,
        out_specs=pl.BlockSpec(memory_space=pltpu.VMEM),
        out_shape=jax.ShapeDtypeStruct((experts * dp * rows, columns), pieces[0].dtype),
        compiler_params=pltpu.CompilerParams(vmem_limit_bytes=32 * 2**20),
        cost_estimate=hint(4),
        name="assemble",
    )(lax.axis_index("dp").astype(jnp.int32).reshape(1), *pieces)


def sum_halves(parts, axis, bit, at):
    own = (lax.axis_index(axis) // bit) % 2

    def side(which):
        picked = []
        for part in parts:
            shape = part.shape
            halves = part.reshape(shape[:at] + (shape[at] // 2, 2) + shape[at + 1 :])
            picked.append(lax.dynamic_index_in_dim(halves, which, at + 1, keepdims=False))
        return jnp.concatenate(picked, axis=-1)

    return (side(own).astype(f32) + swap(side(1 - own), axis, bit).astype(f32)).astype(low)


def sum_over_cores(parts):
    return sum_halves(parts, "dp", 1, 1)


def sum_over_neighbours(held):
    return sum_halves([held], "expert", 1, 0)


def sum_over_pairs(held, partners, keep, *beside):
    experts, dp = lax.axis_size("expert"), lax.axis_size("dp")
    total = lax.dynamic_index_in_dim(held, keep, 0, keepdims=False).astype(f32)
    received = []
    for offset, (far, near) in enumerate(partners, 1):
        block = lax.dynamic_index_in_dim(held, jnp.bitwise_xor(keep, offset), 0, keepdims=False)
        perm = [
            (e * dp + d, (e ^ far) * dp + (d ^ near)) for e in range(experts) for d in range(dp)
        ]
        received.append(lax.ppermute(block, everywhere, perm))
    if beside:
        moved = in_order(*received, *beside)
        received, beside = moved[: len(received)], moved[len(received) :]
    for block in received:
        total = total + block.astype(f32)
    return (total, *beside) if beside else total


def sum_near(held):
    near = held.shape[1]
    held = held.reshape((held.shape[0] // 2, 2 * near) + held.shape[2:]).swapaxes(0, 1)
    partners = [(i // near, i % near * 2) for i in range(1, 2 * near)]
    keep = lax.axis_index("expert") % 2 * near + lax.axis_index("dp") // 2
    return sum_over_pairs(held, partners, keep).astype(low)


def sum_far(held, *beside):
    partners = [(2 * i, 0) for i in range(1, held.shape[0])]
    return sum_over_pairs(held, partners, lax.axis_index("expert") // 2, *beside)


def sum_across(held):
    partners = [(0, 2 * i) for i in range(1, held.shape[0])]
    return sum_over_pairs(held, partners, lax.axis_index("dp") // 2)


def in_order(*values):
    return lax.optimization_barrier(values)


def sum_everywhere(value):
    held = value.reshape(1, 1)
    for axis in ("dp", "expert"):
        distance = 1
        while distance < lax.axis_size(axis):
            held = held + swap(held, axis, distance)
            distance *= 2
    return held[0, 0]


def shards(
    tokens,
    documents,
    routes,
    out_grad,
    norm_params,
    qkv_weight,
    proj_weight,
    centroids,
    expert_in,
    expert_out,
    norm_moment,
    qkv_moment,
    proj_moment,
    centroid_moment,
    in_moment,
    out_moment,
    norm_average,
    qkv_average,
    proj_average,
    centroid_average,
    in_average,
    out_average,
):
    local_tokens, width = tokens.shape
    experts = lax.axis_size("expert")
    dp = lax.axis_size("dp")
    devices = experts * dp
    slot_cap = max(2, 3 * local_tokens // (2 * experts))
    slots = experts * slot_cap
    chunks = 2 if slot_cap % 32 == 0 else 1
    half_cap = slot_cap // chunks
    rows_own = qkv_weight.shape[0]
    norm_own = norm_params.shape[1]
    centre_own = centroids.shape[1]
    groups = 4

    strips = 2
    strip = width // strips
    small = jnp.concatenate([norm_params.reshape(-1), centroids.reshape(-1)]).astype(low)
    small = jnp.pad(small, (0, rows_own * LANES - small.shape[0])).reshape(rows_own, LANES)
    qkv_low = qkv_weight.astype(low)
    qkv_own = [
        [qkv_low[:, s * width + h * strip : s * width + (h + 1) * strip] for s in range(3)]
        for h in range(strips)
    ]
    front = jnp.concatenate([*qkv_own[0], small], axis=1)
    later = jnp.concatenate([proj_weight.astype(low), *qkv_own[1]], axis=1)
    later = lax.all_gather(later, everywhere, axis=0, tiled=True)
    in_low, out_low = expert_in.astype(low), expert_out.astype(low)

    route_ids = routes[:, 0]
    onehot = route_ids[:, None] == jnp.arange(experts, dtype=jnp.int32)[None, :]
    running = jnp.cumsum(onehot.astype(jnp.int32), axis=0)
    within = jnp.sum(running * onehot.astype(jnp.int32), axis=1) - 1
    slot_index = route_ids * slot_cap + within
    chunked = (within // half_cap * experts + route_ids) * half_cap + within % half_cap
    slot_row, slot_col = slot_index[None, :], slot_index[:, None]
    chunked_row, chunked_col = chunked[None, :], chunked[:, None]
    doc_col = documents[:, None]
    doc_row = documents[None, :]

    if rows_own % 16:
        front = lax.all_gather(front, everywhere, axis=0, tiled=True)
    else:
        spread = jnp.broadcast_to(front[None], (experts,) + front.shape)
        spread = lax.all_to_all(spread, "expert", split_axis=0, concat_axis=0, tiled=True)
        spread, in_low, out_low, slot_row, slot_col, chunked_row, chunked_col = in_order(
            spread, in_low, out_low, slot_row, slot_col, chunked_row, chunked_col
        )
        pieces = {0: spread}
        distance = dp // 2
        while distance:
            for t in list(pieces):
                pieces[t | distance] = swap(pieces[t], "dp", distance)
            distance //= 2
        front = assemble([pieces[t] for t in range(dp)])
    weight_in = lax.all_gather(in_low, "dp", axis=1, tiled=True)[0]
    weight_out = lax.all_gather(out_low, "dp", axis=2, tiled=True)[0]
    small_full = front[:, 3 * strip :].reshape(devices, rows_own * LANES)
    norms = (
        small_full[:, : 4 * norm_own].reshape(devices, 4, norm_own).transpose(1, 0, 2)
    ).reshape(4, width).astype(f32)
    centre_table = small_full[:, 4 * norm_own : 4 * norm_own + centre_own].reshape(experts, width)

    normal_one, _ = norm_parts(tokens.astype(f32))
    normed_low = (normal_one * norms[0] + norms[1]).astype(low)
    normed_low, front = in_order(normed_low, front)
    packed, mixed, lse = [], [], []
    for weight in (front[:, : 3 * strip], later[:, width:]):
        packed_h = jnp.dot(normed_low, weight, preferred_element_type=f32).astype(low)
        mixed_h, lse_h = attend(packed_h, doc_col, doc_row)
        packed.append(packed_h)
        mixed.append(mixed_h)
        lse.append(lse_h)
    after, grad_rows, gate, *outgoing = after_attend(
        mixed,
        later,
        tokens,
        out_grad,
        norms,
        centre_table,
        routes,
        chunked_row,
        [slots // chunks] * chunks,
    )

    def exchange(rows):
        rows = rows.reshape(experts, -1, width)
        return lax.all_to_all(rows, "expert", split_axis=0, concat_axis=0, tiled=True)

    grad_outgoing = []
    for c in range(chunks):
        own = jnp.arange(slots // chunks, dtype=jnp.int32)[:, None] + c * (slots // chunks)
        place = (own == chunked_row).astype(low)
        grad_outgoing.append(jnp.dot(place, grad_rows, preferred_element_type=f32).astype(low))
    arrived, slope, hidden = [], [], None
    for c in range(chunks):
        if c:
            arrived[c - 1], outgoing[c], *grad_outgoing = in_order(
                arrived[c - 1], outgoing[c], *grad_outgoing
            )
        arrived.append(exchange(outgoing[c]))
    for c in range(chunks):
        if c == chunks - 1:
            arrived[c], grad_outgoing[0] = in_order(arrived[c], grad_outgoing[0])
        hidden, slope_c = expert_forward(arrived[c], weight_in, c, chunks, hidden)
        slope.append(slope_c)
        if c == 0 and chunks > 1:
            hidden, grad_outgoing[0] = in_order(hidden, grad_outgoing[0])
    grad_arrived = [exchange(grad_outgoing[0])]
    hidden = hidden.reshape(slots, -1)
    result = jnp.dot(hidden, weight_out, preferred_element_type=f32).astype(low)
    result = result.reshape(experts, slot_cap, width)
    for c in range(1, chunks):
        grad_arrived[c - 1], grad_outgoing[c], result = in_order(
            grad_arrived[c - 1], grad_outgoing[c], result
        )
        grad_arrived.append(exchange(grad_outgoing[c]))
    centre_row = lax.dynamic_slice_in_dim(centre_table, lax.axis_index("expert"), 1, 0)
    grad_preact = None
    grad_input, grad_centre = [], 0.0
    for c in range(chunks):
        last = c == chunks - 1
        grad_preact, rows_c, centre_c = expert_back(
            grad_arrived[c],
            slope[c],
            weight_in,
            weight_out,
            arrived[c],
            result,
            centre_row,
            c,
            chunks,
            grad_preact,
        )
        if not last:
            rows_c, grad_arrived[c + 1] = in_order(rows_c, grad_arrived[c + 1])
        elif grad_input:
            rows_c, grad_input[-1] = in_order(rows_c, grad_input[-1])
        grad_input.append(exchange(rows_c).reshape(slots // chunks, width))
        grad_centre = grad_centre + jnp.sum(centre_c, axis=0)
    if chunks > 1:
        hidden, arrived[0], grad_input[0] = in_order(hidden, arrived[0], grad_input[0])
    grad_in, grad_out_turned = weight_grads(
        arrived, grad_arrived, grad_preact, hidden.reshape(experts, slot_cap, -1)
    )
    result, grad_input[-1], grad_in, grad_out_turned = in_order(
        result, grad_input[-1], grad_in, grad_out_turned
    )
    in_grad = lax.psum_scatter(grad_in[None], "dp", scatter_dimension=1, tiled=True)
    out_turned = lax.psum_scatter(grad_out_turned[None], "dp", scatter_dimension=1, tiled=True)
    returned = exchange(result).reshape(slots, width)

    grad_after, grad_low, grad_mixed, sums_two = before_attend_back(
        grad_input, chunked_col, after, out_grad, norms, later
    )

    grad_proj = jnp.concatenate(
        [
            lax.dot_general(m, grad_low, (((0,), (0,)), ((), ())), preferred_element_type=f32)
            for m in mixed
        ],
        axis=0,
    ).astype(low)
    norm_two = jnp.sum(sums_two.reshape(2, 8, width), axis=1)
    norm_two = norm_two.reshape(2, devices, norm_own).transpose(1, 0, 2).reshape(devices, -1)
    mine = jnp.arange(experts)[:, None, None] == lax.axis_index("expert")
    centre_flat = jnp.where(mine, grad_centre.reshape(1, dp, centre_own), 0.0)
    extra = jnp.concatenate([norm_two, centre_flat.reshape(devices, centre_own)], axis=1)
    extra = jnp.pad(extra, ((0, 0), (0, rows_own * LANES - extra.shape[1]))).astype(low)
    extra = extra.reshape(devices * rows_own, LANES)
    each = width // LANES // groups
    wide = each * LANES

    def by_owner(values):
        return values.reshape(experts, dp, rows_own, values.shape[1])

    def back_group(g, *beside):
        h, k = g // (groups // strips), g % (groups // strips)
        part = attend_back(
            packed[h], grad_mixed, mixed[h], lse[h], doc_col, doc_row, k * each, each, g * each
        )
        part, *beside = in_order(part, *beside)
        grad = lax.dot_general(
            normed_low, part, (((0,), (0,)), ((), ())), preferred_element_type=f32
        )
        return part, grad.astype(low), *beside

    parts, grads = [], []
    rest = by_owner(jnp.concatenate([grad_proj, extra], axis=1))
    for g in range(groups):
        if g == 1:
            rest = sum_over_cores([rest])
            rest, grad_mixed = in_order(rest, grad_mixed)
        if g == groups - 1:
            rest = sum_over_neighbours(rest)
            first = sum_over_cores([by_owner(v) for v in grads[: groups // 2]])
            rest, first, grad_mixed, returned = in_order(rest, first, grad_mixed, returned)
            first = sum_over_neighbours(first)
            part, grad, first = back_group(g, first)
        else:
            part, grad = back_group(g)
        grad, grad_mixed = in_order(grad, grad_mixed)
        parts.append(part)
        grads.append(grad)
    second = sum_over_cores([by_owner(v) for v in grads[groups // 2 :]])
    second, first, grad_after = in_order(second, first, grad_after)
    second = sum_near(second)
    first = sum_far(jnp.concatenate([rest, first], axis=-1)).astype(low)
    per_strip = groups // strips
    weights = [(front, s, strip) for s in range(3)]
    weights += [(later, width // strip + s, strip) for s in range(3)]
    input_grad, sums_one = input_gradient(
        [(g // per_strip, g % per_strip * wide, wide) for g in range(groups)],
        parts,
        weights,
        tokens,
        norms,
        grad_after,
    )
    first, second, sums_one, gate = in_order(first, second, sums_one, gate)
    norm_one = jnp.sum(sums_one.reshape(2, 8, width), axis=1)
    norm_one = norm_one.reshape(2, devices, norm_own).transpose(1, 0, 2).reshape(devices, -1)
    norm_one = lax.all_to_all(norm_one, everywhere, split_axis=0, concat_axis=0, tiled=True)
    norm_one, in_grad, out_turned = in_order(norm_one, in_grad, out_turned)
    in_square = jnp.sum(jnp.square(in_grad.astype(f32)))
    out_square = jnp.sum(jnp.square(out_turned.astype(f32)))
    activations = activations_of([returned], slot_col, gate, after)
    norm_one = jnp.sum(norm_one, axis=0).reshape(2, norm_own)
    second, activations, in_square, out_square = sum_far(
        second, activations, in_square, out_square
    )
    first = sum_across(first)
    first, second, in_square, out_square, norm_one, activations = in_order(
        first, second, in_square, out_square, norm_one, activations
    )

    proj_grad = first[:, :width]
    extra = first[:, width : width + LANES].reshape(-1)
    norm_grad = jnp.concatenate([norm_one, extra[: 2 * norm_own].reshape(2, norm_own)], axis=0)
    centre_grad = extra[2 * norm_own : 2 * norm_own + centre_own].reshape(centroids.shape)
    owned = jnp.concatenate([first[:, width + LANES :], second], axis=1)
    qkv_grad = owned.reshape(rows_own, groups, 3, wide).swapaxes(1, 2).reshape(rows_own, 3 * width)
    square_sum = (
        jnp.sum(owned * owned)
        + jnp.sum(proj_grad * proj_grad)
        + jnp.sum(norm_grad * norm_grad)
        + jnp.sum(centre_grad * centre_grad)
        + in_square
        + out_square
    )
    grad_norm = jnp.sqrt(sum_everywhere(square_sum))
    factor = clip_limit / jnp.maximum(grad_norm, clip_limit)
    norm_new = update(norm_params, norm_moment, norm_average, norm_grad, factor, norm_rate)
    qkv_new = update(qkv_weight, qkv_moment, qkv_average, qkv_grad, factor, learn_rate)
    proj_new = update(proj_weight, proj_moment, proj_average, proj_grad, factor, learn_rate)
    centre_new = update(
        centroids, centroid_moment, centroid_average, centre_grad, factor, learn_rate
    )
    stepped = step_experts(
        factor,
        (expert_in, in_moment, in_average, in_grad[0]),
        (expert_out, out_moment, out_average, out_turned[0]),
    )
    in_new, out_new = stepped[:3], stepped[3:]
    return (
        activations,
        input_grad,
        grad_norm,
        norm_new[0],
        qkv_new[0],
        proj_new[0],
        centre_new[0],
        in_new[0],
        out_new[0],
        norm_new[1],
        qkv_new[1],
        proj_new[1],
        centre_new[1],
        in_new[1],
        out_new[1],
        norm_new[2],
        qkv_new[2],
        proj_new[2],
        centre_new[2],
        in_new[2],
        out_new[2],
    )


def solution(mesh):
    placed = (
        P(("expert", "dp"), None),
        P(("expert", "dp")),
        P(("expert", "dp"), None),
        P(("expert", "dp"), None),
        P(None, ("expert", "dp")),
        P(("expert", "dp"), None),
        P(("expert", "dp"), None),
        P("expert", "dp"),
        P("expert", "dp", None),
        P("expert", None, "dp"),
        P(None, ("expert", "dp")),
        P(("expert", "dp"), None),
        P(("expert", "dp"), None),
        P("expert", "dp"),
        P("expert", "dp", None),
        P("expert", None, "dp"),
        P(None, ("expert", "dp")),
        P(("expert", "dp"), None),
        P(("expert", "dp"), None),
        P("expert", "dp"),
        P("expert", "dp", None),
        P("expert", None, "dp"),
    )
    return jax.shard_map(
        shards,
        mesh=mesh,
        in_specs=placed,
        out_specs=(
            P(("expert", "dp"), None),
            P(("expert", "dp"), None),
            P(),
            P(None, ("expert", "dp")),
            P(("expert", "dp"), None),
            P(("expert", "dp"), None),
            P("expert", "dp"),
            P("expert", "dp", None),
            P("expert", None, "dp"),
            P(None, ("expert", "dp")),
            P(("expert", "dp"), None),
            P(("expert", "dp"), None),
            P("expert", "dp"),
            P("expert", "dp", None),
            P("expert", None, "dp"),
            P(None, ("expert", "dp")),
            P(("expert", "dp"), None),
            P(("expert", "dp"), None),
            P("expert", "dp"),
            P("expert", "dp", None),
            P("expert", None, "dp"),
        ),
        check_vma=False,
    )
```
